32 devices in a mesh: section: 2 (over core), dp: 4 (over y, x), tensor: 4 (over z).
Axes of the slice: x: 2, y: 2, z: 4, core: 2. Of those that a mesh axis runs over, the one named last changes fastest.
Arguments:
- hidden_in: bfloat16 [8, 1024, 768], P('dp'), may hold values from -6 to 6
- target: bfloat16 [8, 1024, 768], P('dp'), may hold values from -6 to 6
- tissue: int32 [8], P('dp'), may hold values from 0 to 15
- ln1_gain: bfloat16 [2, 768], P('section'), may hold values from 0.5 to 1.5
- ln1_bias: bfloat16 [2, 768], P('section'), may hold values from -1.75 to 1.75
- ln2_gain: bfloat16 [2, 768], P('section'), may hold values from 0.5 to 1.5
- ln2_bias: bfloat16 [2, 768], P('section'), may hold values from -1.75 to 1.75
- qkv_weight: bfloat16 [2, 768, 2304], P('section', None, 'tensor'), may hold values from -0.21875 to 0.21875
- qkv_bias: bfloat16 [2, 2304], P('section', 'tensor'), may hold values from -1.75 to 1.75
- dense_weight: bfloat16 [2, 768, 768], P('section', 'tensor'), may hold values from -1 to 1
- dense_bias: bfloat16 [2, 768], P('section'), may hold values from -1.75 to 1.75
- fc1_weight: bfloat16 [2, 768, 3072], P('section', None, 'tensor'), may hold values from -0.21875 to 0.21875
- fc1_bias: bfloat16 [2, 3072], P('section', 'tensor'), may hold values from -1.75 to 1.75
- fc2_weight: bfloat16 [2, 3072, 768], P('section', 'tensor'), may hold values from -0.21875 to 0.21875
- fc2_bias: bfloat16 [2, 768], P('section'), may hold values from -1.75 to 1.75
Outputs:
- block_out: bfloat16 [2, 8, 1024, 768], P('section', 'dp', None, 'tensor')
- input_grad: float32 [2, 8, 1024, 768], P('section', 'dp', None, 'tensor')
- ln1_gain_grad: float32 [2, 768], P('section')
- ln1_bias_grad: float32 [2, 768], P('section')
- ln2_gain_grad: float32 [2, 768], P('section')
- ln2_bias_grad: float32 [2, 768], P('section')
- qkv_weight_grad: float32 [2, 768, 2304], P('section', None, 'tensor')
- qkv_bias_grad: float32 [2, 2304], P('section', 'tensor')
- dense_weight_grad: float32 [2, 768, 768], P('section', 'tensor')
- dense_bias_grad: float32 [2, 768], P('section')
- fc1_weight_grad: float32 [2, 768, 3072], P('section', None, 'tensor')
- fc1_bias_grad: float32 [2, 3072], P('section', 'tensor')
- fc2_weight_grad: float32 [2, 3072, 768], P('section', 'tensor')
- fc2_bias_grad: float32 [2, 768], P('section')
The draws below stay inside these ranges and needn't reach their ends.
All inputs are finite; a program needn't handle non-finite values.
Results may differ from the reference program's by a relative error of at most 0.012.
Values may be sent and summed in bfloat16 or wider, within the bound.
A program may use at most 192 MiB of HBM per device.

```python
import jax
import jax.numpy as jnp
from jax import lax

D = 768
HEADS = 12
HEAD = 64
FF = 3072
ROT = 16
LENGTH = 1024
TISSUES = 16
SENTENCES = 8


def place_ends(array, stream_key, smallest, high):
    place = [jax.random.randint(jax.random.fold_in(stream_key, axis), (), 0, length) for axis, length in enumerate(array.shape)]
    main_axis = array.shape.index(max(array.shape))
    next_to = place[:main_axis] + [(place[main_axis] + 1) % array.shape[main_axis]] + place[main_axis + 1:]
    return array.at[tuple(place)].set(smallest).at[tuple(next_to)].set(high)


def shard_levels(stream_key, extent, pieces, smallest, largest):
    loudness = 1.0
    for position, blocks in pieces:
        steps = jax.random.uniform(jax.random.fold_in(jax.random.fold_in(stream_key, 6), position), (blocks,), jnp.float32, smallest / len(pieces), largest / len(pieces))
        loudness = loudness * jnp.repeat(jnp.exp(steps), extent[position] // blocks).reshape((-1,) + (1,) * (len(extent) - 1 - position))
    return loudness


def centred(own_key, dims, scale, reach, split=(), dtype=jnp.bfloat16):
    values = scale * jax.random.normal(own_key, dims, jnp.float32)
    if split:
        values = values * shard_levels(own_key, dims, split, -0.22, 0.18)
    return jnp.clip(values, -reach, reach).astype(dtype)


def setup_inputs(seed: int = 0) -> dict:
    key_of = jax.random.split(jax.random.key(seed), 16)
    hidden_in = centred(key_of[0], (SENTENCES, LENGTH, D), 1.0, 6.0, ((0, 4),))
    target = centred(key_of[1], (SENTENCES, LENGTH, D), 1.0, 6.0, ((0, 4),))
    tissue = place_ends(jax.random.randint(key_of[2], (SENTENCES,), 0, TISSUES), jax.random.fold_in(key_of[2], 1), 0, TISSUES - 1).astype(jnp.int32)
    ln1_gain = jnp.clip(1.0 + 0.1 * jax.random.normal(key_of[3], (2, D), jnp.float32), 0.5, 1.5).astype(jnp.bfloat16)
    ln1_bias = centred(key_of[4], (2, D), 0.3, 1.75, ((0, 2),))
    ln2_gain = jnp.clip(1.0 + 0.1 * jax.random.normal(key_of[5], (2, D), jnp.float32), 0.5, 1.5).astype(jnp.bfloat16)
    ln2_bias = centred(key_of[6], (2, D), 0.3, 1.75, ((0, 2),))
    qkv_weight = centred(key_of[7], (2, D, 3 * D), D ** -0.5, 0.21875, ((0, 2), (2, 4)))
    qkv_bias = centred(key_of[8], (2, 3 * D), 0.3, 1.75, ((0, 2), (1, 4)))
    dense_weight = centred(key_of[9], (2, D, D), (HEAD // 2) ** -0.5, 1.0, ((0, 2), (1, 4)))
    dense_bias = centred(key_of[10], (2, D), 0.3, 1.75, ((0, 2),))
    fc1_weight = centred(key_of[11], (2, D, FF), D ** -0.5, 0.21875, ((0, 2), (2, 4)))
    fc1_bias = centred(key_of[12], (2, FF), 0.3, 1.75, ((0, 2), (1, 4)))
    fc2_weight = centred(key_of[13], (2, FF, D), (FF // 4) ** -0.5, 0.21875, ((0, 2), (1, 4)))
    fc2_bias = centred(key_of[14], (2, D), 0.3, 1.75, ((0, 2),))
    return dict(hidden_in=hidden_in, target=target, tissue=tissue, ln1_gain=ln1_gain, ln1_bias=ln1_bias, ln2_gain=ln2_gain, ln2_bias=ln2_bias, qkv_weight=qkv_weight, qkv_bias=qkv_bias, dense_weight=dense_weight, dense_bias=dense_bias, fc1_weight=fc1_weight, fc1_bias=fc1_bias, fc2_weight=fc2_weight, fc2_bias=fc2_bias)


@jax.custom_vjp
def low(v):
    return lax.optimization_barrier(v.astype(jnp.bfloat16)).astype(jnp.float32)

@jax.custom_vjp
def low_back(v):
    return v

def low_keep(v):
    return (low(v), None)

def low_pass(kept, grad):
    return (grad,)

def back_keep(v):
    return (v, None)

def back_low(kept, grad):
    return (low(grad),)
low.defvjp(low_keep, low_pass)
low_back.defvjp(back_keep, back_low)

def layer_norm(value, gain, bias):
    center = value - lax.optimization_barrier(jnp.mean(value, axis=-1, keepdims=True))
    spread = lax.optimization_barrier(jnp.mean(center * center, axis=-1, keepdims=True))
    return center * lax.rsqrt(spread + 1e-05) * gain + bias

def rotary_tables(seq_len):
    half = ROT // 2
    positions = jnp.arange(seq_len).astype(jnp.float32)
    inverse = jnp.power(10000.0, -2.0 * jnp.arange(half).astype(jnp.float32) / ROT)
    angles = positions[:, None] * inverse[None, :]
    cosines = jnp.concatenate([jnp.cos(angles), jnp.cos(angles)], axis=1)[:, None, :]
    sines = jnp.concatenate([jnp.sin(angles), jnp.sin(angles)], axis=1)[:, None, :]
    return (cosines, sines)

def rotate(heads_in, cosines, sines):
    half = ROT // 2
    turning = heads_in[..., :ROT]
    turned = jnp.concatenate([-turning[..., half:], turning[..., :half]], axis=-1)
    return jnp.concatenate([turning * cosines + turned * sines, heads_in[..., ROT:]], axis=-1)

def smooth_gate(value):
    return jax.nn.gelu(value, approximate=False)

def matmul(left, right):
    return jnp.dot(left, right, precision=lax.Precision.HIGHEST)

def block(params, hidden):
    norm1_gain, norm1_bias, norm2_gain, norm2_bias, qkv_mat, qkv_shift, dense_mat, dense_shift, fc1_mat, fc1_shift, fc2_mat, fc2_shift = params
    seq_len = hidden.shape[0]
    first_norm = low(layer_norm(hidden, norm1_gain, norm1_bias))
    second_norm = low(layer_norm(hidden, norm2_gain, norm2_bias))
    projected = low_back(matmul(first_norm, qkv_mat) + qkv_shift).reshape(seq_len, HEADS, 3, HEAD)
    cosines, sines = rotary_tables(seq_len)
    queries = low(rotate(projected[:, :, 0], cosines, sines))
    key_heads = low(rotate(projected[:, :, 1], cosines, sines))
    value_heads = low(projected[:, :, 2])
    scores = low_back(jnp.einsum('qhd,khd->hqk', queries, key_heads, precision=lax.Precision.HIGHEST) * HEAD ** (-0.5))
    causal = jnp.arange(seq_len)[:, None] >= jnp.arange(seq_len)[None, :]
    scores = jnp.where(causal[None], scores, -1e+30)
    highest = lax.optimization_barrier(jnp.max(scores, axis=-1, keepdims=True))
    raised = jnp.exp(scores - highest)
    probs = low(raised / lax.optimization_barrier(jnp.sum(raised, axis=-1, keepdims=True)))
    context = jnp.einsum('hqk,khd->qhd', probs, value_heads, precision=lax.Precision.HIGHEST).reshape(seq_len, HEADS * HEAD)
    context = low_back(low(context))
    attention = low_back(matmul(context, dense_mat) + dense_shift)
    pre_act = low_back(matmul(second_norm, fc1_mat) + fc1_shift)
    activated = low(smooth_gate(pre_act))
    feedforward = low_back(matmul(activated, fc2_mat) + fc2_shift)
    return hidden + attention + feedforward

def reference(hidden_in, target, tissue, ln1_gain, ln1_bias, ln2_gain, ln2_bias, qkv_weight, qkv_bias, dense_weight, dense_bias, fc1_weight, fc1_bias, fc2_weight, fc2_bias):
    arrays = (ln1_gain, ln1_bias, ln2_gain, ln2_bias, qkv_weight, qkv_bias, dense_weight, dense_bias, fc1_weight, fc1_bias, fc2_weight, fc2_bias)
    first_params = tuple((item[0].astype(jnp.float32) for item in arrays))
    second_params = tuple((item[1].astype(jnp.float32) for item in arrays))
    labels = (tissue[:, None] == jnp.arange(TISSUES)[None, :]).astype(jnp.float32)
    counts = lax.optimization_barrier(jnp.sum(labels, axis=0))
    own_count = lax.optimization_barrier(jnp.sum(labels * counts[None, :], axis=1))
    share = SENTENCES / TISSUES / own_count
    zero_grads = tuple((jnp.zeros(item[0].shape, jnp.float32) for item in arrays))

    def sentence_step(carry, inputs):
        hidden, goal, weight = inputs
        first_totals, second_totals = carry
        first_out, first_back = jax.vjp(block, first_params, hidden.astype(jnp.float32))
        passed = low(first_out)
        second_out, second_back = jax.vjp(block, second_params, passed)
        second_grads, passed_grad = second_back(weight * goal.astype(jnp.float32))
        first_grads, entry_grad = first_back(low(passed_grad))
        first_totals = tuple((a + b for a, b in zip(first_totals, first_grads)))
        second_totals = tuple((a + b for a, b in zip(second_totals, second_grads)))
        outputs = (first_out.astype(jnp.bfloat16), second_out.astype(jnp.bfloat16), entry_grad, passed_grad)
        return ((first_totals, second_totals), outputs)
    totals, outputs = lax.scan(sentence_step, (zero_grads, zero_grads), (hidden_in, target, share))
    block_out = jnp.stack([outputs[0], outputs[1]])
    gradient_in = jnp.stack([outputs[2], outputs[3]])
    grads = tuple((jnp.stack([a, b]) for a, b in zip(totals[0], totals[1])))
    return (block_out, gradient_in, grads[0], grads[1], grads[2], grads[3], grads[4], grads[5], grads[6], grads[7], grads[8], grads[9], grads[10], grads[11])
```

```python
import functools

import jax
import jax.numpy as jnp
import numpy as np
from jax import lax
from jax.experimental import pallas as pl
from jax.experimental.pallas import tpu as pltpu
from jax.sharding import PartitionSpec as P

HEAD = 64
ROT = 16
TISSUES = 16
ROWS = 256
LANES = 128
EPS = 1e-05
MESH = pl.DeviceIdType.MESH
F32 = jnp.float32
BF16 = jnp.bfloat16


def dot_nn(a, b):
    return lax.dot_general(a, b, (((1,), (0,)), ((), ())), preferred_element_type=F32)


def dot_nt(a, b):
    return lax.dot_general(a, b, (((1,), (1,)), ((), ())), preferred_element_type=F32)


def dot_tn(a, b):
    return lax.dot_general(a, b, (((0,), (0,)), ((), ())), preferred_element_type=F32)


def rotary_tables(seq_len):
    half = ROT // 2
    inverse = 10000.0 ** (-2.0 * np.arange(half) / ROT)
    angles = np.arange(seq_len)[:, None] * inverse[None, :]
    cosines = np.ones((seq_len, HEAD))
    left = np.zeros((seq_len, HEAD))
    right = np.zeros((seq_len, HEAD))
    cosines[:, :half] = np.cos(angles)
    cosines[:, half:ROT] = np.cos(angles)
    left[:, :half] = -np.sin(angles)
    right[:, half:ROT] = np.sin(angles)
    tables = np.stack([np.tile(item, (1, LANES // HEAD)) for item in (cosines, left, right)])
    return tables.astype(np.float32)


def pack_columns(weight, lanes):
    lead = weight.shape[:-1]
    heads = weight.shape[-1] // (3 * HEAD)
    split = jnp.moveaxis(weight.reshape(lead + (heads, 3, HEAD)), -2, -3)
    split = split.reshape(lead + (3, heads * HEAD))
    split = jnp.pad(split, [(0, 0)] * (len(lead) + 1) + [(0, lanes - heads * HEAD)])
    return split.reshape(lead + (3 * lanes,))


def unpack_columns(weight, heads):
    lead = weight.shape[:-1]
    split = weight.reshape(lead + (3, -1))[..., : heads * HEAD]
    split = split.reshape(lead + (3, heads, HEAD))
    return jnp.moveaxis(split, -3, -2).reshape(lead + (3 * heads * HEAD,))


def normalise(value):
    center = value - jnp.mean(value, axis=-1, keepdims=True)
    rstd = lax.rsqrt(jnp.mean(center * center, axis=-1, keepdims=True) + EPS)
    return center * rstd, rstd


def train_kernel(
    heads,
    x_in,
    target_in,
    share_in,
    tables,
    wq_in,
    wd_in,
    w1_in,
    w2_in,
    vec_in,
    out_cols,
    grad_cols,
    grads,
    small,
    wq,
    wd,
    w1,
    w2,
    vec,
    chain,
    norm1,
    norm2,
    qkv,
    ctx,
    act,
    gate,
    key_grad,
    value_grad,
    part,
    got,
    met,
    away,
    probs,
    load_sem,
    give_sem,
    take_sem,
    hop_send,
    hop_recv,
    swap_send,
    swap_recv,
):
    section = lax.axis_index("section")
    place = lax.axis_index("tensor")
    chunks, rows, width = part.shape
    lanes = wd.shape[1]
    columns = out_cols.shape[-1]
    inner = jnp.logical_and(place > 0, place < 3)
    outer = jnp.logical_not(inner)
    beside = jnp.where(place == 0, 1, jnp.where(place == 3, 2, jnp.where(place == 1, 0, 3)))
    across = 3 - place

    def at_place(index):
        return {"tensor": index}

    twin = {"section": 1 - section}

    barrier = pltpu.get_barrier_semaphore()
    pl.semaphore_signal(barrier, inc=1, device_id=twin, device_id_type=MESH)
    pl.semaphore_signal(barrier, inc=1, device_id=at_place(beside), device_id_type=MESH)

    @pl.when(inner)
    def _():
        pl.semaphore_signal(barrier, inc=1, device_id=at_place(across), device_id_type=MESH)

    loads = []
    for index, (source, goal) in enumerate(
        ((wq_in, wq), (vec_in, vec), (w1_in, w1), (wd_in, wd), (w2_in, w2))
    ):
        loads.append(pltpu.make_async_copy(source, goal.at[section], load_sem.at[index]))
    input_load = pltpu.make_async_copy(x_in.at[section], chain.at[0], load_sem.at[5])
    target_load = pltpu.make_async_copy(target_in.at[section], chain.at[3], load_sem.at[6])
    input_load.start()
    for item in loads:
        item.start()
    target_load.start()
    pl.semaphore_wait(barrier, jnp.where(inner, 3, 2))
    gifts = []
    for index, (source, goal) in enumerate(
        ((wq_in, wq), (vec_in, vec), (w1_in, w1), (wd_in, wd), (w2_in, w2))
    ):
        gifts.append(
            pltpu.make_async_remote_copy(
                src_ref=source,
                dst_ref=goal.at[section],
                send_sem=give_sem.at[index],
                recv_sem=take_sem.at[index],
                device_id=twin,
                device_id_type=MESH,
            )
        )
    for item in gifts:
        item.start()

    lane = lax.broadcasted_iota(jnp.int32, (1, lanes), 1) // HEAD
    head_masks = [lane == h for h in range(heads)]
    factor = HEAD ** (-0.5)

    def wide(table, start):
        piece = tables[table, start : start + rows, :]
        return jnp.concatenate([piece] * (lanes // LANES), axis=1)

    def turn(value, start):
        ahead = pltpu.roll(value, lanes - ROT // 2, 1)
        behind = pltpu.roll(value, ROT // 2, 1)
        return value * wide(0, start) + ahead * wide(1, start) + behind * wide(2, start)

    def turn_back(value, start):
        ahead = pltpu.roll(value, lanes - ROT // 2, 1)
        behind = pltpu.roll(value, ROT // 2, 1)
        return value * wide(0, start) - ahead * wide(1, start) - behind * wide(2, start)

    def only(mask, value):
        return jnp.where(mask, value, jnp.zeros_like(value))

    def forward_chunk(layer, c):
        start = c * rows
        here = slice(start, start + rows)
        spread, _ = normalise(chain[layer, c].astype(F32))
        first = (spread * vec[layer, 0:1] + vec[layer, 1:2]).astype(BF16)
        second = (spread * vec[layer, 2:3] + vec[layer, 3:4]).astype(BF16)
        projected = dot_nn(first, wq[layer]) + vec[layer, 5:6]
        query = turn(projected[:, :lanes], start).astype(BF16)
        qkv[layer, here, :lanes] = query
        qkv[layer, here, lanes : 2 * lanes] = turn(projected[:, lanes : 2 * lanes], start).astype(
            BF16
        )
        qkv[layer, here, 2 * lanes :] = projected[:, 2 * lanes :].astype(BF16)
        pre = dot_nn(second, w1[layer]) + vec[layer, 6:7]
        below = 0.5 * (1.0 + lax.erf(pre * (0.5**0.5)))
        active = (pre * below).astype(BF16)
        act[layer, here, :] = active
        slope = below + pre * (jnp.exp(-0.5 * pre * pre) * ((2.0 * np.pi) ** -0.5))
        gate[layer, here, :] = slope.astype(BF16)
        diagonal = lax.broadcasted_iota(jnp.int32, (rows, rows), 0) >= lax.broadcasted_iota(
            jnp.int32, (rows, rows), 1
        )
        context = jnp.zeros((rows, lanes), F32)
        for h in range(heads):
            asked = only(head_masks[h], query) * jnp.asarray(factor, BF16)
            near = dot_nt(asked, qkv[layer, here, lanes : 2 * lanes])
            near = jnp.where(diagonal, near, -1e30)
            highest = jnp.max(near, axis=-1, keepdims=True)
            if c > 0:
                far = dot_nt(asked, qkv[layer, :start, lanes : 2 * lanes])
                highest = jnp.maximum(highest, jnp.max(far, axis=-1, keepdims=True))
                far = jnp.exp(far - highest)
            near = jnp.exp(near - highest)
            total = jnp.sum(near, axis=-1, keepdims=True)
            if c > 0:
                total = total + jnp.sum(far, axis=-1, keepdims=True)
            inverse = 1.0 / total
            near = (near * inverse).astype(BF16)
            probs[c][layer, h, :, start:] = near
            mixed = dot_nn(near, qkv[layer, here, 2 * lanes :])
            if c > 0:
                far = (far * inverse).astype(BF16)
                probs[c][layer, h, :, :start] = far
                mixed = mixed + dot_nn(far, qkv[layer, :start, 2 * lanes :])
            context = jnp.where(head_masks[h], mixed, context)
        context = context.astype(BF16)
        ctx[layer, here, :] = context
        part[c] = (dot_nn(context, wd[layer]) + dot_nn(active, w2[layer])).astype(BF16)

    def backward_chunk(layer, c):
        start = c * rows
        stop = start + rows
        here = slice(start, stop)
        first_turn = c == chunks - 1
        slot = chunks - 1 - c
        cotangent = chain[4 - layer, c]
        context_grad = dot_nt(cotangent, wd[layer]).astype(BF16)
        pre_grad = (dot_nt(cotangent, w2[layer]) * gate[layer, here, :].astype(F32)).astype(BF16)
        gate[layer, here, :] = pre_grad
        second_back = dot_nt(pre_grad, w1[layer])
        query = qkv[layer, here, :lanes]
        weighed = context_grad.astype(F32) * ctx[layer, here, :].astype(F32)
        query_grad = jnp.zeros((rows, lanes), F32)
        key_sum = None
        value_sum = None
        for h in range(heads):
            mask = head_masks[h]
            own_grad = only(mask, context_grad)
            asked = only(mask, query) * jnp.asarray(factor, BF16)
            row_dot = jnp.sum(only(mask, weighed), axis=-1, keepdims=True)
            prob = probs[c][layer, h]
            prob_grad = dot_nt(own_grad, qkv[layer, :stop, 2 * lanes :])
            score_grad = (prob.astype(F32) * (prob_grad - row_dot)).astype(BF16)
            query_grad = jnp.where(
                mask, dot_nn(score_grad, qkv[layer, :stop, lanes : 2 * lanes]), query_grad
            )
            key_part = dot_tn(score_grad, asked)
            value_part = dot_tn(prob, own_grad)
            key_sum = key_part if key_sum is None else key_sum + key_part
            value_sum = value_part if value_sum is None else value_sum + value_part
        if first_turn:
            key_grad[:stop] = key_sum
            value_grad[:stop] = value_sum
        else:
            key_grad[:stop] += key_sum
            value_grad[:stop] += value_sum
        qkv[layer, here, :lanes] = turn_back(query_grad * factor, start).astype(BF16)
        qkv[layer, here, lanes : 2 * lanes] = turn_back(key_grad[here], start).astype(BF16)
        qkv[layer, here, 2 * lanes :] = value_grad[here].astype(BF16)
        projected_grad = qkv[layer, here, :]
        first_back = dot_nt(projected_grad, wq[layer])
        spread, rstd = normalise(chain[layer, c].astype(F32))
        norm1[here] = (spread * vec[layer, 0:1] + vec[layer, 1:2]).astype(BF16)
        norm2[here] = (spread * vec[layer, 2:3] + vec[layer, 3:4]).astype(BF16)
        sums = (
            first_back * spread,
            first_back,
            second_back * spread,
            second_back,
            projected_grad.astype(F32),
            cotangent.astype(F32),
            pre_grad.astype(F32),
        )
        for index, item in enumerate(sums):
            line = jnp.sum(item, axis=0, keepdims=True)
            if first_turn:
                small[layer, index : index + 1] = line
            else:
                small[layer, index : index + 1] += line
        if first_turn:
            small[layer, len(sums) :] = jnp.zeros((8 - len(sums), width), F32)
        back = first_back * vec[layer, 0:1] + second_back * vec[layer, 2:3]
        middle = jnp.mean(back, axis=-1, keepdims=True)
        tilt = jnp.mean(back * spread, axis=-1, keepdims=True)
        part[slot] = (rstd * (back - middle - spread * tilt)).astype(BF16)

    def weight_grads(layer):
        cotangent = chain[4 - layer].reshape(chunks * rows, width)
        step = 256
        base = 0
        for left, right in (
            (norm1, qkv.at[layer]),
            (norm2, gate.at[layer]),
            (act.at[layer], None),
            (ctx.at[layer], None),
        ):
            size = left.shape[-1]
            for at in range(0, size, step):
                grads[layer, base + at : base + at + step] = dot_tn(
                    left[:, at : at + step], cotangent if right is None else right[...]
                ).astype(BF16)
            base += size

    def locate(turn_index):
        kind = turn_index // chunks
        slot = lax.rem(turn_index, chunks)
        row = jnp.where(kind < 2, slot, chunks - 1 - slot)
        base = kind + jnp.where(kind < 2, 0, 1)
        return kind, slot, row, base

    def hop(stage, slot, source, goal, target):
        return pltpu.make_async_remote_copy(
            src_ref=source,
            dst_ref=goal,
            send_sem=hop_send.at[stage, slot],
            recv_sem=hop_recv.at[stage, slot],
            device_id=at_place(target),
            device_id_type=MESH,
        )

    def first_hop(slot):
        return hop(0, slot, part.at[slot], got.at[slot], beside)

    def second_hop(slot):
        return hop(1, slot, part.at[slot], met.at[slot], across)

    def third_hop(slot, row, base):
        piece = chain.at[base + 1, row]
        return hop(2, slot, piece, piece, beside)

    def launch(turn_index):
        _, slot, _, _ = locate(turn_index)

        @pl.when(outer)
        def _():
            first_hop(slot).start()

    def meet(turn_index):
        _, slot, _, _ = locate(turn_index)

        @pl.when(inner)
        def _():
            first_hop(slot).wait_recv()
            part[slot] = (part[slot].astype(F32) + got[slot].astype(F32)).astype(BF16)
            second_hop(slot).start()

    def settle(turn_index):
        kind, slot, row, base = locate(turn_index)

        @pl.when(inner)
        def _():
            second_hop(slot).wait_recv()
            keep = jnp.where(kind < 2, 1.0, 0.0)
            shift = vec[jnp.minimum(kind, 1), 4:5] * keep
            total = part[slot].astype(F32) + met[slot].astype(F32)
            chain[base + 1, row] = (chain[base, row].astype(F32) + (total + shift)).astype(BF16)
            third_hop(slot, row, base).start()

    def finish(turn_index):
        _, slot, row, base = locate(turn_index)

        @pl.when(outer)
        def _():
            first_hop(slot).wait_send()
            third_hop(slot, row, base).wait_recv()

        @pl.when(inner)
        def _():
            second_hop(slot).wait_send()
            third_hop(slot, row, base).wait_send()

    def need(index, layer):
        @pl.when(section == layer)
        def _():
            loads[index].wait()

        @pl.when(section != layer)
        def _():
            gifts[index].wait_recv()

    input_load.wait()

    def forward_layer(layer, carry):
        for index in range(len(loads)):
            need(index, layer)
        for c in range(chunks):
            now = layer * chunks + c

            @pl.when(layer > 0)
            def _():
                finish(now - chunks)

            forward_chunk(layer, c)
            launch(now)

            @pl.when(now > 0)
            def _():
                meet(now - 1)

            @pl.when(now > 1)
            def _():
                settle(now - 2)

        return carry

    lax.fori_loop(0, 2, forward_layer, 0)
    target_load.wait()
    share = share_in[0:1, 0:1]
    for c in range(chunks):
        chain[3, c] = (share * chain[3, c].astype(F32)).astype(BF16)

    def backward_layer(turn_index, carry):
        layer = 1 - turn_index
        for at in range(chunks):
            now = (2 + turn_index) * chunks + at
            finish(now - chunks)
            backward_chunk(layer, chunks - 1 - at)
            launch(now)
            meet(now - 1)
            settle(now - 2)
        weight_grads(layer)
        return carry

    lax.fori_loop(0, 2, backward_layer, 0)
    last = 4 * chunks
    meet(last - 1)
    settle(last - 2)
    settle(last - 1)
    for at in range(chunks):
        finish(last - chunks + at)

    pick = (
        lax.broadcasted_iota(jnp.int32, (width, columns), 0)
        == lax.broadcasted_iota(jnp.int32, (width, columns), 1) + place * columns
    ).astype(BF16)

    def narrow(index):
        return dot_nn(chain[index].reshape(chunks * rows, width), pick).astype(BF16)

    away[0] = narrow(2 - section)
    away[1] = narrow(4 + section)
    swaps = []
    for index, goal in enumerate((out_cols, grad_cols)):
        swaps.append(
            pltpu.make_async_remote_copy(
                src_ref=away.at[index],
                dst_ref=goal.at[section],
                send_sem=swap_send.at[index],
                recv_sem=swap_recv.at[index],
                device_id=twin,
                device_id_type=MESH,
            )
        )
    for item in swaps:
        item.start()
    out_cols[section] = narrow(1 + section)
    grad_cols[section] = narrow(5 - section)
    for item in swaps:
        item.wait()
    for item in gifts:
        item.wait_send()


def train(x, target, share, weights, vec, heads):
    wq, wd, w1, w2 = weights
    count, seq_len, width = x.shape
    rows = min(ROWS, seq_len)
    chunks = seq_len // rows
    lanes = wd.shape[0]
    units = w1.shape[1]
    columns = width // lax.axis_size("tensor")
    tables = jnp.asarray(rotary_tables(seq_len))
    total_rows = width + width + units + lanes
    hbm = pl.BlockSpec(memory_space=pl.ANY)
    vmem = pl.BlockSpec(memory_space=pltpu.VMEM)
    return pl.pallas_call(
        functools.partial(spread_refs, heads, chunks),
        out_shape=(
            jax.ShapeDtypeStruct((count, seq_len, columns), BF16),
            jax.ShapeDtypeStruct((count, seq_len, columns), BF16),
            jax.ShapeDtypeStruct((2, total_rows, width), BF16),
            jax.ShapeDtypeStruct((2, 8, width), F32),
        ),
        in_specs=[hbm, hbm, vmem, vmem, hbm, hbm, hbm, hbm, hbm],
        out_specs=(vmem, vmem, vmem, vmem),
        scratch_shapes=[
            pltpu.VMEM((2,) + wq.shape, BF16),
            pltpu.VMEM((2,) + wd.shape, BF16),
            pltpu.VMEM((2,) + w1.shape, BF16),
            pltpu.VMEM((2,) + w2.shape, BF16),
            pltpu.VMEM((2,) + vec.shape, F32),
            pltpu.VMEM((6, chunks, rows, width), BF16),
            pltpu.VMEM((seq_len, width), BF16),
            pltpu.VMEM((seq_len, width), BF16),
            pltpu.VMEM((2, seq_len, 3 * lanes), BF16),
            pltpu.VMEM((2, seq_len, lanes), BF16),
            pltpu.VMEM((2, seq_len, units), BF16),
            pltpu.VMEM((2, seq_len, units), BF16),
            pltpu.VMEM((seq_len, lanes), F32),
            pltpu.VMEM((seq_len, lanes), F32),
            pltpu.VMEM((chunks, rows, width), BF16),
            pltpu.VMEM((chunks, rows, width), BF16),
            pltpu.VMEM((chunks, rows, width), BF16),
            pltpu.VMEM((2, seq_len, columns), BF16),
        ]
        + [pltpu.VMEM((2, heads, rows, (c + 1) * rows), BF16) for c in range(chunks)]
        + [
            pltpu.SemaphoreType.DMA((7,)),
            pltpu.SemaphoreType.DMA((5,)),
            pltpu.SemaphoreType.DMA((5,)),
            pltpu.SemaphoreType.DMA((3, chunks)),
            pltpu.SemaphoreType.DMA((3, chunks)),
            pltpu.SemaphoreType.DMA((2,)),
            pltpu.SemaphoreType.DMA((2,)),
        ],
        compiler_params=pltpu.CompilerParams(
            collective_id=0, has_side_effects=True, vmem_limit_bytes=63 * 2**20
        ),
    )(
        x.reshape(count, chunks, rows, width),
        target.reshape(count, chunks, rows, width),
        share,
        tables,
        wq,
        wd,
        w1,
        w2,
        vec,
    )


def spread_refs(heads, chunks, *refs):
    before = 9 + 4 + 18
    train_kernel(heads, *refs[:before], refs[before : before + chunks], *refs[before + chunks :])


def per_device(
    hidden_in,
    target,
    tissue,
    ln1_gain,
    ln1_bias,
    ln2_gain,
    ln2_bias,
    qkv_weight,
    qkv_bias,
    dense_weight,
    dense_bias,
    fc1_weight,
    fc1_bias,
    fc2_weight,
    fc2_bias,
):
    count, seq_len, width = hidden_in.shape
    section = lax.axis_index("section")
    heads = qkv_weight.shape[-1] // (3 * HEAD)
    lanes = -(-heads * HEAD // LANES) * LANES
    units = fc1_weight.shape[-1]
    labels = (tissue[:, None] == jnp.arange(TISSUES)[None, :]).astype(F32)
    counts = lax.psum(jnp.sum(labels, axis=0), "dp")
    own_count = jnp.sum(labels * counts[None, :], axis=1)
    share = count * lax.axis_size("dp") / TISSUES / own_count
    own_share = lax.dynamic_index_in_dim(share, section, 0, keepdims=False)
    share_tile = jnp.full((8, LANES), own_share, F32)
    weights = (
        pack_columns(qkv_weight[0], lanes),
        jnp.pad(dense_weight[0], [(0, lanes - heads * HEAD), (0, 0)]),
        fc1_weight[0],
        fc2_weight[0],
    )
    vec = jnp.stack(
        [
            ln1_gain[0].astype(F32),
            ln1_bias[0].astype(F32),
            ln2_gain[0].astype(F32),
            ln2_bias[0].astype(F32),
            dense_bias[0].astype(F32) + fc2_bias[0].astype(F32),
            pack_columns(qkv_bias[0], lanes).astype(F32),
            fc1_bias[0].astype(F32),
            jnp.zeros((width,), F32),
        ]
    )
    out_cols, grad_cols, grads, small = train(hidden_in, target, share_tile, weights, vec, heads)
    own = lax.dynamic_index_in_dim(grads, section, 0, keepdims=False)
    other = lax.dynamic_index_in_dim(grads, 1 - section, 0, keepdims=False)
    other = lax.ppermute(other, "section", [(0, 1), (1, 0)])
    total = lax.psum(own + other, "dp").astype(F32)
    small = lax.psum(small, ("section", "dp"))
    small = lax.dynamic_index_in_dim(small, section, 0, keepdims=False)
    norms = lax.psum(small[:4], "tensor")
    valid = heads * HEAD
    return (
        out_cols[None],
        grad_cols.astype(F32)[None],
        norms[0:1],
        norms[1:2],
        norms[2:3],
        norms[3:4],
        unpack_columns(total[:width], heads)[None],
        unpack_columns(small[4], heads)[None],
        total[2 * width + units :][:valid][None],
        small[5:6],
        total[width : 2 * width][None],
        small[6:7],
        total[2 * width : 2 * width + units][None],
        small[5:6],
    )


def solution(mesh):
    return jax.shard_map(
        per_device,
        mesh=mesh,
        in_specs=(
            P("dp", None, None),
            P("dp", None, None),
            P("dp"),
            P("section", None),
            P("section", None),
            P("section", None),
            P("section", None),
            P("section", None, "tensor"),
            P("section", "tensor"),
            P("section", "tensor", None),
            P("section", None),
            P("section", None, "tensor"),
            P("section", "tensor"),
            P("section", "tensor", None),
            P("section", None),
        ),
        out_specs=(
            P("section", "dp", None, "tensor"),
            P("section", "dp", None, "tensor"),
            P("section", None),
            P("section", None),
            P("section", None),
            P("section", None),
            P("section", None, "tensor"),
            P("section", "tensor"),
            P("section", "tensor", None),
            P("section", None),
            P("section", None, "tensor"),
            P("section", "tensor"),
            P("section", "tensor", None),
            P("section", None),
        ),
        check_vma=False,
    )
```

```python
import functools
import math

import jax
import jax.numpy as jnp
import numpy as np
from jax import lax
from jax.experimental import pallas as pl
from jax.experimental.pallas import tpu as pltpu
from jax.sharding import PartitionSpec as P

HEAD = 64
ROT = 16
TISSUES = 16
ROWS = 256
LANES = 128
EPS = 1e-05
MESH = pl.DeviceIdType.MESH
F32 = jnp.float32
BF16 = jnp.bfloat16


def dot_nn(a, b):
    return lax.dot_general(a, b, (((1,), (0,)), ((), ())), preferred_element_type=F32)


def dot_nt(a, b):
    return lax.dot_general(a, b, (((1,), (1,)), ((), ())), preferred_element_type=F32)


def dot_tn(a, b):
    return lax.dot_general(a, b, (((0,), (0,)), ((), ())), preferred_element_type=F32)


def rotary_tables(seq_len):
    half = ROT // 2
    inverse = 10000.0 ** (-2.0 * np.arange(half) / ROT)
    angles = np.arange(seq_len)[:, None] * inverse[None, :]
    cosines = np.ones((seq_len, HEAD))
    sines = np.zeros((seq_len, HEAD))
    cosines[:, :half] = np.cos(angles)
    cosines[:, half:ROT] = np.cos(angles)
    sines[:, :half] = -np.sin(angles)
    sines[:, half:ROT] = np.sin(angles)
    tables = np.stack([np.tile(item, (1, LANES // HEAD)) for item in (cosines, sines)])
    return tables.astype(np.float32)


def unpack_rows(packed, heads):
    width = packed.shape[-1]
    split = packed.reshape(3, heads, HEAD, width)
    return split.transpose(3, 1, 0, 2).reshape(width, 3 * heads * HEAD)


def unpack_line(line, heads):
    split = line.reshape(3, -1)[:, : heads * HEAD].reshape(3, heads, HEAD)
    return split.transpose(1, 0, 2).reshape(1, 3 * heads * HEAD)


def normalise(value):
    center = value - jnp.mean(value, axis=-1, keepdims=True)
    rstd = lax.rsqrt(jnp.mean(center * center, axis=-1, keepdims=True) + EPS)
    return center * rstd, rstd


def train_kernel(
    heads,
    x_in,
    target_in,
    tissue,
    tables,
    wq_in,
    wd_in,
    w1_in,
    w2_in,
    qkv_bias,
    vec_in,
    out_cols,
    grad_cols,
    grads,
    small,
    wq,
    wd,
    w1,
    w2,
    raw,
    vec,
    chain,
    qkv,
    ctx,
    act,
    gate,
    key_grad,
    value_grad,
    part,
    got,
    met,
    total,
    half_got,
    first_got,
    second_got,
    more_got,
    line_got,
    tally,
    tally_got,
    probs,
    load_sem,
    give_sem,
    take_sem,
    hop_send,
    hop_recv,
    swap_send,
    swap_recv,
    sum_send,
    sum_recv,
    line_send,
    line_recv,
    tally_send,
    tally_recv,
    store_sem,
):
    section = lax.axis_index("section")
    replica = lax.axis_index("dp")
    place = lax.axis_index("tensor")
    copies = lax.axis_size("dp")
    bits = copies.bit_length() - 1
    chunks, rows, width = part.shape
    lanes = wd.shape[1]
    valid = heads * HEAD
    padded = out_cols.shape[-1]
    columns = width // lax.axis_size("tensor")
    inner = jnp.logical_and(place > 0, place < 3)
    outer = jnp.logical_not(inner)
    beside = place + 1 - 2 * lax.rem(place, 2)
    across = 3 - place

    def flipped(bit):
        return replica + (1 << bit) * (1 - 2 * lax.rem(replica // (1 << bit), 2))

    twin = {"section": 1 - section}
    mates = [{"dp": flipped(bit)} for bit in range(bits)]
    near = {"tensor": beside}
    far = {"tensor": across}
    friends = [twin, near, far] + mates

    def send(source, goal, sems, target):
        return pltpu.make_async_remote_copy(
            src_ref=source,
            dst_ref=goal,
            send_sem=sems[0],
            recv_sem=sems[1],
            device_id=target,
            device_id_type=MESH,
        )

    barrier = pltpu.get_barrier_semaphore()
    for friend in friends:
        pl.semaphore_signal(barrier, inc=1, device_id=friend, device_id_type=MESH)

    raw_load = pltpu.make_async_copy(wq_in, raw, load_sem.at[0])
    raw_load.start()
    input_load = pltpu.make_async_copy(x_in.at[section], chain.at[0], load_sem.at[1])
    input_load.start()
    pairs = ((w1_in, w1.at[section]), (wd_in, wd.at[section, :valid]), (w2_in, w2.at[section]))
    loads = [
        pltpu.make_async_copy(source, goal, load_sem.at[2 + index])
        for index, (source, goal) in enumerate(pairs)
    ]
    for item in loads:
        item.start()
    target_load = pltpu.make_async_copy(target_in.at[section], chain.at[3], load_sem.at[5])
    target_load.start()

    column = lax.broadcasted_iota(jnp.int32, (3 * valid, 3 * lanes), 0)
    head_of, rest = column // (3 * HEAD), lax.rem(column, 3 * HEAD)
    goal_of = (rest // HEAD) * lanes + head_of * HEAD + lax.rem(rest, HEAD)
    pack = (goal_of == lax.broadcasted_iota(jnp.int32, goal_of.shape, 1)).astype(BF16)
    for index, item in enumerate(vec_in):
        vec[section, index : index + 1] = item[...].astype(F32)
    vec[section, 4:5] = vec_in[4][...].astype(F32) + vec_in[5][...].astype(F32)
    vec[section, 5:6] = dot_nn(jnp.broadcast_to(qkv_bias[...], (16, 3 * valid)), pack)[0:1]
    vec[section, 7:8] = jnp.zeros((1, width), F32)
    for layer in range(2):
        wd[layer, valid:] = jnp.zeros((lanes - valid, width), BF16)
    raw_load.wait()
    wq[section] = dot_nn(raw[...], pack).astype(BF16)
    pl.semaphore_wait(barrier, len(friends))
    gifts = [
        send(source, goal, (give_sem.at[index], take_sem.at[index]), twin)
        for index, (source, goal) in enumerate(
            ((wq.at[section], wq.at[section]), (vec.at[section], vec.at[section])) + pairs
        )
    ]
    for item in gifts:
        item.start()

    tissue_lane = lax.broadcasted_iota(jnp.int32, (8, LANES), 1)
    marks = [(tissue_lane == tissue[index]).astype(F32) for index in range(tissue.shape[0])]
    tally[...] = functools.reduce(lambda a, b: a + b, marks)

    def tally_step(bit):
        return send(
            tally, tally_got.at[bit], (tally_send.at[bit], tally_recv.at[bit]), mates[bit]
        )

    if bits:
        tally_step(0).start()

    def count_on(bit):
        step = tally_step(bit)
        step.wait()
        tally[...] += tally_got[bit]
        if bit + 1 < bits:
            tally_step(bit + 1).start()

    lane = lax.broadcasted_iota(jnp.int32, (1, lanes), 1) // HEAD
    head_masks = [lane == h for h in range(heads)]
    factor = HEAD ** (-0.5)

    left_half = lax.rem(lax.broadcasted_iota(jnp.int32, (1, lanes), 1), HEAD) < ROT // 2

    def wide(table, start):
        piece = tables[table, start : start + rows, :]
        return jnp.concatenate([piece] * (lanes // LANES), axis=1)

    def turned(value):
        ahead = pltpu.roll(value, lanes - ROT // 2, 1)
        behind = pltpu.roll(value, ROT // 2, 1)
        return jnp.where(left_half, ahead, behind)

    def turn(value, start):
        return value * wide(0, start) + turned(value) * wide(1, start)

    def turn_back(value, start):
        return value * wide(0, start) - turned(value) * wide(1, start)

    def only(mask, value):
        return jnp.where(mask, value, jnp.zeros_like(value))

    def forward_chunk(layer, c):
        start = c * rows
        here = slice(start, start + rows)
        spread, _ = normalise(chain[layer, c].astype(F32))
        first = (spread * vec[layer, 0:1] + vec[layer, 1:2]).astype(BF16)
        second = (spread * vec[layer, 2:3] + vec[layer, 3:4]).astype(BF16)
        projected = dot_nn(first, wq[layer]) + vec[layer, 5:6]
        query = turn(projected[:, :lanes], start).astype(BF16)
        qkv[layer, here, :lanes] = query
        qkv[layer, here, lanes : 2 * lanes] = turn(projected[:, lanes : 2 * lanes], start).astype(
            BF16
        )
        qkv[layer, here, 2 * lanes :] = projected[:, 2 * lanes :].astype(BF16)
        pre = dot_nn(second, w1[layer]) + vec[layer, 6:7]
        below = 0.5 * (1.0 + lax.erf(pre * (0.5**0.5)))
        active = (pre * below).astype(BF16)
        act[layer, here, :] = active
        slope = below + pre * (jnp.exp(-0.5 * pre * pre) * ((2.0 * np.pi) ** -0.5))
        gate[layer, here, :] = slope.astype(BF16)
        diagonal = lax.broadcasted_iota(jnp.int32, (rows, rows), 0) >= lax.broadcasted_iota(
            jnp.int32, (rows, rows), 1
        )
        context = jnp.zeros((rows, lanes), F32)
        for h in range(heads):
            asked = only(head_masks[h], query) * jnp.asarray(factor, BF16)
            near = dot_nt(asked, qkv[layer, here, lanes : 2 * lanes])
            near = jnp.where(diagonal, near, -1e30)
            highest = jnp.max(near, axis=-1, keepdims=True)
            if c > 0:
                far = dot_nt(asked, qkv[layer, :start, lanes : 2 * lanes])
                highest = jnp.maximum(highest, jnp.max(far, axis=-1, keepdims=True))
                far = jnp.exp(far - highest)
            near = jnp.exp(near - highest)
            total = jnp.sum(near, axis=-1, keepdims=True)
            if c > 0:
                total = total + jnp.sum(far, axis=-1, keepdims=True)
            inverse = 1.0 / total
            near = (near * inverse).astype(BF16)
            probs[c][layer, h, :, start:] = near
            mixed = dot_nn(near, qkv[layer, here, 2 * lanes :])
            if c > 0:
                far = (far * inverse).astype(BF16)
                probs[c][layer, h, :, :start] = far
                mixed = mixed + dot_nn(far, qkv[layer, :start, 2 * lanes :])
            context = jnp.where(head_masks[h], mixed, context)
        context = context.astype(BF16)
        ctx[layer, here, :] = context
        part[c] = (dot_nn(context, wd[layer]) + dot_nn(active, w2[layer])).astype(BF16)

    def backward_chunk(layer, c):
        start = c * rows
        stop = start + rows
        here = slice(start, stop)
        first_turn = c == chunks - 1
        slot = chunks - 1 - c
        cotangent = chain[4 - layer, c]
        context_grad = dot_nt(cotangent, wd[layer]).astype(BF16)
        pre_grad = (dot_nt(cotangent, w2[layer]) * gate[layer, here, :].astype(F32)).astype(BF16)
        gate[layer, here, :] = pre_grad
        second_back = dot_nt(pre_grad, w1[layer])
        query = qkv[layer, here, :lanes]
        weighed = context_grad.astype(F32) * ctx[layer, here, :].astype(F32)
        query_grad = jnp.zeros((rows, lanes), F32)
        key_sum = None
        value_sum = None
        for h in range(heads):
            mask = head_masks[h]
            own_grad = only(mask, context_grad)
            asked = only(mask, query) * jnp.asarray(factor, BF16)
            row_dot = jnp.sum(only(mask, weighed), axis=-1, keepdims=True)
            prob = probs[c][layer, h]
            prob_grad = dot_nt(own_grad, qkv[layer, :stop, 2 * lanes :])
            score_grad = (prob.astype(F32) * (prob_grad - row_dot)).astype(BF16)
            query_grad = jnp.where(
                mask, dot_nn(score_grad, qkv[layer, :stop, lanes : 2 * lanes]), query_grad
            )
            key_part = dot_tn(score_grad, asked)
            value_part = dot_tn(prob, own_grad)
            key_sum = key_part if key_sum is None else key_sum + key_part
            value_sum = value_part if value_sum is None else value_sum + value_part
        if first_turn:
            key_grad[:stop] = key_sum
            value_grad[:stop] = value_sum
        else:
            key_grad[:stop] += key_sum
            value_grad[:stop] += value_sum
        qkv[layer, here, :lanes] = turn_back(query_grad * factor, start).astype(BF16)
        qkv[layer, here, lanes : 2 * lanes] = turn_back(key_grad[here], start).astype(BF16)
        qkv[layer, here, 2 * lanes :] = value_grad[here].astype(BF16)
        projected_grad = qkv[layer, here, :]
        first_back = dot_nt(projected_grad, wq[layer])
        spread, rstd = normalise(chain[layer, c].astype(F32))
        first = (spread * vec[layer, 0:1] + vec[layer, 1:2]).astype(BF16)
        second = (spread * vec[layer, 2:3] + vec[layer, 3:4]).astype(BF16)
        sums = (
            first_back * spread,
            first_back,
            second_back * spread,
            second_back,
            projected_grad.astype(F32),
            cotangent.astype(F32),
            pre_grad.astype(F32),
        )
        for index, item in enumerate(sums):
            line = jnp.sum(item, axis=0, keepdims=True)
            if first_turn:
                small[layer, index : index + 1] = line
            else:
                small[layer, index : index + 1] += line
        if first_turn:
            small[layer, len(sums) :] = jnp.zeros((8 - len(sums), width), F32)
        back = first_back * vec[layer, 0:1] + second_back * vec[layer, 2:3]
        middle = jnp.mean(back, axis=-1, keepdims=True)
        tilt = jnp.mean(back * spread, axis=-1, keepdims=True)
        part[slot] = (rstd * (back - middle - spread * tilt)).astype(BF16)
        return here, first_turn, first, second, pre_grad, cotangent

    def add_weight_grads(layer, here, first_turn, first, second, pre_grad, cotangent):
        step = lanes
        base = 0
        sources = (
            (qkv.at[layer, here], first, valid),
            (second, pre_grad, step),
            (act.at[layer, here], cotangent, step),
            (ctx.at[layer, here], cotangent, valid),
        )
        for left, right, kept in sources:
            for at in range(0, left.shape[-1], step):
                piece = dot_tn(left[:, at : at + step], right)[:kept]
                goal = slice(base, base + kept)
                if not first_turn:
                    piece = piece + total[layer, goal].astype(F32)
                total[layer, goal] = piece.astype(BF16)
                base += kept

    all_rows = total.shape[1]
    share_rows = all_rows // 2
    folds = min(bits, 2)

    def spans(group):
        order = (0, 1)[:folds] if group == 0 else (1, 0)[-folds:] if folds else ()
        size = share_rows // 2
        start = section * share_rows + group * size
        steps = []
        for bit in order:
            size = size // 2
            upper = lax.rem(replica // (1 << bit), 2)
            steps.append((bit, start + upper * size, start + (1 - upper) * size, size))
            start = start + upper * size
        return steps, start, size

    groups = [spans(0), spans(1)]
    sum_steps = 2 + 2 * folds + (bits - folds)

    group_rows = share_rows // 2

    def sums_of(layer, start, size):
        return total.at[layer, pl.ds(pl.multiple_of(start, 16), size)]

    def gathered(layer, group, start, size):
        start = start - section * share_rows - group * group_rows
        return (act, gate)[group].at[layer, pl.ds(pl.multiple_of(start, 16), size)]

    def sum_sems(layer, step, group):
        return sum_send.at[layer, step, group], sum_recv.at[layer, step, group]

    def sum_copies(layer, step):
        if step == 0:
            source = sums_of(layer, (1 - section) * share_rows, share_rows)
            return [send(source, half_got.at[layer], sum_sems(layer, 0, 0), twin)]
        copies_now = []
        for group, (steps, start, size) in enumerate(groups):
            sems = sum_sems(layer, step, group)
            if step <= folds:
                bit, _, gone, size = steps[step - 1]
                goal = (first_got, second_got)[step - 1].at[group]
                copies_now.append(send(sums_of(layer, gone, size), goal, sems, mates[bit]))
            elif step <= bits:
                goal = more_got.at[layer, step - 1 - folds, group]
                source = gathered(layer, group, start, size)
                copies_now.append(send(source, goal, sems, mates[step - 1]))
            else:
                bit, start, _, size = steps[bits - step]
                piece = gathered(layer, group, start, size)
                copies_now.append(send(piece, piece, sems, mates[bit]))
        return copies_now

    def last_copies(layer):
        pieces = []
        for group in range(2):
            first_row = section * share_rows + group * group_rows
            piece = gathered(layer, group, first_row, group_rows)
            goal = grads.at[pl.ds(pl.multiple_of(first_row, 16), group_rows)]
            sems = sum_sems(layer, sum_steps - 1, group)
            other_row = (1 - section) * share_rows + group * group_rows
            other = grads.at[pl.ds(pl.multiple_of(other_row, 16), group_rows)]
            pieces.append(
                (
                    send(piece, goal, sems, twin),
                    send(piece, other, sems, twin),
                    pltpu.make_async_copy(piece, goal, store_sem.at[group]),
                )
            )
        return pieces

    def sum_start(layer, step):
        if step < sum_steps - 1:
            for item in sum_copies(layer, step):
                item.start()
            return
        for give, _, keep in last_copies(layer):
            pl.when(section != layer)(give.start)
            pl.when(section == layer)(keep.start)

    def add_rows(goal, base, source):
        size = source.shape[0]
        piece = math.gcd(size, 144)

        def add_piece(index, carry):
            here = pl.ds(pl.multiple_of(index * piece, 16), piece)
            goal[here] = (base[here].astype(F32) + source[here].astype(F32)).astype(BF16)
            return carry

        lax.fori_loop(0, size // piece, add_piece, 0)

    def sum_end(layer, step):
        if step == sum_steps - 1:
            for give, take, keep in last_copies(layer):
                pl.when(section != layer)(give.wait_send)
                pl.when(section == layer)(take.wait_recv)
                pl.when(section == layer)(keep.wait)
            return
        for item in sum_copies(layer, step):
            item.wait()
        if step == 0:
            base = sums_of(layer, section * share_rows, share_rows)
            add_rows(base, base, half_got.at[layer])
            return
        if step > bits:
            return
        for group, (steps, start, size) in enumerate(groups):
            goal = gathered(layer, group, start, size)
            if step < folds:
                base = sums_of(layer, steps[step - 1][1], steps[step - 1][3])
                add_rows(base, base, first_got.at[group])
            elif step == folds:
                add_rows(goal, sums_of(layer, start, size), second_got.at[group])
            else:
                add_rows(goal, goal, more_got.at[layer, step - 1 - folds, group])

    line_friends = [twin] + mates + [near, far]

    def line_copy(step):
        sems = (line_send.at[step], line_recv.at[step])
        return send(small, line_got.at[step], sems, line_friends[step])

    def line_end(step):
        line_copy(step).wait()
        if step <= bits:
            small[...] += line_got[step]
        else:
            small[:, 0:4] += line_got[step, :, 0:4]

    def locate(turn_index):
        kind = turn_index // chunks
        slot = lax.rem(turn_index, chunks)
        row = jnp.where(kind < 2, slot, chunks - 1 - slot)
        base = kind + jnp.where(kind < 2, 0, 1)
        goal = jnp.where(kind == 3, 3, base + 1)
        return kind, slot, row, base, goal

    def hop(stage, slot, source, goal, target):
        return pltpu.make_async_remote_copy(
            src_ref=source,
            dst_ref=goal,
            send_sem=hop_send.at[stage, slot],
            recv_sem=hop_recv.at[stage, slot],
            device_id=target,
            device_id_type=MESH,
        )

    def first_hop(slot):
        return hop(0, slot, part.at[slot], got.at[slot], near)

    def second_hop(slot):
        return hop(1, slot, part.at[slot], met.at[slot], far)

    def third_hop(slot, row, goal):
        piece = chain.at[goal, row]
        return hop(2, slot, piece, piece, near)

    def launch(turn_index):
        _, slot, _, _, _ = locate(turn_index)

        @pl.when(outer)
        def _():
            first_hop(slot).start()

    def meet(turn_index):
        _, slot, _, _, _ = locate(turn_index)

        @pl.when(inner)
        def _():
            first_hop(slot).wait_recv()
            part[slot] = (part[slot].astype(F32) + got[slot].astype(F32)).astype(BF16)
            second_hop(slot).start()

    def settle(turn_index):
        kind, slot, row, base, goal = locate(turn_index)

        @pl.when(inner)
        def _():
            second_hop(slot).wait_recv()
            keep = jnp.where(kind < 2, 1.0, 0.0)
            shift = vec[jnp.minimum(kind, 1), 4:5] * keep
            total = part[slot].astype(F32) + met[slot].astype(F32)
            chain[goal, row] = (chain[base, row].astype(F32) + (total + shift)).astype(BF16)
            third_hop(slot, row, goal).start()

    def finish(turn_index):
        _, slot, row, _, goal = locate(turn_index)

        @pl.when(outer)
        def _():
            first_hop(slot).wait_send()
            third_hop(slot, row, goal).wait_recv()

        @pl.when(inner)
        def _():
            second_hop(slot).wait_send()
            third_hop(slot, row, goal).wait_send()

    def need(index, layer):
        @pl.when(section == layer)
        def _():
            if index > 1:
                loads[index - 2].wait()

        @pl.when(section != layer)
        def _():
            gifts[index].wait_recv()

    input_load.wait()

    def forward_layer(layer, carry):
        for index in range(len(gifts)):
            need(index, layer)
        for c in range(chunks):
            now = layer * chunks + c

            @pl.when(layer > 0)
            def _():
                finish(now - chunks)

            forward_chunk(layer, c)
            launch(now)

            @pl.when(now > 0)
            def _():
                meet(now - 1)

            @pl.when(now > 1)
            def _():
                settle(now - 2)

            for bit in range(bits):
                if bit % chunks == c:
                    pl.when(layer == bit // chunks)(functools.partial(count_on, bit))
        return carry

    lax.fori_loop(0, 2, forward_layer, 0)
    target_load.wait()
    own_mark = jnp.where(section == 0, marks[0], marks[1])[0:1]
    own_count = jnp.sum(own_mark * tally[0:1], axis=-1, keepdims=True)
    share = (tissue.shape[0] * copies / TISSUES) / own_count
    for c in range(chunks):
        chain[3, c] = (share * chain[3, c].astype(F32)).astype(BF16)

    def backward_layer(turn_index, carry):
        layer = 1 - turn_index
        for at in range(chunks):
            now = (2 + turn_index) * chunks + at
            if at == 0:

                @pl.when(layer == 0)
                def _():
                    sum_end(1, 0)
                    sum_start(1, 1)

            finish(now - chunks)

            @pl.when(layer == 0)
            def _():
                sum_end(1, at + 1)
                sum_start(1, at + 2)

            kept = backward_chunk(layer, chunks - 1 - at)
            launch(now)
            add_weight_grads(layer, *kept)
            meet(now - 1)
            settle(now - 2)

        sum_start(layer, 0)
        return carry

    lax.fori_loop(0, 2, backward_layer, 0)
    last = 4 * chunks
    line_copy(0).start()
    meet(last - 1)
    settle(last - 2)
    for step in range(chunks + 1, sum_steps - 1):
        sum_end(1, step)
        sum_start(1, step + 1)
    for step in range(max(sum_steps, len(line_friends))):
        if step < sum_steps:
            sum_end(0, step)
            if step + 1 < sum_steps:
                sum_start(0, step + 1)
        if step < len(line_friends):
            line_end(step)
            if step + 1 < len(line_friends):
                line_copy(step + 1).start()
        if step == 0:
            settle(last - 1)
            sum_end(1, sum_steps - 1)
    for at in range(chunks):
        finish(last - chunks + at)

    own_column = lax.broadcasted_iota(jnp.int32, (width, padded), 1)
    pick = jnp.logical_and(
        lax.broadcasted_iota(jnp.int32, (width, padded), 0) == own_column + place * columns,
        own_column < columns,
    ).astype(BF16)

    def narrow(index, goal):
        def narrow_chunk(c, carry):
            here = pl.ds(pl.multiple_of(c * rows, rows), rows)
            goal[here] = dot_nn(chain[index, c], pick).astype(BF16)
            return carry

        lax.fori_loop(0, chunks, narrow_chunk, 0)

    goals = (out_cols, grad_cols)
    away = [qkv.at[0, :, index * padded : (index + 1) * padded] for index in range(2)]
    home = [qkv.at[1, :, index * padded : (index + 1) * padded] for index in range(2)]
    moves = []
    for index, goal in enumerate(goals):
        narrow((2 - section, 4 - section)[index], away[index])
        sems = (swap_send.at[index], swap_recv.at[index])
        moves.append(send(away[index], goal.at[section], sems, twin))
        moves[-1].start()
        narrow((1 + section, 3 + section)[index], home[index])
        moves.append(
            pltpu.make_async_copy(home[index], goal.at[section], load_sem.at[1 + index])
        )
        moves[-1].start()
    for item in moves:
        item.wait()
    for item in gifts:
        item.wait_send()


def train(x, target, tissue, weights, qkv_bias, vec):
    wq, wd, w1, w2 = weights
    count, seq_len, width = x.shape
    rows = min(ROWS, seq_len)
    chunks = seq_len // rows
    valid = wd.shape[0]
    heads = valid // HEAD
    lanes = -(-valid // LANES) * LANES
    units = w1.shape[1]
    columns = -(-width // lax.axis_size("tensor") // LANES) * LANES
    bits = lax.axis_size("dp").bit_length() - 1
    tables = jnp.asarray(rotary_tables(seq_len))
    total_rows = 3 * valid + width + units + valid
    hbm = pl.BlockSpec(memory_space=pl.ANY)
    vmem = pl.BlockSpec(memory_space=pltpu.VMEM)
    smem = pl.BlockSpec(memory_space=pltpu.SMEM)
    return pl.pallas_call(
        functools.partial(gather_refs, heads, chunks, len(vec)),
        out_shape=(
            jax.ShapeDtypeStruct((count, seq_len, columns), BF16),
            jax.ShapeDtypeStruct((count, seq_len, columns), BF16),
            jax.ShapeDtypeStruct((total_rows, width), BF16),
            jax.ShapeDtypeStruct((2, 8, width), F32),
        ),
        in_specs=[hbm, hbm, smem, vmem, hbm, hbm, hbm, hbm, vmem] + [vmem] * len(vec),
        out_specs=(hbm, hbm, hbm, vmem),
        scratch_shapes=[
            pltpu.VMEM((2, width, 3 * lanes), BF16),
            pltpu.VMEM((2, lanes, width), BF16),
            pltpu.VMEM((2,) + w1.shape, BF16),
            pltpu.VMEM((2,) + w2.shape, BF16),
            pltpu.VMEM(wq.shape, BF16),
            pltpu.VMEM((2, 8, width), F32),
            pltpu.VMEM((5, chunks, rows, width), BF16),
            pltpu.VMEM((2, seq_len, 3 * lanes), BF16),
            pltpu.VMEM((2, seq_len, lanes), BF16),
            pltpu.VMEM((2, seq_len, units), BF16),
            pltpu.VMEM((2, seq_len, units), BF16),
            pltpu.VMEM((seq_len, lanes), F32),
            pltpu.VMEM((seq_len, lanes), F32),
            pltpu.VMEM((chunks, rows, width), BF16),
            pltpu.VMEM((chunks, rows, width), BF16),
            pltpu.VMEM((chunks, rows, width), BF16),
            pltpu.VMEM((2, total_rows, width), BF16),
            pltpu.VMEM((2, total_rows // 2, width), BF16),
            pltpu.VMEM((2, total_rows // 8, width), BF16),
            pltpu.VMEM((2, total_rows // 16, width), BF16),
            pltpu.VMEM((2, max(bits - 2, 1), 2, total_rows // 16 if bits > 2 else 16, width), BF16),
            pltpu.VMEM((3 + bits, 2, 8, width), F32),
            pltpu.VMEM((8, LANES), F32),
            pltpu.VMEM((max(bits, 1), 8, LANES), F32),
        ]
        + [pltpu.VMEM((2, heads, rows, (c + 1) * rows), BF16) for c in range(chunks)]
        + [
            pltpu.SemaphoreType.DMA((6,)),
            pltpu.SemaphoreType.DMA((5,)),
            pltpu.SemaphoreType.DMA((5,)),
            pltpu.SemaphoreType.DMA((3, chunks)),
            pltpu.SemaphoreType.DMA((3, chunks)),
            pltpu.SemaphoreType.DMA((2,)),
            pltpu.SemaphoreType.DMA((2,)),
            pltpu.SemaphoreType.DMA((2, bits + 4, 2)),
            pltpu.SemaphoreType.DMA((2, bits + 4, 2)),
            pltpu.SemaphoreType.DMA((3 + bits,)),
            pltpu.SemaphoreType.DMA((3 + bits,)),
            pltpu.SemaphoreType.DMA((max(bits, 1),)),
            pltpu.SemaphoreType.DMA((max(bits, 1),)),
            pltpu.SemaphoreType.DMA((2,)),
        ],
        compiler_params=pltpu.CompilerParams(
            collective_id=0, has_side_effects=True, vmem_limit_bytes=63 * 2**20
        ),
    )(
        x.reshape(count, chunks, rows, width),
        target.reshape(count, chunks, rows, width),
        tissue,
        tables,
        wq,
        wd,
        w1,
        w2,
        qkv_bias,
        *vec,
    )


def gather_refs(heads, chunks, lines, *refs):
    ends = (9, 9 + lines, 9 + lines + 4 + 24)
    probs = refs[ends[2] : ends[2] + chunks]
    head, vec, body = refs[: ends[0]], refs[ends[0] : ends[1]], refs[ends[1] : ends[2]]
    train_kernel(heads, *head, vec, *body, probs, *refs[ends[2] + chunks :])


def per_device(
    hidden_in,
    target,
    tissue,
    ln1_gain,
    ln1_bias,
    ln2_gain,
    ln2_bias,
    qkv_weight,
    qkv_bias,
    dense_weight,
    dense_bias,
    fc1_weight,
    fc1_bias,
    fc2_weight,
    fc2_bias,
):
    width = hidden_in.shape[-1]
    section = lax.axis_index("section")
    valid = dense_weight.shape[1]
    heads = valid // HEAD
    units = fc1_weight.shape[-1]
    weights = (qkv_weight[0], dense_weight[0], fc1_weight[0], fc2_weight[0])
    vec = (ln1_gain, ln1_bias, ln2_gain, ln2_bias, dense_bias, fc2_bias, fc1_bias)
    out_cols, grad_cols, total, small = train(hidden_in, target, tissue, weights, qkv_bias, vec)
    small = lax.dynamic_index_in_dim(small, section, 0, keepdims=False)
    columns = width // lax.axis_size("tensor")
    total = total.astype(F32)
    ends = np.cumsum([3 * valid, width, units])
    return (
        out_cols[None, ..., :columns],
        grad_cols[None, ..., :columns].astype(F32),
        small[0:1],
        small[1:2],
        small[2:3],
        small[3:4],
        unpack_rows(total[: ends[0]], heads)[None],
        unpack_line(small[4], heads),
        total[ends[2] :][None],
        small[5:6],
        total[ends[0] : ends[1]][None],
        small[6:7],
        total[ends[1] : ends[2]][None],
        small[5:6],
    )


def solution(mesh):
    return jax.shard_map(
        per_device,
        mesh=mesh,
        in_specs=(
            P("dp", None, None),
            P("dp", None, None),
            P("dp"),
            P("section", None),
            P("section", None),
            P("section", None),
            P("section", None),
            P("section", None, "tensor"),
            P("section", "tensor"),
            P("section", "tensor", None),
            P("section", None),
            P("section", None, "tensor"),
            P("section", "tensor"),
            P("section", "tensor", None),
            P("section", None),
        ),
        out_specs=(
            P("section", "dp", None, "tensor"),
            P("section", "dp", None, "tensor"),
            P("section", None),
            P("section", None),
            P("section", None),
            P("section", None),
            P("section", None, "tensor"),
            P("section", "tensor"),
            P("section", "tensor", None),
            P("section", None),
            P("section", None, "tensor"),
            P("section", "tensor"),
            P("section", "tensor", None),
            P("section", None),
        ),
        check_vma=False,
    )
```

```python
import functools
import math

import jax
import jax.numpy as jnp
import numpy as np
from jax import lax
from jax.experimental import pallas as pl
from jax.experimental.pallas import tpu as pltpu
from jax.sharding import PartitionSpec as P

HEAD = 64
ROT = 16
TISSUES = 16
ROWS = 256
UNIT = 128
LANES = 128
EPS = 1e-05
MESH = pl.DeviceIdType.MESH
F32 = jnp.float32
BF16 = jnp.bfloat16


def dot_nn(a, b):
    return lax.dot_general(a, b, (((1,), (0,)), ((), ())), preferred_element_type=F32)


def dot_nt(a, b):
    return lax.dot_general(a, b, (((1,), (1,)), ((), ())), preferred_element_type=F32)


def dot_tn(a, b):
    return lax.dot_general(a, b, (((0,), (0,)), ((), ())), preferred_element_type=F32)


def rotary_tables(seq_len):
    half = ROT // 2
    inverse = 10000.0 ** (-2.0 * np.arange(half) / ROT)
    angles = np.arange(seq_len)[:, None] * inverse[None, :]
    cosines = np.ones((seq_len, HEAD))
    sines = np.zeros((seq_len, HEAD))
    cosines[:, :half] = np.cos(angles)
    cosines[:, half:ROT] = np.cos(angles)
    sines[:, :half] = -np.sin(angles)
    sines[:, half:ROT] = np.sin(angles)
    tables = np.stack([np.tile(item, (1, LANES // HEAD)) for item in (cosines, sines)])
    return tables.astype(np.float32)


def normalise(value):
    center = value - jnp.mean(value, axis=-1, keepdims=True)
    rstd = lax.rsqrt(jnp.mean(center * center, axis=-1, keepdims=True) + EPS)
    return center * rstd, rstd


def train_kernel(
    heads,
    x_in,
    target_in,
    tissue,
    tables,
    wq_in,
    wd_in,
    w1_in,
    w2_in,
    qkv_bias,
    vec_in,
    out_cols,
    grad_cols,
    grads,
    lines,
    small,
    wq,
    wd,
    w1,
    w2,
    vec,
    chain,
    qkv,
    ctx,
    act,
    gate,
    key_grad,
    value_grad,
    part,
    late_part,
    got,
    met,
    late_got,
    late_met,
    total,
    half_got,
    first_got,
    second_got,
    more_got,
    line_got,
    tally,
    tally_got,
    probs,
    load_sem,
    give_sem,
    take_sem,
    hop_send,
    hop_recv,
    swap_send,
    swap_recv,
    sum_send,
    sum_recv,
    line_send,
    line_recv,
    tally_send,
    tally_recv,
    store_sem,
    free_sem,
):
    section = lax.axis_index("section")
    replica = lax.axis_index("dp")
    place = lax.axis_index("tensor")
    copies = lax.axis_size("dp")
    bits = copies.bit_length() - 1
    _, chunks, rows, width = chain.shape
    unit = part.shape[1]
    halves = rows // unit
    units = chunks * halves
    half_width = late_met.shape[-1]
    lanes = wd.shape[1]
    valid = heads * HEAD
    columns = out_cols.shape[1]
    padded = -(-columns // LANES) * LANES
    inner = jnp.logical_and(place > 0, place < 3)
    outer = jnp.logical_not(inner)
    beside = place + 1 - 2 * lax.rem(place, 2)
    across = 3 - place

    def flipped(bit):
        return replica + (1 << bit) * (1 - 2 * lax.rem(replica // (1 << bit), 2))

    twin = {"section": 1 - section}
    mates = [{"dp": flipped(bit)} for bit in range(bits)]
    near = {"tensor": beside}
    far = {"tensor": across}
    friends = [twin, near, far] + mates

    def send(source, goal, sems, target):
        return pltpu.make_async_remote_copy(
            src_ref=source,
            dst_ref=goal,
            send_sem=sems[0],
            recv_sem=sems[1],
            device_id=target,
            device_id_type=MESH,
        )

    barrier = pltpu.get_barrier_semaphore()
    for friend in friends:
        pl.semaphore_signal(barrier, inc=1, device_id=friend, device_id_type=MESH)

    input_load = pltpu.make_async_copy(x_in.at[section], chain.at[0], load_sem.at[0])
    input_load.start()
    pairs = []
    for part_index in range(3):
        for h in range(heads):
            source = slice((3 * h + part_index) * HEAD, (3 * h + part_index + 1) * HEAD)
            goal = slice(part_index * lanes + h * HEAD, part_index * lanes + (h + 1) * HEAD)
            pairs.append((wq_in.at[source], wq.at[section, goal]))
    pairs += [(w1_in, w1.at[section]), (wd_in, wd.at[section, :valid]), (w2_in, w2.at[section])]
    loads = [
        pltpu.make_async_copy(source, goal, load_sem.at[4 + index])
        for index, (source, goal) in enumerate(pairs)
    ]
    for item in loads:
        item.start()
    target_load = pltpu.make_async_copy(target_in.at[section], chain.at[2], load_sem.at[3])
    target_load.start()

    for index, item in enumerate(vec_in):
        vec[section, index : index + 1] = item[...].astype(F32)
    vec[section, 4:5] = vec_in[4][...].astype(F32) + vec_in[5][...].astype(F32)
    line = qkv_bias[...].astype(F32)
    gap = [jnp.zeros((1, lanes - valid), F32)] if lanes > valid else []
    packed = []
    for part_index in range(3):
        for h in range(heads):
            packed.append(line[:, (3 * h + part_index) * HEAD : (3 * h + part_index + 1) * HEAD])
        packed += gap
    vec[section, 5:6] = jnp.concatenate(packed, axis=1)
    vec[section, 7:8] = jnp.zeros((1, width), F32)
    for layer in range(2):
        wd[layer, valid:] = jnp.zeros((lanes - valid, width), BF16)
        for part_index in range(3):
            pad = slice(part_index * lanes + valid, (part_index + 1) * lanes)
            wq[layer, pad] = jnp.zeros((lanes - valid, width), BF16)
    pl.semaphore_wait(barrier, len(friends))
    gifts = [
        send(source, goal, (give_sem.at[index], take_sem.at[index]), twin)
        for index, (source, goal) in enumerate(
            [(vec.at[section], vec.at[section])] + pairs
        )
    ]
    for item in gifts:
        item.start()

    tissue_lane = lax.broadcasted_iota(jnp.int32, (8, LANES), 1)
    marks = [(tissue_lane == tissue[index]).astype(F32) for index in range(tissue.shape[0])]
    tally[...] = functools.reduce(lambda a, b: a + b, marks)

    def tally_step(bit):
        return send(
            tally, tally_got.at[bit], (tally_send.at[bit], tally_recv.at[bit]), mates[bit]
        )

    if bits:
        tally_step(0).start()

    def count_on(bit):
        step = tally_step(bit)
        step.wait()
        tally[...] += tally_got[bit]
        if bit + 1 < bits:
            tally_step(bit + 1).start()

    lane = lax.broadcasted_iota(jnp.int32, (1, lanes), 1) // HEAD
    head_masks = [lane == h for h in range(heads)]
    factor = HEAD ** (-0.5)

    left_half = lax.rem(lax.broadcasted_iota(jnp.int32, (1, lanes), 1), HEAD) < ROT // 2

    def wide(table, start):
        piece = tables[table, start : start + rows, :]
        return jnp.concatenate([piece] * (lanes // LANES), axis=1)

    def turned(value):
        ahead = pltpu.roll(value, lanes - ROT // 2, 1)
        behind = pltpu.roll(value, ROT // 2, 1)
        return jnp.where(left_half, ahead, behind)

    def turn(value, start):
        return value * wide(0, start) + turned(value) * wide(1, start)

    def turn_back(value, start):
        return value * wide(0, start) - turned(value) * wide(1, start)

    def only(mask, value):
        return jnp.where(mask, value, jnp.zeros_like(value))

    def put(goal, slot, value):
        for half in range(halves):
            piece = value[half * unit : (half + 1) * unit]
            goal[slot * halves + half] = piece.astype(BF16)

    def forward_chunk(layer, c):
        start = c * rows
        here = slice(start, start + rows)
        if c == 0:
            need(0, 1 + projection, layer)
        spread, _ = normalise(chain[layer, c].astype(F32))
        first = (spread * vec[layer, 0:1] + vec[layer, 1:2]).astype(BF16)
        second = (spread * vec[layer, 2:3] + vec[layer, 3:4]).astype(BF16)
        projected = dot_nt(first, wq[layer]) + vec[layer, 5:6]
        query = turn(projected[:, :lanes], start).astype(BF16)
        qkv[layer, here, :lanes] = query
        qkv[layer, here, lanes : 2 * lanes] = turn(projected[:, lanes : 2 * lanes], start).astype(
            BF16
        )
        qkv[layer, here, 2 * lanes :] = projected[:, 2 * lanes :].astype(BF16)
        if c == 0:
            need(1 + projection, 2 + projection, layer)
        pre = dot_nn(second, w1[layer]) + vec[layer, 6:7]
        below = 0.5 * (1.0 + lax.erf(pre * (0.5**0.5)))
        active = (pre * below).astype(BF16)
        act[layer, here, :] = active
        slope = below + pre * (jnp.exp(-0.5 * pre * pre) * ((2.0 * np.pi) ** -0.5))
        gate[layer, here, :] = slope.astype(BF16)
        diagonal = lax.broadcasted_iota(jnp.int32, (rows, rows), 0) >= lax.broadcasted_iota(
            jnp.int32, (rows, rows), 1
        )
        context = jnp.zeros((rows, lanes), F32)
        for h in range(heads):
            asked = only(head_masks[h], query) * jnp.asarray(factor, BF16)
            near = dot_nt(asked, qkv[layer, here, lanes : 2 * lanes])
            near = jnp.where(diagonal, near, -1e30)
            highest = jnp.max(near, axis=-1, keepdims=True)
            if c > 0:
                far = dot_nt(asked, qkv[layer, :start, lanes : 2 * lanes])
                highest = jnp.maximum(highest, jnp.max(far, axis=-1, keepdims=True))
                far = jnp.exp(far - highest)
            near = jnp.exp(near - highest)
            total = jnp.sum(near, axis=-1, keepdims=True)
            if c > 0:
                total = total + jnp.sum(far, axis=-1, keepdims=True)
            inverse = 1.0 / total
            near = (near * inverse).astype(BF16)
            probs[c][layer, h, :, start:] = near
            mixed = dot_nn(near, qkv[layer, here, 2 * lanes :])
            if c > 0:
                far = (far * inverse).astype(BF16)
                probs[c][layer, h, :, :start] = far
                mixed = mixed + dot_nn(far, qkv[layer, :start, 2 * lanes :])
            context = jnp.where(head_masks[h], mixed, context)
        context = context.astype(BF16)
        ctx[layer, here, :] = context
        if c == 0:
            need(2 + projection, 4 + projection, layer)
        result = (dot_nn(context, wd[layer]) + dot_nn(active, w2[layer])).astype(BF16)
        for index, goal in enumerate((part, late_part)):
            pl.when(layer == index)(functools.partial(put, goal, c, result))

    def backward_chunk(layer, c):
        start = c * rows
        stop = start + rows
        here = slice(start, stop)
        first_turn = c == chunks - 1
        slot = chunks - 1 - c
        cotangent = chain[3 - layer, c]
        context_grad = dot_nt(cotangent, wd[layer]).astype(BF16)
        pre_grad = (dot_nt(cotangent, w2[layer]) * gate[layer, here, :].astype(F32)).astype(BF16)
        gate[layer, here, :] = pre_grad
        second_back = dot_nt(pre_grad, w1[layer])
        query = qkv[layer, here, :lanes]
        weighed = context_grad.astype(F32) * ctx[layer, here, :].astype(F32)
        query_grad = jnp.zeros((rows, lanes), F32)
        key_sum = None
        value_sum = None
        for h in range(heads):
            mask = head_masks[h]
            own_grad = only(mask, context_grad)
            asked = only(mask, query) * jnp.asarray(factor, BF16)
            row_dot = jnp.sum(only(mask, weighed), axis=-1, keepdims=True)
            prob = probs[c][layer, h]
            prob_grad = dot_nt(own_grad, qkv[layer, :stop, 2 * lanes :])
            score_grad = (prob.astype(F32) * (prob_grad - row_dot)).astype(BF16)
            query_grad = jnp.where(
                mask, dot_nn(score_grad, qkv[layer, :stop, lanes : 2 * lanes]), query_grad
            )
            key_part = dot_tn(score_grad, asked)
            value_part = dot_tn(prob, own_grad)
            key_sum = key_part if key_sum is None else key_sum + key_part
            value_sum = value_part if value_sum is None else value_sum + value_part
        if first_turn:
            key_grad[:stop] = key_sum
            value_grad[:stop] = value_sum
        else:
            key_grad[:stop] += key_sum
            value_grad[:stop] += value_sum
        qkv[layer, here, :lanes] = turn_back(query_grad * factor, start).astype(BF16)
        qkv[layer, here, lanes : 2 * lanes] = turn_back(key_grad[here], start).astype(BF16)
        qkv[layer, here, 2 * lanes :] = value_grad[here].astype(BF16)
        projected_grad = qkv[layer, here, :]
        first_back = dot_nn(projected_grad, wq[layer])
        spread, rstd = normalise(chain[layer, c].astype(F32))
        first = (spread * vec[layer, 0:1] + vec[layer, 1:2]).astype(BF16)
        second = (spread * vec[layer, 2:3] + vec[layer, 3:4]).astype(BF16)
        sums = (
            first_back * spread,
            first_back,
            second_back * spread,
            second_back,
            projected_grad.astype(F32),
            cotangent.astype(F32),
            pre_grad.astype(F32),
        )
        for index, item in enumerate(sums):
            line = jnp.sum(item, axis=0, keepdims=True)
            if first_turn:
                small[layer, index : index + 1] = line
            else:
                small[layer, index : index + 1] += line
        if first_turn:
            small[layer, len(sums) :] = jnp.zeros((8 - len(sums), width), F32)
        back = first_back * vec[layer, 0:1] + second_back * vec[layer, 2:3]
        middle = jnp.mean(back, axis=-1, keepdims=True)
        tilt = jnp.mean(back * spread, axis=-1, keepdims=True)
        put(part, slot, rstd * (back - middle - spread * tilt))
        return here, first_turn, first, second, pre_grad, cotangent

    def add_weight_grads(layer, here, first_turn, first, second, pre_grad, cotangent):
        step = lanes

        def add(start, piece):
            goal = slice(start, start + piece.shape[0])
            if not first_turn:
                piece = piece + total[layer, goal].astype(F32)
            total[layer, goal] = piece.astype(BF16)

        for part_index in range(3):
            at = part_index * lanes
            piece = dot_tn(qkv[layer, here, at : at + lanes], first)
            for h in range(heads):
                add((3 * h + part_index) * HEAD, piece[h * HEAD : (h + 1) * HEAD])
        base = 3 * valid
        for at in range(0, width, step):
            add(base + at, dot_tn(second[:, at : at + step], pre_grad))
        base += width
        for at in range(0, act.shape[-1], step):
            add(base + at, dot_tn(act[layer, here, at : at + step], cotangent))
        base += act.shape[-1]
        add(base, dot_tn(ctx[layer, here], cotangent)[:valid])

    all_rows = total.shape[1]
    share_rows = all_rows // 2
    folds = min(bits, 2)

    def spans(group):
        order = (0, 1)[:folds] if group == 0 else (1, 0)[-folds:] if folds else ()
        size = share_rows // 2
        start = section * share_rows + group * size
        steps = []
        for bit in order:
            size = size // 2
            upper = lax.rem(replica // (1 << bit), 2)
            steps.append((bit, start + upper * size, start + (1 - upper) * size, size))
            start = start + upper * size
        return steps, start, size

    groups = [spans(0), spans(1)]
    sum_steps = 2 + 2 * folds + (bits - folds)

    group_rows = share_rows // 2

    def sums_of(layer, start, size):
        return total.at[layer, pl.ds(pl.multiple_of(start, 16), size)]

    def gathered(layer, group, start, size):
        start = start - section * share_rows - group * group_rows
        return (act, gate)[group].at[layer, pl.ds(pl.multiple_of(start, 16), size)]

    def sum_sems(layer, step, group):
        return sum_send.at[layer, step, group], sum_recv.at[layer, step, group]

    def sum_copies(layer, step):
        if step == 0:
            source = sums_of(layer, (1 - section) * share_rows, share_rows)
            return [send(source, half_got.at[layer], sum_sems(layer, 0, 0), twin)]
        copies_now = []
        for group, (steps, start, size) in enumerate(groups):
            sems = sum_sems(layer, step, group)
            if step <= folds:
                bit, _, gone, size = steps[step - 1]
                goal = (first_got, second_got)[step - 1].at[group]
                copies_now.append(send(sums_of(layer, gone, size), goal, sems, mates[bit]))
            elif step <= bits:
                goal = more_got.at[layer, step - 1 - folds, group]
                source = gathered(layer, group, start, size)
                copies_now.append(send(source, goal, sems, mates[step - 1]))
            else:
                bit, start, _, size = steps[bits - step]
                piece = gathered(layer, group, start, size)
                copies_now.append(send(piece, piece, sems, mates[bit]))
        return copies_now

    def last_copies(layer):
        pieces = []
        for group in range(2):
            first_row = section * share_rows + group * group_rows
            piece = gathered(layer, group, first_row, group_rows)
            goal = grads.at[pl.ds(pl.multiple_of(first_row, 16), group_rows)]
            sems = sum_sems(layer, sum_steps - 1, group)
            other_row = (1 - section) * share_rows + group * group_rows
            other = grads.at[pl.ds(pl.multiple_of(other_row, 16), group_rows)]
            pieces.append(
                (
                    send(piece, goal, sems, twin),
                    send(piece, other, sems, twin),
                    pltpu.make_async_copy(piece, goal, store_sem.at[group]),
                )
            )
        return pieces

    def sum_start(layer, step):
        if step < sum_steps - 1:
            if isinstance(layer, int) and layer == 0 and 1 <= step <= folds:
                for group in range(2):
                    pl.semaphore_wait(free_sem.at[step - 1, group], 1)
            for item in sum_copies(layer, step):
                item.start()
            return
        for give, _, keep in last_copies(layer):
            pl.when(section != layer)(give.start)
            pl.when(section == layer)(keep.start)

    def add_rows(goal, base, source):
        size = source.shape[0]
        piece = math.gcd(size, 144)

        def add_piece(index, carry):
            here = pl.ds(pl.multiple_of(index * piece, 16), piece)
            goal[here] = (base[here].astype(F32) + source[here].astype(F32)).astype(BF16)
            return carry

        lax.fori_loop(0, size // piece, add_piece, 0)

    def sum_end(layer, step):
        if step == sum_steps - 1:
            for give, take, keep in last_copies(layer):
                pl.when(section != layer)(give.wait_send)
                pl.when(section == layer)(take.wait_recv)
                pl.when(section == layer)(keep.wait)
            return
        for item in sum_copies(layer, step):
            item.wait()
        if step == 0:
            base = sums_of(layer, section * share_rows, share_rows)
            add_rows(base, base, half_got.at[layer])
            return
        if step > bits:
            return
        for group, (steps, start, size) in enumerate(groups):
            goal = gathered(layer, group, start, size)
            if step < folds:
                base = sums_of(layer, steps[step - 1][1], steps[step - 1][3])
                add_rows(base, base, first_got.at[group])
            elif step == folds:
                add_rows(goal, sums_of(layer, start, size), second_got.at[group])
            else:
                add_rows(goal, goal, more_got.at[layer, step - 1 - folds, group])
            if layer == 1 and step <= folds:
                mate = mates[steps[step - 1][0]]
                pl.semaphore_signal(
                    free_sem.at[step - 1, group], inc=1, device_id=mate, device_id_type=MESH
                )

    line_friends = [twin] + mates + [near, far]

    def line_copy(step):
        sems = (line_send.at[step], line_recv.at[step])
        return send(small, line_got.at[step], sems, line_friends[step])

    def line_end(step):
        line_copy(step).wait()
        if step <= bits:
            small[...] += line_got[step]
        else:
            small[:, 0:4] += line_got[step, :, 0:4]

    low_side = place < 2
    own_half = pl.multiple_of(jnp.where(low_side, 0, half_width), LANES)
    other_half = pl.multiple_of(jnp.where(low_side, half_width, 0), LANES)
    window = place * columns // LANES * LANES
    window = pl.multiple_of(window, LANES)
    end_window = pl.multiple_of(jnp.where(low_side, 0, width - padded), LANES)

    sent_width = width - LANES
    sent_lanes = pl.ds(pl.multiple_of(jnp.where(low_side, LANES, 0), LANES), sent_width)

    def spot(kind, u):
        chunk = u // halves if kind < 2 else chunks - 1 - u // halves
        return chunk, slice(u % halves * unit, (u % halves + 1) * unit)

    def buffers(kind, u):
        if kind == 1:
            return late_part.at[u], late_got.at[u], late_met.at[u]
        return part.at[u], got.at[u], met.at[u] if kind != 3 else met.at[u, :, :half_width]

    def hop_sems(kind, stage, u):
        return hop_send.at[int(kind == 1), stage, u], hop_recv.at[int(kind == 1), stage, u]

    def first_hop(kind, u):
        own, landing, _ = buffers(kind, u)
        if kind in (1, 3):
            own, landing = own.at[:, sent_lanes], landing.at[:, :sent_width]
        return send(own, landing, hop_sems(kind, 0, u), near)

    def second_hop(kind, u):
        own, _, landing = buffers(kind, u)
        if kind in (1, 3):
            own = own.at[:, pl.ds(other_half, half_width)]
        return send(own, landing, hop_sems(kind, 1, u), far)

    def third_hop(kind, u):
        own, _, landing = buffers(kind, u)
        if kind in (1, 3):
            own, landing = own.at[:, pl.ds(end_window, padded)], landing.at[:, :padded]
        else:
            chunk, here = spot(kind, u)
            own = landing = chain.at[kind + 1, chunk, here]
        return send(own, landing, hop_sems(kind, 2, u), near)

    def by_rows(count, work, step=32):
        def turn_rows(index, carry):
            work(pl.ds(pl.multiple_of(index * step, step), step))
            return carry

        lax.fori_loop(0, count // step, turn_rows, 0)

    def launch(kind, c):
        @pl.when(outer)
        def _():
            for half in range(halves):
                first_hop(kind, c * halves + half).start()

    def meet(kind, u):
        @pl.when(inner)
        def _():
            first_hop(kind, u).wait_recv()
            own, landed, _ = buffers(kind, u)
            if kind in (1, 3):
                own, landed = own.at[:, sent_lanes], landed.at[:, :sent_width]

            def add(here):
                own[here] = (own[here].astype(F32) + landed[here].astype(F32)).astype(BF16)

            by_rows(unit, add)
            second_hop(kind, u).start()

    def settle(kind, u):
        chunk, here = spot(kind, u)

        @pl.when(inner)
        def _():
            second_hop(kind, u).wait_recv()
            own, _, landed = buffers(kind, u)
            if kind in (1, 3):
                lanes_here = pl.ds(own_half, half_width)
                goal = own.at[:, lanes_here]
                source = goal
                base = chain.at[kind, chunk, here, lanes_here]
            else:
                lanes_here = slice(None)
                goal = chain.at[kind + 1, chunk, here]
                source = own
                base = chain.at[kind, chunk, here]

            def add(at):
                value = source[at].astype(F32) + landed[at].astype(F32) + base[at].astype(F32)
                if kind < 2:
                    value = value + vec[kind, 4:5, lanes_here]
                goal[at] = value.astype(BF16)

            by_rows(unit, add)
            if kind > 1:
                third_hop((0, 2)[kind - 2], u).wait_send()
            third_hop(kind, u).start()

    def arrive(kind, c):
        @pl.when(outer)
        def _():
            for half in range(halves):
                third_hop(kind, c * halves + half).wait_recv()

    def release(kind, c):
        for half in range(halves):
            u = c * halves + half
            pl.when(outer)(first_hop(kind, u).wait_send)
            pl.when(inner)(second_hop(kind, u).wait_send)

    def let_go(kind):
        for u in range(units):
            pl.when(inner)(third_hop(kind, u).wait_send)

    def serve(kind, meets, settles):
        for index in range(max(len(meets), len(settles))):
            if index < len(meets):
                meet(kind, meets[index])
            if index < len(settles):
                settle(kind, settles[index])

    projection = 3 * heads

    def need(first, last, layer):
        @pl.when(section == layer)
        def _():
            for index in range(max(first, 1), last):
                loads[index - 1].wait()

        @pl.when(section != layer)
        def _():
            for index in range(first, last):
                gifts[index].wait_recv()

    input_load.wait()

    forward_turns = (
        (((), ()), ((), ()), ((0,), ()), ((1, 2, 3), (0, 1, 2))),
        (((4,), (3,)), ((5, 6), (4, 5)), ((7,), (6, 7)), ((), ())),
    )

    def forward_layer(layer, carry):
        for c in range(chunks):
            pl.when(layer == 1)(functools.partial(arrive, 0, c))
            forward_chunk(layer, c)
            pl.when(layer == 0)(functools.partial(launch, 0, c))
            for index in range(2):
                pl.when(layer == index)(functools.partial(serve, 0, *forward_turns[index][c]))

            if c == 2:

                @pl.when(layer == 1)
                def _():
                    launch(1, 0)
                    launch(1, 1)

            for bit in range(bits):
                if bit % chunks == c:
                    pl.when(layer == bit // chunks)(functools.partial(count_on, bit))
        return carry

    lax.fori_loop(0, 2, forward_layer, 0)
    target_load.wait()
    own_mark = jnp.where(section == 0, marks[0], marks[1])[0:1]
    own_count = jnp.sum(own_mark * tally[0:1], axis=-1, keepdims=True)
    share = (tissue.shape[0] * copies / TISSUES) / own_count
    gifts[0].wait_send()
    vec[0, 7:8] = jnp.broadcast_to(share, (1, width))

    def weigh(c, carry):
        chain[2, c] = (vec[0, 7:8] * chain[2, c].astype(F32)).astype(BF16)
        return carry

    lax.fori_loop(0, chunks, weigh, 0)

    backward_turns = (
        (
            ((1, (0, 1), ()),),
            ((1, (2, 3), (0, 1)),),
            ((1, (), (2, 3)), (2, (0,), ())),
            ((2, (1, 2), (0, 1)),),
        ),
        (
            ((2, (3, 4), (2, 3)),),
            ((2, (5, 6), (4, 5)),),
            ((2, (7,), (6, 7)),),
            ((3, (0, 1), (0,)),),
        ),
    )

    def serve_all(turns):
        for item in turns:
            serve(*item)

    early_sums = ((0, None), (None, 1), (None, 2), (3, None))

    def move_sum(step):
        if step is not None:
            sum_end(1, step)
            sum_start(1, step + 1)

    def backward_layer(turn_index, carry):
        layer = 1 - turn_index
        for at in range(chunks):
            now = early_sums[at]

            @pl.when(layer == 0)
            def _():
                arrive(2, at)
                release(2, at)
                move_sum(now[0])

            pl.when(layer == 1)(functools.partial(release, 0, at))
            kept = backward_chunk(layer, chunks - 1 - at)
            for index in range(2):
                pl.when(turn_index == index)(functools.partial(launch, 2 + index, at))
            add_weight_grads(layer, *kept)
            if at == chunks - 1:
                sum_start(layer, 0)

                @pl.when(layer == 0)
                def _():
                    launch(1, 2)
                    launch(1, 3)

            @pl.when(layer == 0)
            def _():
                if at == 1:
                    move_sum(now[1])

            for index in range(2):
                pl.when(turn_index == index)(
                    functools.partial(serve_all, backward_turns[index][at])
                )

            @pl.when(layer == 0)
            def _():
                if at == 2:
                    move_sum(now[1])

        return carry

    lax.fori_loop(0, 2, backward_layer, 0)

    shift = lax.rem(place * columns, LANES)

    def staged(index, layer):
        return probs[-1].at[layer, index, :columns]

    def stage(index, layer, row, value):
        turned_value = value.astype(F32).T
        low = turned_value[:columns]
        high = turned_value[LANES // 2 : LANES // 2 + columns]
        goal = pl.ds(pl.multiple_of(row, unit), unit)
        staged(index, layer)[:, goal] = jnp.where(shift == 0, low, high).astype(BF16)

    def stage_whole(index, layer, kind):
        def stage_unit(u, carry):
            rows_here = pl.ds(pl.multiple_of(lax.rem(u, halves) * unit, unit), unit)
            source = chain.at[kind + 1, u // halves, rows_here, pl.ds(window, padded)]
            stage(index, layer, u * unit, source[...])
            return carry

        lax.fori_loop(0, units, stage_unit, 0)

    def stage_own(index, layer, kind):
        for c in range(chunks):
            arrive(kind, c)
            release(kind, c)
        let_go(kind)
        tile = lax.broadcasted_iota(jnp.int32, (1, padded), 1) // LANES
        unsent = tile == jnp.where(low_side, 0, padded // LANES - 1)
        store, landing = (late_part, late_met) if kind == 1 else (part, met)

        def stage_unit(u, carry):
            chunk = u // halves if kind == 1 else chunks - 1 - u // halves
            row = chunk * rows + lax.rem(u, halves) * unit

            @pl.when(outer)
            def _():
                mine = store[u, :, pl.ds(end_window, padded)]
                value = landing[u, :, :padded].astype(F32) + only(unsent, mine.astype(F32))
                stage(index, layer, row, value)

            @pl.when(inner)
            def _():
                stage(index, layer, row, store[u, :, pl.ds(window, padded)])

            return carry

        lax.fori_loop(0, units, stage_unit, 0)

    def swap_columns(index, goal):
        sems = (swap_send.at[index], swap_recv.at[index])
        return [
            send(staged(index, 1 - section), goal.at[section], sems, twin),
            pltpu.make_async_copy(staged(index, section), goal.at[section], load_sem.at[1 + index]),
        ]

    def sum_next(step):
        if step < sum_steps:
            sum_end(0, step)
            if step + 1 < sum_steps:
                sum_start(0, step + 1)

    def line_next(step):
        if step < len(line_friends):
            line_end(step)
            if step + 1 < len(line_friends):
                line_copy(step + 1).start()

    line_copy(0).start()
    sum_next(0)
    line_next(0)
    serve(3, (2, 3), (1, 2))
    stage_whole(0, 0, 0)
    stage_whole(1, 1, 2)
    serve(3, (4, 5), (3, 4))
    for step in range(chunks, sum_steps - 1):
        sum_end(1, step)
        sum_start(1, step + 1)
    sum_next(1)
    line_next(1)
    serve(3, (6, 7), (5, 6))
    sum_next(2)
    line_next(2)
    settle(3, 7)
    sum_end(1, sum_steps - 1)
    meet(1, 4)
    sum_next(3)
    line_next(3)
    stage_own(1, 0, 3)
    moves = swap_columns(1, grad_cols)
    for item in moves:
        item.start()
    serve(1, (5, 6, 7), (4, 5, 6))
    sum_next(4)
    line_next(4)
    settle(1, 7)
    stage_own(0, 1, 1)
    late_moves = swap_columns(0, out_cols)
    for item in late_moves:
        item.start()
    for step in range(5, max(sum_steps, len(line_friends))):
        sum_next(step)
        line_next(step)
    lines[...] = small[section]
    for item in moves + late_moves:
        item.wait()
    for item in gifts[1:]:
        item.wait_send()


def train(x, target, tissue, weights, qkv_bias, vec):
    wq, wd, w1, w2 = weights
    count, seq_len, width = x.shape
    rows = min(ROWS, seq_len)
    chunks = seq_len // rows
    unit = min(UNIT, rows)
    pieces = seq_len // unit
    valid = wd.shape[0]
    heads = valid // HEAD
    lanes = -(-valid // LANES) * LANES
    units = w1.shape[1]
    columns = width // lax.axis_size("tensor")
    bits = lax.axis_size("dp").bit_length() - 1
    tables = jnp.asarray(rotary_tables(seq_len))
    total_rows = 3 * valid + width + units + valid
    hbm = pl.BlockSpec(memory_space=pl.ANY)
    vmem = pl.BlockSpec(memory_space=pltpu.VMEM)
    smem = pl.BlockSpec(memory_space=pltpu.SMEM)
    scratch = [
        pltpu.VMEM((2, 8, width), F32),
        pltpu.VMEM((2, 3 * lanes, width), BF16),
        pltpu.VMEM((2, lanes, width), BF16),
        pltpu.VMEM((2,) + w1.shape, BF16),
        pltpu.VMEM((2,) + w2.shape, BF16),
        pltpu.VMEM((2, 8, width), F32),
        pltpu.VMEM((4, chunks, rows, width), BF16),
        pltpu.VMEM((2, seq_len, 3 * lanes), BF16),
        pltpu.VMEM((2, seq_len, lanes), BF16),
        pltpu.VMEM((2, seq_len, units), BF16),
        pltpu.VMEM((2, seq_len, units), BF16),
        pltpu.VMEM((seq_len, lanes), F32),
        pltpu.VMEM((seq_len, lanes), F32),
        pltpu.VMEM((pieces, unit, width), BF16),
        pltpu.VMEM((pieces, unit, width), BF16),
        pltpu.VMEM((pieces, unit, width), BF16),
        pltpu.VMEM((pieces, unit, width), BF16),
        pltpu.VMEM((pieces, unit, width - LANES), BF16),
        pltpu.VMEM((pieces, unit, width // 2), BF16),
        pltpu.VMEM((2, total_rows, width), BF16),
        pltpu.VMEM((2, total_rows // 2, width), BF16),
        pltpu.VMEM((2, total_rows // 8, width), BF16),
        pltpu.VMEM((2, total_rows // 16, width), BF16),
        pltpu.VMEM((2, max(bits - 2, 1), 2, total_rows // 16 if bits > 2 else 16, width), BF16),
        pltpu.VMEM((3 + bits, 2, 8, width), F32),
        pltpu.VMEM((8, LANES), F32),
        pltpu.VMEM((max(bits, 1), 8, LANES), F32),
    ]
    probs = [pltpu.VMEM((2, heads, rows, (c + 1) * rows), BF16) for c in range(chunks)]
    semaphores = [
        pltpu.SemaphoreType.DMA((4 + 3 * heads + 3,)),
        pltpu.SemaphoreType.DMA((4 + 3 * heads,)),
        pltpu.SemaphoreType.DMA((4 + 3 * heads,)),
        pltpu.SemaphoreType.DMA((2, 3, pieces)),
        pltpu.SemaphoreType.DMA((2, 3, pieces)),
        pltpu.SemaphoreType.DMA((2,)),
        pltpu.SemaphoreType.DMA((2,)),
        pltpu.SemaphoreType.DMA((2, bits + 4, 2)),
        pltpu.SemaphoreType.DMA((2, bits + 4, 2)),
        pltpu.SemaphoreType.DMA((3 + bits,)),
        pltpu.SemaphoreType.DMA((3 + bits,)),
        pltpu.SemaphoreType.DMA((max(bits, 1),)),
        pltpu.SemaphoreType.DMA((max(bits, 1),)),
        pltpu.SemaphoreType.DMA((2,)),
        pltpu.SemaphoreType.REGULAR((2, 2)),
    ]

    def body(*refs):
        ends = np.cumsum([9, len(vec), 4 + len(scratch), chunks])
        head, lines, main, kept = (
            refs[start:stop] for start, stop in zip([0, *ends[:-1]], ends, strict=True)
        )
        train_kernel(heads, *head, lines, *main, kept, *refs[ends[-1] :])

    return pl.pallas_call(
        body,
        out_shape=(
            jax.ShapeDtypeStruct((count, columns, seq_len), BF16),
            jax.ShapeDtypeStruct((count, columns, seq_len), BF16),
            jax.ShapeDtypeStruct((total_rows, width), BF16),
            jax.ShapeDtypeStruct((8, width), F32),
        ),
        in_specs=[hbm, hbm, smem, vmem, hbm, hbm, hbm, hbm, vmem] + [vmem] * len(vec),
        out_specs=(hbm, hbm, hbm, vmem),
        scratch_shapes=scratch + probs + semaphores,
        compiler_params=pltpu.CompilerParams(
            collective_id=0, has_side_effects=True, vmem_limit_bytes=63 * 2**20
        ),
    )(
        x.reshape(count, chunks, rows, width),
        target.reshape(count, chunks, rows, width),
        tissue,
        tables,
        wq,
        wd,
        w1,
        w2,
        qkv_bias,
        *vec,
    )


def widen_kernel(heads, cols, grad_cols, *refs):
    sources, lines = refs[:4], refs[4]
    out_cols, out_grad_cols, *goals = refs[5:]
    out_cols[...] = cols[...]
    out_grad_cols[...] = grad_cols[...].astype(F32)
    for source, goal in zip(sources, goals[:4], strict=True):
        goal[...] = source[...].astype(F32)
    for index, goal in zip((0, 1, 2, 3, 5, 6), goals[4:10], strict=True):
        goal[...] = lines[index : index + 1]
    line = lines[4:5]
    lanes = line.shape[1] // 3
    pieces = []
    for h in range(heads):
        for part_index in range(3):
            start = part_index * lanes + h * HEAD
            pieces.append(line[:, start : start + HEAD])
    goals[10][...] = jnp.concatenate(pieces, axis=1)


def widen(out_cols, grad_cols, total, lines, heads, units):
    steps = 4
    count, columns, seq_len = out_cols.shape
    width = total.shape[1]
    sizes = (3 * heads * HEAD, width, units, heads * HEAD)
    starts = [0, *np.cumsum(sizes[:-1]).tolist()]
    col_spec = pl.BlockSpec((count, columns // steps, seq_len), lambda i: (0, i, 0))

    def rows_from(start, size):
        block = size // steps
        return pl.BlockSpec((block, width), lambda i: (start // block + i, 0))

    def line_spec(lanes):
        return pl.BlockSpec((1, lanes), lambda i: (0, 0))

    line = jax.ShapeDtypeStruct((1, width), F32)
    return pl.pallas_call(
        functools.partial(widen_kernel, heads),
        grid=(steps,),
        in_specs=[col_spec, col_spec]
        + [rows_from(start, size) for start, size in zip(starts, sizes, strict=True)]
        + [pl.BlockSpec(lines.shape, lambda i: (0, 0))],
        out_specs=[col_spec, col_spec]
        + [rows_from(0, size) for size in sizes]
        + [line_spec(width)] * 6
        + [line_spec(sizes[0])],
        out_shape=[
            jax.ShapeDtypeStruct(out_cols.shape, BF16),
            jax.ShapeDtypeStruct(out_cols.shape, F32),
        ]
        + [jax.ShapeDtypeStruct((size, width), F32) for size in sizes]
        + [line] * 6
        + [jax.ShapeDtypeStruct((1, sizes[0]), F32)],
    )(out_cols, grad_cols, total, total, total, total, lines)


def per_device(
    hidden_in,
    target,
    tissue,
    ln1_gain,
    ln1_bias,
    ln2_gain,
    ln2_bias,
    qkv_weight,
    qkv_bias,
    dense_weight,
    dense_bias,
    fc1_weight,
    fc1_bias,
    fc2_weight,
    fc2_bias,
):
    heads = dense_weight.shape[1] // HEAD
    units = fc1_weight.shape[-1]
    weights = (qkv_weight[0].T, dense_weight[0], fc1_weight[0], fc2_weight[0])
    vec = (ln1_gain, ln1_bias, ln2_gain, ln2_bias, dense_bias, fc2_bias, fc1_bias)
    out_cols, grad_cols, total, lines = train(hidden_in, target, tissue, weights, qkv_bias, vec)
    out_cols, grad_cols, qkv_grad, fc1_grad, fc2_grad, dense_grad, *lines = widen(
        out_cols, grad_cols, total, lines, heads, units
    )
    gain1, bias1, gain2, bias2, out_bias, fc1_bias_grad, qkv_bias_grad = lines
    return (
        out_cols.transpose(0, 2, 1)[None],
        grad_cols.transpose(0, 2, 1)[None],
        gain1,
        bias1,
        gain2,
        bias2,
        qkv_grad.T[None],
        qkv_bias_grad,
        dense_grad[None],
        out_bias,
        fc1_grad[None],
        fc1_bias_grad,
        fc2_grad[None],
        out_bias,
    )


def solution(mesh):
    return jax.shard_map(
        per_device,
        mesh=mesh,
        in_specs=(
            P("dp", None, None),
            P("dp", None, None),
            P("dp"),
            P("section", None),
            P("section", None),
            P("section", None),
            P("section", None),
            P("section", None, "tensor"),
            P("section", "tensor"),
            P("section", "tensor", None),
            P("section", None),
            P("section", None, "tensor"),
            P("section", "tensor"),
            P("section", "tensor", None),
            P("section", None),
        ),
        out_specs=(
            P("section", "dp", None, "tensor"),
            P("section", "dp", None, "tensor"),
            P("section", None),
            P("section", None),
            P("section", None),
            P("section", None),
            P("section", None, "tensor"),
            P("section", "tensor"),
            P("section", "tensor", None),
            P("section", None),
            P("section", None, "tensor"),
            P("section", "tensor"),
            P("section", "tensor", None),
            P("section", None),
        ),
        check_vma=False,
    )
```

```python
import functools
import math

import jax
import jax.numpy as jnp
import numpy as np
from jax import lax
from jax.experimental import pallas as pl
from jax.experimental.pallas import tpu as pltpu
from jax.sharding import PartitionSpec as P

HEAD = 64
ROT = 16
TISSUES = 16
ROWS = 256
UNIT = 128
LANES = 128
EPS = 1e-05
MESH = pl.DeviceIdType.MESH
F32 = jnp.float32
BF16 = jnp.bfloat16


def dot_nn(a, b):
    return lax.dot_general(a, b, (((1,), (0,)), ((), ())), preferred_element_type=F32)


def dot_nt(a, b):
    return lax.dot_general(a, b, (((1,), (1,)), ((), ())), preferred_element_type=F32)


def dot_tn(a, b):
    return lax.dot_general(a, b, (((0,), (0,)), ((), ())), preferred_element_type=F32)


def rotary_tables(seq_len):
    half = ROT // 2
    inverse = 10000.0 ** (-2.0 * np.arange(half) / ROT)
    angles = np.arange(seq_len)[:, None] * inverse[None, :]
    cosines = np.ones((seq_len, HEAD))
    sines = np.zeros((seq_len, HEAD))
    cosines[:, :half] = np.cos(angles)
    cosines[:, half:ROT] = np.cos(angles)
    sines[:, :half] = -np.sin(angles)
    sines[:, half:ROT] = np.sin(angles)
    tables = np.stack([np.tile(item, (1, LANES // HEAD)) for item in (cosines, sines)])
    return tables.astype(np.float32)


def normalise(value):
    center = value - jnp.mean(value, axis=-1, keepdims=True)
    rstd = lax.rsqrt(jnp.mean(center * center, axis=-1, keepdims=True) + EPS)
    return center * rstd, rstd


def train_kernel(
    heads,
    x_in,
    target_in,
    tissue,
    tables,
    wq_in,
    wd_in,
    w1_in,
    w2_in,
    qkv_bias,
    vec_in,
    out_cols,
    grad_cols,
    grads,
    lines,
    small,
    wq,
    wd,
    w1,
    w2,
    vec,
    chain,
    qkv,
    ctx,
    act,
    gate,
    key_grad,
    value_grad,
    part,
    late_part,
    got,
    met,
    late_got,
    late_met,
    norm_rows,
    context_grad,
    query_back,
    total,
    half_got,
    first_got,
    second_got,
    more_got,
    line_got,
    tally,
    tally_got,
    probs,
    load_sem,
    give_sem,
    take_sem,
    hop_send,
    hop_recv,
    swap_send,
    swap_recv,
    sum_send,
    sum_recv,
    line_send,
    line_recv,
    tally_send,
    tally_recv,
    store_sem,
    free_sem,
):
    section = lax.axis_index("section")
    replica = lax.axis_index("dp")
    place = lax.axis_index("tensor")
    copies = lax.axis_size("dp")
    bits = copies.bit_length() - 1
    _, chunks, rows, width = chain.shape
    unit = part.shape[1]
    halves = rows // unit
    units = chunks * halves
    half_width = late_met.shape[-1]
    lanes = wd.shape[1]
    valid = heads * HEAD
    columns = out_cols.shape[1]
    padded = -(-columns // LANES) * LANES
    inner = jnp.logical_and(place > 0, place < 3)
    outer = jnp.logical_not(inner)
    beside = place + 1 - 2 * lax.rem(place, 2)
    across = 3 - place

    def flipped(bit):
        return replica + (1 << bit) * (1 - 2 * lax.rem(replica // (1 << bit), 2))

    twin = {"section": 1 - section}
    mates = [{"dp": flipped(bit)} for bit in range(bits)]
    near = {"tensor": beside}
    far = {"tensor": across}
    friends = [twin, near, far] + mates

    def send(source, goal, sems, target):
        return pltpu.make_async_remote_copy(
            src_ref=source,
            dst_ref=goal,
            send_sem=sems[0],
            recv_sem=sems[1],
            device_id=target,
            device_id_type=MESH,
        )

    barrier = pltpu.get_barrier_semaphore()
    for friend in friends:
        pl.semaphore_signal(barrier, inc=1, device_id=friend, device_id_type=MESH)

    input_load = pltpu.make_async_copy(x_in.at[section], chain.at[0], load_sem.at[0])
    input_load.start()
    pairs = []
    for part_index in range(3):
        for h in range(heads):
            source = slice((3 * h + part_index) * HEAD, (3 * h + part_index + 1) * HEAD)
            goal = slice(part_index * lanes + h * HEAD, part_index * lanes + (h + 1) * HEAD)
            pairs.append((wq_in.at[source], wq.at[section, goal]))
    pairs += [(w1_in, w1.at[section]), (wd_in, wd.at[section, :valid]), (w2_in, w2.at[section])]
    loads = [
        pltpu.make_async_copy(source, goal, load_sem.at[4 + index])
        for index, (source, goal) in enumerate(pairs)
    ]
    for item in loads:
        item.start()
    target_load = pltpu.make_async_copy(target_in.at[section], chain.at[2], load_sem.at[3])
    target_load.start()

    for index, item in enumerate(vec_in):
        vec[section, index : index + 1] = item[...].astype(F32)
    vec[section, 4:5] = vec_in[4][...].astype(F32) + vec_in[5][...].astype(F32)
    line = qkv_bias[...].astype(F32)
    gap = [jnp.zeros((1, lanes - valid), F32)] if lanes > valid else []
    packed = []
    for part_index in range(3):
        for h in range(heads):
            packed.append(line[:, (3 * h + part_index) * HEAD : (3 * h + part_index + 1) * HEAD])
        packed += gap
    vec[section, 5:6] = jnp.concatenate(packed, axis=1)
    vec[section, 7:8] = jnp.zeros((1, width), F32)
    for layer in range(2):
        wd[layer, valid:] = jnp.zeros((lanes - valid, width), BF16)
        for part_index in range(3):
            pad = slice(part_index * lanes + valid, (part_index + 1) * lanes)
            wq[layer, pad] = jnp.zeros((lanes - valid, width), BF16)
    pl.semaphore_wait(barrier, len(friends))
    gifts = [
        send(source, goal, (give_sem.at[index], take_sem.at[index]), twin)
        for index, (source, goal) in enumerate(
            [(vec.at[section], vec.at[section])] + pairs
        )
    ]
    projection = 3 * heads
    for item in gifts[: 1 + projection]:
        item.start()

    small[...] = jnp.zeros_like(small)
    tissue_lane = lax.broadcasted_iota(jnp.int32, (8, LANES), 1)
    marks = [(tissue_lane == tissue[index]).astype(F32) for index in range(tissue.shape[0])]
    tally[...] = functools.reduce(lambda a, b: a + b, marks)

    def tally_step(bit):
        return send(
            tally, tally_got.at[bit], (tally_send.at[bit], tally_recv.at[bit]), mates[bit]
        )

    if bits:
        tally_step(0).start()

    def count_on(bit):
        step = tally_step(bit)
        step.wait()
        tally[...] += tally_got[bit]
        if bit + 1 < bits:
            tally_step(bit + 1).start()

    lane = lax.broadcasted_iota(jnp.int32, (1, lanes), 1) // HEAD
    head_masks = [lane == h for h in range(heads)]
    factor = HEAD ** (-0.5)

    left_half = lax.rem(lax.broadcasted_iota(jnp.int32, (1, lanes), 1), HEAD) < ROT // 2

    def wide(table, start):
        piece = tables[table, pl.ds(start, rows), :]
        return jnp.concatenate([piece] * (lanes // LANES), axis=1)

    def turned(value):
        ahead = pltpu.roll(value, lanes - ROT // 2, 1)
        behind = pltpu.roll(value, ROT // 2, 1)
        return jnp.where(left_half, ahead, behind)

    def turn(value, start):
        return value * wide(0, start) + turned(value) * wide(1, start)

    def turn_back(value, start):
        return value * wide(0, start) - turned(value) * wide(1, start)

    def only(mask, value):
        return jnp.where(mask, value, jnp.zeros_like(value))

    def put(goal, slot, value):
        for half in range(halves):
            piece = value[half * unit : (half + 1) * unit]
            goal[slot * halves + half] = piece.astype(BF16)

    def forward_chunk(layer, c):
        start = c * rows
        here = slice(start, start + rows)
        if c == 0:
            need(0, 1 + projection, layer)
            pl.when(layer == 0)(gifts[1 + projection].start)
        spread, _ = normalise(chain[layer, c].astype(F32))
        first = (spread * vec[layer, 0:1] + vec[layer, 1:2]).astype(BF16)
        second = (spread * vec[layer, 2:3] + vec[layer, 3:4]).astype(BF16)
        projected = dot_nt(first, wq[layer]) + vec[layer, 5:6]
        query = turn(projected[:, :lanes], start).astype(BF16)
        qkv[layer, here, :lanes] = query
        qkv[layer, here, lanes : 2 * lanes] = turn(projected[:, lanes : 2 * lanes], start).astype(
            BF16
        )
        qkv[layer, here, 2 * lanes :] = projected[:, 2 * lanes :].astype(BF16)
        if c == 0:
            for item in gifts[2 + projection :]:
                pl.when(layer == 0)(item.start)
            need(1 + projection, 2 + projection, layer)
        pre = dot_nn(second, w1[layer]) + vec[layer, 6:7]
        below = 0.5 * (1.0 + lax.erf(pre * (0.5**0.5)))
        active = (pre * below).astype(BF16)
        act[layer, here, :] = active
        slope = below + pre * (jnp.exp(-0.5 * pre * pre) * ((2.0 * np.pi) ** -0.5))
        gate[layer, here, :] = slope.astype(BF16)
        diagonal = lax.broadcasted_iota(jnp.int32, (rows, rows), 0) >= lax.broadcasted_iota(
            jnp.int32, (rows, rows), 1
        )
        context = jnp.zeros((rows, lanes), F32)
        for h in range(heads):
            asked = only(head_masks[h], query) * jnp.asarray(factor, BF16)
            near = dot_nt(asked, qkv[layer, here, lanes : 2 * lanes])
            near = jnp.where(diagonal, near, -1e30)
            highest = jnp.max(near, axis=-1, keepdims=True)
            if c > 0:
                far = dot_nt(asked, qkv[layer, :start, lanes : 2 * lanes])
                highest = jnp.maximum(highest, jnp.max(far, axis=-1, keepdims=True))
                far = jnp.exp(far - highest)
            near = jnp.exp(near - highest)
            total = jnp.sum(near, axis=-1, keepdims=True)
            if c > 0:
                total = total + jnp.sum(far, axis=-1, keepdims=True)
            inverse = 1.0 / total
            near = (near * inverse).astype(BF16)
            probs[c][layer, h, :, start:] = near
            mixed = dot_nn(near, qkv[layer, here, 2 * lanes :])
            if c > 0:
                far = (far * inverse).astype(BF16)
                probs[c][layer, h, :, :start] = far
                mixed = mixed + dot_nn(far, qkv[layer, :start, 2 * lanes :])
            context = jnp.where(head_masks[h], mixed, context)
        context = context.astype(BF16)
        ctx[layer, here, :] = context
        if c == 0:
            need(2 + projection, 4 + projection, layer)
        result = (dot_nn(context, wd[layer]) + dot_nn(active, w2[layer])).astype(BF16)
        for index, goal in enumerate((part, late_part)):
            pl.when(layer == index)(functools.partial(put, goal, c, result))
        return second

    def feed_back(c, second):
        here = slice(c * rows, (c + 1) * rows)
        cotangent = chain[2, c]
        pre_grad = (dot_nt(cotangent, w2[1]) * gate[1, here, :].astype(F32)).astype(BF16)
        gate[1, here, :] = pre_grad
        if c < chunks - 1:
            norm_rows[...] = second
            add_forward_grads(1, c, c == 0)

    def rows_of(c):
        return pl.ds(pl.multiple_of(c * rows, rows), rows)

    def backward_front(layer, c):
        here = rows_of(c)
        cotangent = chain[3 - layer, c]
        context_grad[...] = dot_nt(cotangent, wd[layer]).astype(BF16)

        @pl.when(layer == 0)
        def _():
            back = dot_nt(cotangent, w2[0]) * gate[0, here, :].astype(F32)
            gate[0, here, :] = back.astype(BF16)

    def backward_attention(layer, c):
        start = c * rows
        stop = start + rows
        here = slice(start, stop)
        own = context_grad[...]
        query = qkv[layer, here, :lanes]
        weighed = own.astype(F32) * ctx[layer, here, :].astype(F32)
        query_grad = jnp.zeros((rows, lanes), F32)
        key_sum = None
        value_sum = None
        for h in range(heads):
            mask = head_masks[h]
            own_grad = only(mask, own)
            asked = only(mask, query) * jnp.asarray(factor, BF16)
            row_dot = jnp.sum(only(mask, weighed), axis=-1, keepdims=True)
            prob = probs[c][layer, h]
            prob_grad = dot_nt(own_grad, qkv[layer, :stop, 2 * lanes :])
            score_grad = (prob.astype(F32) * (prob_grad - row_dot)).astype(BF16)
            query_grad = jnp.where(
                mask, dot_nn(score_grad, qkv[layer, :stop, lanes : 2 * lanes]), query_grad
            )
            key_part = dot_tn(score_grad, asked)
            value_part = dot_tn(prob, own_grad)
            key_sum = key_part if key_sum is None else key_sum + key_part
            value_sum = value_part if value_sum is None else value_sum + value_part
        query_back[...] = query_grad * factor
        if c == chunks - 1:
            key_grad[:stop] = key_sum
            value_grad[:stop] = value_sum
        else:
            key_grad[:stop] += key_sum
            value_grad[:stop] += value_sum

    def backward_rest(layer, c):
        here = rows_of(c)
        start = pl.multiple_of(c * rows, rows)
        pre_grad = gate[layer, here]
        second_back = dot_nt(pre_grad, w1[layer])
        qkv[layer, here, :lanes] = turn_back(query_back[...], start).astype(BF16)
        qkv[layer, here, lanes : 2 * lanes] = turn_back(key_grad[here], start).astype(BF16)
        qkv[layer, here, 2 * lanes :] = value_grad[here].astype(BF16)
        projected_grad = qkv[layer, here, :]
        first_back = dot_nn(projected_grad, wq[layer])
        spread, rstd = normalise(chain[layer, c].astype(F32))
        back = first_back * vec[layer, 0:1] + second_back * vec[layer, 2:3]
        middle = jnp.mean(back, axis=-1, keepdims=True)
        tilt = jnp.mean(back * spread, axis=-1, keepdims=True)
        put(part, chunks - 1 - c, rstd * (back - middle - spread * tilt))
        first = (spread * vec[layer, 0:1] + vec[layer, 1:2]).astype(BF16)
        norm_rows[...] = (spread * vec[layer, 2:3] + vec[layer, 3:4]).astype(BF16)
        sums = (
            first_back * spread,
            first_back,
            second_back * spread,
            second_back,
            projected_grad.astype(F32),
            chain[3 - layer, c].astype(F32),
            pre_grad.astype(F32),
        )
        for index, item in enumerate(sums):
            small[layer, index : index + 1] += jnp.sum(item, axis=0, keepdims=True)
        return first

    def add_piece_grads(layer, start, piece, first_turn):
        goal = slice(start, start + piece.shape[0])
        before = jnp.where(first_turn, 0.0, total[layer, goal].astype(F32))
        total[layer, goal] = (piece + before).astype(BF16)

    def add_forward_grads(layer, c, first_turn):
        here = rows_of(c)
        cotangent = chain.at[3 - layer, c]

        def add_block(index, carry):
            block = pl.ds(pl.multiple_of(index * lanes, lanes), lanes)
            goal = pl.ds(pl.multiple_of(width + index * lanes, lanes), lanes)
            pieces = (
                (block, dot_tn(norm_rows[:, block], gate[layer, here])),
                (goal, dot_tn(act[layer, here, block], cotangent[...])),
            )
            for at, piece in pieces:
                before = jnp.where(first_turn, 0.0, total[layer, at].astype(F32))
                total[layer, at] = (piece + before).astype(BF16)
            return carry

        lax.fori_loop(0, width // lanes, add_block, 0)

    def add_weight_grads(layer, c, first):
        base = width + act.shape[-1]
        here = rows_of(c)
        first_turn = c == chunks - 1
        for part_index in range(3):
            at = part_index * lanes
            piece = dot_tn(qkv[layer, here, at : at + lanes], first)
            for h in range(heads):
                row = base + (3 * h + part_index) * HEAD
                add_piece_grads(layer, row, piece[h * HEAD : (h + 1) * HEAD], first_turn)
        piece = dot_tn(ctx[layer, here], chain[3 - layer, c])[:valid]
        add_piece_grads(layer, base + 3 * valid, piece, first_turn)

    cut = width + act.shape[-1]
    jobs = ((0, cut), (cut, total.shape[1] - cut))
    folds = min(bits, 2)
    sum_steps = 2 + 2 * folds + (bits - folds)

    def spans(job, group):
        order = ((0, 1), (1, 0))[group][:folds]
        base, size = jobs[job]
        size = size // 4
        start = base + section * size * 2 + group * size
        steps = []
        for bit in order:
            size = size // 2
            upper = lax.rem(replica // (1 << bit), 2)
            steps.append((bit, start + upper * size, start + (1 - upper) * size, size))
            start = start + upper * size
        return steps, start, size

    groups = [[spans(job, group) for group in range(2)] for job in range(2)]

    def sums_of(layer, start, size):
        return total.at[layer, pl.ds(pl.multiple_of(start, 16), size)]

    def gathered(layer, job, group, start, size):
        base, job_rows = jobs[job]
        start = start - base - section * (job_rows // 2) - group * (job_rows // 4) + base // 4
        return (act, gate)[group].at[layer, pl.ds(pl.multiple_of(start, 16), size)]

    def sum_sems(layer, job, step, group):
        return sum_send.at[layer, job, step, group], sum_recv.at[layer, job, step, group]

    def landing_of(buffer, job, parts):
        base, job_rows = jobs[job]
        return buffer.at[base // parts : (base + job_rows) // parts]

    def sum_copies(layer, job, step):
        base, job_rows = jobs[job]
        if step == 0:
            source = sums_of(layer, base + (1 - section) * (job_rows // 2), job_rows // 2)
            goal = landing_of(half_got.at[layer], job, 2)
            return [send(source, goal, sum_sems(layer, job, 0, 0), twin)]
        copies_now = []
        for group, (steps, start, size) in enumerate(groups[job]):
            sems = sum_sems(layer, job, step, group)
            if step <= folds:
                bit, _, gone, size = steps[step - 1]
                goal = landing_of((first_got, second_got)[step - 1].at[group], job, 4 << step)
                copies_now.append(send(sums_of(layer, gone, size), goal, sems, mates[bit]))
            elif step <= bits:
                goal = landing_of(more_got.at[layer, step - 1 - folds, group], job, 16)
                source = gathered(layer, job, group, start, size)
                copies_now.append(send(source, goal, sems, mates[step - 1]))
            else:
                bit, start, _, size = steps[bits - step]
                piece = gathered(layer, job, group, start, size)
                copies_now.append(send(piece, piece, sems, mates[bit]))
        return copies_now

    def last_copies(layer, job):
        base, job_rows = jobs[job]
        size = job_rows // 4
        pieces = []
        for group in range(2):
            first_row = base + section * (job_rows // 2) + group * size
            piece = gathered(layer, job, group, first_row, size)
            goal = grads.at[pl.ds(pl.multiple_of(first_row, 16), size)]
            sems = sum_sems(layer, job, sum_steps - 1, group)
            other_row = base + (1 - section) * (job_rows // 2) + group * size
            other = grads.at[pl.ds(pl.multiple_of(other_row, 16), size)]
            pieces.append(
                (
                    send(piece, goal, sems, twin),
                    send(piece, other, sems, twin),
                    pltpu.make_async_copy(piece, goal, store_sem.at[job, group]),
                )
            )
        return pieces

    def sum_start(layer, job, step):
        if step < sum_steps - 1:
            if layer == 0 and 1 <= step <= folds:
                for group in range(2):
                    pl.semaphore_wait(free_sem.at[job, step - 1, group], 1)
            for item in sum_copies(layer, job, step):
                item.start()
            return
        for give, _, keep in last_copies(layer, job):
            pl.when(section != layer)(give.start)
            pl.when(section == layer)(keep.start)

    def add_rows(goal, base, source):
        size = source.shape[0]
        piece = math.gcd(size, 192)

        def add_piece(index, carry):
            here = pl.ds(pl.multiple_of(index * piece, 16), piece)
            goal[here] = (base[here].astype(F32) + source[here].astype(F32)).astype(BF16)
            return carry

        lax.fori_loop(0, size // piece, add_piece, 0)

    def sum_end(layer, job, step):
        if step == sum_steps - 1:
            for give, take, keep in last_copies(layer, job):
                pl.when(section != layer)(give.wait_send)
                pl.when(section == layer)(take.wait_recv)
                pl.when(section == layer)(keep.wait)
            return
        for item in sum_copies(layer, job, step):
            item.wait()
        if step == 0:
            base, job_rows = jobs[job]
            kept = sums_of(layer, base + section * (job_rows // 2), job_rows // 2)
            add_rows(kept, kept, landing_of(half_got.at[layer], job, 2))
            return
        if step > bits:
            return
        for group, (steps, start, size) in enumerate(groups[job]):
            goal = gathered(layer, job, group, start, size)
            if step < folds:
                base = sums_of(layer, steps[step - 1][1], steps[step - 1][3])
                add_rows(base, base, landing_of(first_got.at[group], job, 8))
            elif step == folds:
                add_rows(goal, sums_of(layer, start, size), landing_of(second_got.at[group], job, 16))
            else:
                landed = landing_of(more_got.at[layer, step - 1 - folds, group], job, 16)
                add_rows(goal, goal, landed)
            if layer == 1 and step <= folds:
                mate = mates[steps[step - 1][0]]
                pl.semaphore_signal(
                    free_sem.at[job, step - 1, group],
                    inc=1,
                    device_id=mate,
                    device_id_type=MESH,
                )

    steps_done = {(layer, job): 0 for layer in range(2) for job in range(2)}

    def move_sum(layer, job, step=None):
        step = steps_done[layer, job] if step is None else step
        if step < sum_steps:
            sum_end(layer, job, step)
            if step + 1 < sum_steps:
                sum_start(layer, job, step + 1)
            steps_done[layer, job] = max(steps_done[layer, job], step + 1)

    line_friends = [twin] + mates + [near, far]

    def line_copy(step):
        sems = (line_send.at[step], line_recv.at[step])
        return send(small, line_got.at[step], sems, line_friends[step])

    def line_end(step):
        line_copy(step).wait()
        if step <= bits:
            small[...] += line_got[step]
        else:
            small[:, 0:4] += line_got[step, :, 0:4]

    low_side = place < 2
    own_half = pl.multiple_of(jnp.where(low_side, 0, half_width), LANES)
    other_half = pl.multiple_of(jnp.where(low_side, half_width, 0), LANES)
    window = place * columns // LANES * LANES
    window = pl.multiple_of(window, LANES)
    end_window = pl.multiple_of(jnp.where(low_side, 0, width - padded), LANES)

    sent_width = width - LANES
    sent_lanes = pl.ds(pl.multiple_of(jnp.where(low_side, LANES, 0), LANES), sent_width)

    def spot(kind, u):
        chunk = u // halves if kind < 2 else chunks - 1 - u // halves
        return chunk, pl.ds(pl.multiple_of(lax.rem(u, halves) * unit, unit), unit)

    def buffers(kind, u):
        if kind == 1:
            return late_part.at[u], late_got.at[u], late_met.at[u]
        return part.at[u], got.at[u], met.at[u] if kind != 3 else met.at[u, :, :half_width]

    def hop_sems(kind, stage, u):
        return hop_send.at[int(kind == 1), stage, u], hop_recv.at[int(kind == 1), stage, u]

    def first_hop(kind, u):
        own, landing, _ = buffers(kind, u)
        if kind in (1, 3):
            own, landing = own.at[:, sent_lanes], landing.at[:, :sent_width]
        return send(own, landing, hop_sems(kind, 0, u), near)

    def second_hop(kind, u):
        own, _, landing = buffers(kind, u)
        if kind in (1, 3):
            own = own.at[:, pl.ds(other_half, half_width)]
        return send(own, landing, hop_sems(kind, 1, u), far)

    def third_hop(kind, u):
        own, _, landing = buffers(kind, u)
        if kind in (1, 3):
            own, landing = own.at[:, pl.ds(end_window, padded)], landing.at[:, :padded]
        else:
            chunk, here = spot(kind, u)
            own = landing = chain.at[kind + 1, chunk, here]
        return send(own, landing, hop_sems(kind, 2, u), near)

    def by_rows(count, work, step=32):
        def turn_rows(index, carry):
            work(pl.ds(pl.multiple_of(index * step, step), step))
            return carry

        lax.fori_loop(0, count // step, turn_rows, 0)

    def launch(kind, c):
        @pl.when(outer)
        def _():
            for half in range(halves):
                first_hop(kind, c * halves + half).start()

    def meet(kind, u):
        @pl.when(inner)
        def _():
            first_hop(kind, u).wait_recv()
            own, landed, _ = buffers(kind, u)
            if kind in (1, 3):
                own, landed = own.at[:, sent_lanes], landed.at[:, :sent_width]

            def add(here):
                own[here] = (own[here].astype(F32) + landed[here].astype(F32)).astype(BF16)

            by_rows(unit, add)
            second_hop(kind, u).start()

    def settle(kind, u):
        chunk, here = spot(kind, u)

        @pl.when(inner)
        def _():
            second_hop(kind, u).wait_recv()
            own, _, landed = buffers(kind, u)
            if kind in (1, 3):
                lanes_here = pl.ds(own_half, half_width)
                goal = own.at[:, lanes_here]
                source = goal
                base = chain.at[kind, chunk, here, lanes_here]
            else:
                lanes_here = slice(None)
                goal = chain.at[kind + 1, chunk, here]
                source = own
                base = chain.at[kind, chunk, here]

            def add(at):
                value = source[at].astype(F32) + landed[at].astype(F32) + base[at].astype(F32)
                if kind < 2:
                    value = value + vec[kind, 4:5, lanes_here]
                goal[at] = value.astype(BF16)

            by_rows(unit, add)
            if kind > 1:
                third_hop((0, 2)[kind - 2], u).wait_send()
            third_hop(kind, u).start()

    def arrive(kind, c):
        @pl.when(outer)
        def _():
            for half in range(halves):
                third_hop(kind, c * halves + half).wait_recv()

    def release(kind, c):
        for half in range(halves):
            u = c * halves + half
            pl.when(outer)(first_hop(kind, u).wait_send)
            pl.when(inner)(second_hop(kind, u).wait_send)

    def let_go(kind):
        for u in range(units):
            pl.when(inner)(third_hop(kind, u).wait_send)

    def serve(kind, meets, settles):
        for index in range(max(len(meets), len(settles))):
            if index < len(meets):
                meet(kind, meets[index])
            if index < len(settles):
                settle(kind, settles[index])

    def need(first, last, layer):
        @pl.when(section == layer)
        def _():
            for index in range(max(first, 1), last):
                loads[index - 1].wait()

        @pl.when(section != layer)
        def _():
            for index in range(first, last):
                gifts[index].wait_recv()

    input_load.wait()

    first_turns = (((), ()), ((), ()), ((0,), ()), ((1, 2), (0, 1)))
    second_turns = (
        (((3,), (2,)), ((4,), (3,))),
        (((5,), (4,)), ((6,), (5,))),
        (((7,), (6,)), ((), (7,))),
        (((), ()), ((), ())),
    )

    def weigh(c):
        chain[2, c] = (vec[0, 7:8] * chain[2, c].astype(F32)).astype(BF16)

    def find_share():
        own_mark = jnp.where(section == 0, marks[0], marks[1])[0:1]
        own_count = jnp.sum(own_mark * tally[0:1], axis=-1, keepdims=True)
        share = (tissue.shape[0] * copies / TISSUES) / own_count
        gifts[0].wait_send()
        vec[0, 7:8] = jnp.broadcast_to(share, (1, width))
        target_load.wait()

    def forward_layer(layer, carry):
        for c in range(chunks):
            pl.when(layer == 1)(functools.partial(arrive, 0, c))
            second = forward_chunk(layer, c)

            @pl.when(layer == 0)
            def _():
                launch(0, c)
                serve(0, *first_turns[c])
                for bit in range(bits):
                    if min(bit, chunks - 1) == c:
                        count_on(bit)

            @pl.when(layer == 1)
            def _():
                serve(0, *second_turns[c][0])
                if c in (1, 2):
                    launch(1, c - 1)
                if c == 0:
                    find_share()
                weigh(c)
                feed_back(c, second)
                serve(0, *second_turns[c][1])

        return carry

    lax.fori_loop(0, 2, forward_layer, 0)

    meets = {1: (1, 1, 3, 3), 2: (4, 5, 6, 7, 8, 9, 10, 11), 3: (13,)}
    settles = {1: (3, 3, 4, 4), 2: (6, 7, 8, 9, 10, 11, 12, 12), 3: ()}
    backward_points = [[] for _ in range(8 * 2)]
    for kind in (1, 2, 3):
        order = [(2 * u, meet, kind, u, meets[kind][u]) for u in range(len(meets[kind]))]
        order += [(2 * u + 3, settle, kind, u, settles[kind][u]) for u in range(len(settles[kind]))]
        for _, work, kind_now, u, point in sorted(order, key=lambda item: item[0]):
            backward_points[point].append((work, kind_now, u))

    def serve_point(point):
        for work, kind, u in backward_points[point]:
            work(kind, u)

    sum_moves = {
        3: ((0, 0),),
        8: ((1, 0),),
        9: ((0, 2),),
        10: ((1, 1),),
        11: ((0, 3),),
        12: ((1, 2),),
        13: ((1, 3),),
    }

    def serve_at(step, point):
        for index in range(2 * chunks):
            number = index * 2 + point

            @pl.when(step == index)
            def _():
                serve_point(number)
                for job, end in sum_moves.get(number, ()):
                    move_sum(1, job, end)

    def backward_step(step, carry):
        turn_index = step // chunks
        at = lax.rem(step, chunks)
        layer = 1 - turn_index
        c = chunks - 1 - at
        last_step = step == 2 * chunks - 1

        @pl.when(layer == 0)
        def _():
            pl.when(at == 0)(functools.partial(move_sum, 1, 0, 1))
            arrive(2, at)
            release(2, at)

        pl.when(layer == 1)(functools.partial(release, 0, at))
        backward_front(layer, c)

        @pl.when(last_step)
        def _():
            spread, _ = normalise(chain[0, 0].astype(F32))
            norm_rows[...] = (spread * vec[0, 2:3] + vec[0, 3:4]).astype(BF16)
            add_forward_grads(0, 0, False)
            sum_start(0, 0, 0)

        for index in range(chunks):
            pl.when(c == index)(functools.partial(backward_attention, layer, index))
        serve_at(step, 0)
        first = backward_rest(layer, c)
        for index in range(2):
            pl.when(turn_index == index)(functools.partial(launch, 2 + index, at))
        pl.when(last_step)(functools.partial(move_sum, 0, 0))
        add_weight_grads(layer, c, first)

        @pl.when(jnp.logical_or(step == 0, jnp.logical_and(layer == 0, c > 0)))
        def _():
            add_forward_grads(layer, c, step == chunks)

        @pl.when(step == 0)
        def _():
            sum_start(1, 0, 0)

        @pl.when(jnp.logical_and(layer == 0, at > 1))
        def _():
            launch(1, at)

        pl.when(step == chunks - 1)(functools.partial(sum_start, 1, 1, 0))
        pl.when(last_step)(functools.partial(sum_start, 0, 1, 0))
        serve_at(step, 1)
        return carry

    lax.fori_loop(0, 2 * chunks, backward_step, 0)

    shift = lax.rem(place * columns, LANES)

    def staged(index, layer):
        return probs[-1].at[layer, index, :columns]

    def stage(index, layer, row, value):
        turned_value = value.astype(F32).T
        low = turned_value[:columns]
        high = turned_value[LANES // 2 : LANES // 2 + columns]
        goal = pl.ds(pl.multiple_of(row, unit), unit)
        staged(index, layer)[:, goal] = jnp.where(shift == 0, low, high).astype(BF16)

    def stage_whole(index, layer, kind):
        def stage_unit(u, carry):
            rows_here = pl.ds(pl.multiple_of(lax.rem(u, halves) * unit, unit), unit)
            source = chain.at[kind + 1, u // halves, rows_here, pl.ds(window, padded)]
            stage(index, layer, u * unit, source[...])
            return carry

        lax.fori_loop(0, units, stage_unit, 0)

    def stage_own(index, layer, kind):
        for c in range(chunks):
            arrive(kind, c)
            release(kind, c)
        let_go(kind)
        tile = lax.broadcasted_iota(jnp.int32, (1, padded), 1) // LANES
        unsent = tile == jnp.where(low_side, 0, padded // LANES - 1)
        store, landing = (late_part, late_met) if kind == 1 else (part, met)

        def stage_unit(u, carry):
            chunk = u // halves if kind == 1 else chunks - 1 - u // halves
            row = chunk * rows + lax.rem(u, halves) * unit

            @pl.when(outer)
            def _():
                mine = store[u, :, pl.ds(end_window, padded)]
                value = landing[u, :, :padded].astype(F32) + only(unsent, mine.astype(F32))
                stage(index, layer, row, value)

            @pl.when(inner)
            def _():
                stage(index, layer, row, store[u, :, pl.ds(window, padded)])

            return carry

        lax.fori_loop(0, units, stage_unit, 0)

    def swap_columns(index, goal):
        sems = (swap_send.at[index], swap_recv.at[index])
        return [
            send(staged(index, 1 - section), goal.at[section], sems, twin),
            pltpu.make_async_copy(staged(index, section), goal.at[section], load_sem.at[1 + index]),
        ]

    def line_next(step):
        if step < len(line_friends):
            line_end(step)
            if step + 1 < len(line_friends):
                line_copy(step + 1).start()

    line_copy(0).start()
    serve(3, (1, 2), (0,))
    move_sum(0, 1)
    settle(3, 1)
    line_next(0)
    stage_whole(0, 0, 0)
    serve(3, (3, 4), (2, 3))
    stage_whole(1, 1, 2)
    meet(3, 5)
    move_sum(1, 0)
    settle(3, 4)
    meet(1, 4)
    move_sum(0, 0)
    settle(3, 5)
    meet(1, 5)
    move_sum(0, 1)
    line_next(1)
    settle(1, 4)
    meet(3, 6)
    move_sum(0, 0)
    settle(1, 5)
    meet(3, 7)
    move_sum(0, 1)
    line_next(2)
    settle(3, 6)
    meet(1, 6)
    move_sum(0, 0)
    settle(3, 7)
    meet(1, 7)
    move_sum(0, 1)
    line_next(3)
    stage_own(1, 0, 3)
    moves = swap_columns(1, grad_cols)
    for item in moves:
        item.start()
    settle(1, 6)
    settle(1, 7)
    move_sum(1, 1)
    move_sum(0, 0)
    stage_own(0, 1, 1)
    late_moves = swap_columns(0, out_cols)
    for item in late_moves:
        item.start()
    move_sum(0, 1)
    for step in range(4, len(line_friends)):
        line_next(step)
    for _ in range(sum_steps):
        for job in range(2):
            move_sum(0, job)
            move_sum(1, job)
    lines[...] = small[section]
    for item in moves + late_moves:
        item.wait()
    for item in gifts[1:]:
        item.wait_send()


def train(x, target, tissue, weights, qkv_bias, vec):
    wq, wd, w1, w2 = weights
    count, seq_len, width = x.shape
    rows = min(ROWS, seq_len)
    chunks = seq_len // rows
    unit = min(UNIT, rows)
    pieces = seq_len // unit
    valid = wd.shape[0]
    heads = valid // HEAD
    lanes = -(-valid // LANES) * LANES
    units = w1.shape[1]
    columns = width // lax.axis_size("tensor")
    bits = lax.axis_size("dp").bit_length() - 1
    tables = jnp.asarray(rotary_tables(seq_len))
    total_rows = 3 * valid + width + units + valid
    hbm = pl.BlockSpec(memory_space=pl.ANY)
    vmem = pl.BlockSpec(memory_space=pltpu.VMEM)
    smem = pl.BlockSpec(memory_space=pltpu.SMEM)
    scratch = [
        pltpu.VMEM((2, 8, width), F32),
        pltpu.VMEM((2, 3 * lanes, width), BF16),
        pltpu.VMEM((2, lanes, width), BF16),
        pltpu.VMEM((2,) + w1.shape, BF16),
        pltpu.VMEM((2,) + w2.shape, BF16),
        pltpu.VMEM((2, 8, width), F32),
        pltpu.VMEM((4, chunks, rows, width), BF16),
        pltpu.VMEM((2, seq_len, 3 * lanes), BF16),
        pltpu.VMEM((2, seq_len, lanes), BF16),
        pltpu.VMEM((2, seq_len, units), BF16),
        pltpu.VMEM((2, seq_len, units), BF16),
        pltpu.VMEM((seq_len, lanes), F32),
        pltpu.VMEM((seq_len, lanes), F32),
        pltpu.VMEM((pieces, unit, width), BF16),
        pltpu.VMEM((pieces, unit, width), BF16),
        pltpu.VMEM((pieces, unit, width), BF16),
        pltpu.VMEM((pieces, unit, width), BF16),
        pltpu.VMEM((pieces, unit, width - LANES), BF16),
        pltpu.VMEM((pieces, unit, width // 2), BF16),
        pltpu.VMEM((rows, width), BF16),
        pltpu.VMEM((rows, lanes), BF16),
        pltpu.VMEM((rows, lanes), F32),
        pltpu.VMEM((2, total_rows, width), BF16),
        pltpu.VMEM((2, total_rows // 2, width), BF16),
        pltpu.VMEM((2, total_rows // 8, width), BF16),
        pltpu.VMEM((2, total_rows // 16, width), BF16),
        pltpu.VMEM((2, max(bits - 2, 1), 2, total_rows // 16 if bits > 2 else 16, width), BF16),
        pltpu.VMEM((3 + bits, 2, 8, width), F32),
        pltpu.VMEM((8, LANES), F32),
        pltpu.VMEM((max(bits, 1), 8, LANES), F32),
    ]
    probs = [pltpu.VMEM((2, heads, rows, (c + 1) * rows), BF16) for c in range(chunks)]
    semaphores = [
        pltpu.SemaphoreType.DMA((4 + 3 * heads + 3,)),
        pltpu.SemaphoreType.DMA((4 + 3 * heads,)),
        pltpu.SemaphoreType.DMA((4 + 3 * heads,)),
        pltpu.SemaphoreType.DMA((2, 3, pieces)),
        pltpu.SemaphoreType.DMA((2, 3, pieces)),
        pltpu.SemaphoreType.DMA((2,)),
        pltpu.SemaphoreType.DMA((2,)),
        pltpu.SemaphoreType.DMA((2, 2, bits + 4, 2)),
        pltpu.SemaphoreType.DMA((2, 2, bits + 4, 2)),
        pltpu.SemaphoreType.DMA((3 + bits,)),
        pltpu.SemaphoreType.DMA((3 + bits,)),
        pltpu.SemaphoreType.DMA((max(bits, 1),)),
        pltpu.SemaphoreType.DMA((max(bits, 1),)),
        pltpu.SemaphoreType.DMA((2, 2)),
        pltpu.SemaphoreType.REGULAR((2, 2, 2)),
    ]

    def body(*refs):
        ends = np.cumsum([9, len(vec), 4 + len(scratch), chunks])
        head, lines, main, kept = (
            refs[start:stop] for start, stop in zip([0, *ends[:-1]], ends, strict=True)
        )
        train_kernel(heads, *head, lines, *main, kept, *refs[ends[-1] :])

    return pl.pallas_call(
        body,
        out_shape=(
            jax.ShapeDtypeStruct((count, columns, seq_len), BF16),
            jax.ShapeDtypeStruct((count, columns, seq_len), BF16),
            jax.ShapeDtypeStruct((total_rows, width), BF16),
            jax.ShapeDtypeStruct((8, width), F32),
        ),
        in_specs=[hbm, hbm, smem, vmem, hbm, hbm, hbm, hbm, vmem] + [vmem] * len(vec),
        out_specs=(hbm, hbm, hbm, vmem),
        scratch_shapes=scratch + probs + semaphores,
        compiler_params=pltpu.CompilerParams(
            collective_id=0, has_side_effects=True, vmem_limit_bytes=63 * 2**20
        ),
    )(
        x.reshape(count, chunks, rows, width),
        target.reshape(count, chunks, rows, width),
        tissue,
        tables,
        wq,
        wd,
        w1,
        w2,
        qkv_bias,
        *vec,
    )


def widen_kernel(heads, cols, grad_cols, *refs):
    sources, lines = refs[:4], refs[4]
    out_cols, out_grad_cols, *goals = refs[5:]
    out_cols[...] = cols[...]
    out_grad_cols[...] = grad_cols[...].astype(F32)
    for source, goal in zip(sources, goals[:4], strict=True):
        goal[...] = source[...].astype(F32)
    for index, goal in zip((0, 1, 2, 3, 5, 6), goals[4:10], strict=True):
        goal[...] = lines[index : index + 1]
    line = lines[4:5]
    lanes = line.shape[1] // 3
    pieces = []
    for h in range(heads):
        for part_index in range(3):
            start = part_index * lanes + h * HEAD
            pieces.append(line[:, start : start + HEAD])
    goals[10][...] = jnp.concatenate(pieces, axis=1)


def widen(out_cols, grad_cols, total, lines, heads, units):
    steps = 6
    count, columns, seq_len = out_cols.shape
    width = total.shape[1]
    sizes = (width, units, 3 * heads * HEAD, heads * HEAD)
    starts = [0, *np.cumsum(sizes[:-1]).tolist()]
    col_spec = pl.BlockSpec((count, columns // steps, seq_len), lambda i: (0, i, 0))

    def rows_from(start, size):
        block = size // steps
        return pl.BlockSpec((block, width), lambda i: (start // block + i, 0))

    def line_spec(lanes):
        return pl.BlockSpec((1, lanes), lambda i: (0, 0))

    line = jax.ShapeDtypeStruct((1, width), F32)
    return pl.pallas_call(
        functools.partial(widen_kernel, heads),
        grid=(steps,),
        in_specs=[col_spec, col_spec]
        + [rows_from(start, size) for start, size in zip(starts, sizes, strict=True)]
        + [pl.BlockSpec(lines.shape, lambda i: (0, 0))],
        out_specs=[col_spec, col_spec]
        + [rows_from(0, size) for size in sizes]
        + [line_spec(width)] * 6
        + [line_spec(sizes[2])],
        out_shape=[
            jax.ShapeDtypeStruct(out_cols.shape, BF16),
            jax.ShapeDtypeStruct(out_cols.shape, F32),
        ]
        + [jax.ShapeDtypeStruct((size, width), F32) for size in sizes]
        + [line] * 6
        + [jax.ShapeDtypeStruct((1, sizes[2]), F32)],
    )(out_cols, grad_cols, total, total, total, total, lines)


def per_device(
    hidden_in,
    target,
    tissue,
    ln1_gain,
    ln1_bias,
    ln2_gain,
    ln2_bias,
    qkv_weight,
    qkv_bias,
    dense_weight,
    dense_bias,
    fc1_weight,
    fc1_bias,
    fc2_weight,
    fc2_bias,
):
    heads = dense_weight.shape[1] // HEAD
    units = fc1_weight.shape[-1]
    weights = (qkv_weight[0].T, dense_weight[0], fc1_weight[0], fc2_weight[0])
    vec = (ln1_gain, ln1_bias, ln2_gain, ln2_bias, dense_bias, fc2_bias, fc1_bias)
    out_cols, grad_cols, total, lines = train(hidden_in, target, tissue, weights, qkv_bias, vec)
    out_cols, grad_cols, fc1_grad, fc2_grad, qkv_grad, dense_grad, *lines = widen(
        out_cols, grad_cols, total, lines, heads, units
    )
    gain1, bias1, gain2, bias2, out_bias, fc1_bias_grad, qkv_bias_grad = lines
    return (
        out_cols.transpose(0, 2, 1)[None],
        grad_cols.transpose(0, 2, 1)[None],
        gain1,
        bias1,
        gain2,
        bias2,
        qkv_grad.T[None],
        qkv_bias_grad,
        dense_grad[None],
        out_bias,
        fc1_grad[None],
        fc1_bias_grad,
        fc2_grad[None],
        out_bias,
    )


def solution(mesh):
    return jax.shard_map(
        per_device,
        mesh=mesh,
        in_specs=(
            P("dp", None, None),
            P("dp", None, None),
            P("dp"),
            P("section", None),
            P("section", None),
            P("section", None),
            P("section", None),
            P("section", None, "tensor"),
            P("section", "tensor"),
            P("section", "tensor", None),
            P("section", None),
            P("section", None, "tensor"),
            P("section", "tensor"),
            P("section", "tensor", None),
            P("section", None),
        ),
        out_specs=(
            P("section", "dp", None, "tensor"),
            P("section", "dp", None, "tensor"),
            P("section", None),
            P("section", None),
            P("section", None),
            P("section", None),
            P("section", None, "tensor"),
            P("section", "tensor"),
            P("section", "tensor", None),
            P("section", None),
            P("section", None, "tensor"),
            P("section", "tensor"),
            P("section", "tensor", None),
            P("section", None),
        ),
        check_vma=False,
    )
```

```python
import functools
import math

import jax
import jax.numpy as jnp
import numpy as np
from jax import lax
from jax.experimental import pallas as pl
from jax.experimental.pallas import tpu as pltpu
from jax.sharding import PartitionSpec as P

HEAD = 64
ROT = 16
TISSUES = 16
ROWS = 256
UNIT = 128
LANES = 128
EPS = 1e-05
MESH = pl.DeviceIdType.MESH
F32 = jnp.float32
BF16 = jnp.bfloat16


def dot_nn(a, b):
    return lax.dot_general(a, b, (((1,), (0,)), ((), ())), preferred_element_type=F32)


def dot_nt(a, b):
    return lax.dot_general(a, b, (((1,), (1,)), ((), ())), preferred_element_type=F32)


def dot_tn(a, b):
    return lax.dot_general(a, b, (((0,), (0,)), ((), ())), preferred_element_type=F32)


def rotary_tables(seq_len):
    half = ROT // 2
    inverse = 10000.0 ** (-2.0 * np.arange(half) / ROT)
    angles = np.arange(seq_len)[:, None] * inverse[None, :]
    cosines = np.ones((seq_len, HEAD))
    sines = np.zeros((seq_len, HEAD))
    cosines[:, :half] = np.cos(angles)
    cosines[:, half:ROT] = np.cos(angles)
    sines[:, :half] = -np.sin(angles)
    sines[:, half:ROT] = np.sin(angles)
    tables = np.stack([np.tile(item, (1, LANES // HEAD)) for item in (cosines, sines)])
    return tables.astype(np.float32)


def normalise(value):
    center = value - jnp.mean(value, axis=-1, keepdims=True)
    rstd = lax.rsqrt(jnp.mean(center * center, axis=-1, keepdims=True) + EPS)
    return center * rstd, rstd


def train_kernel(
    heads,
    x_in,
    target_in,
    tissue,
    tables,
    wq_in,
    wd_in,
    w1_in,
    w2_in,
    qkv_bias,
    vec_in,
    out_cols,
    grad_cols,
    grads,
    lines,
    small,
    wq,
    wd,
    w1,
    w2,
    vec,
    chain,
    qkv,
    ctx,
    act,
    gate,
    key_grad,
    value_grad,
    part,
    late_part,
    got,
    met,
    late_got,
    late_met,
    norm_rows,
    context_grad,
    query_back,
    total,
    half_got,
    first_got,
    second_got,
    more_got,
    line_got,
    tally,
    tally_got,
    probs,
    load_sem,
    give_sem,
    take_sem,
    hop_send,
    hop_recv,
    swap_send,
    swap_recv,
    sum_send,
    sum_recv,
    line_send,
    line_recv,
    tally_send,
    tally_recv,
    store_sem,
    free_sem,
):
    section = lax.axis_index("section")
    replica = lax.axis_index("dp")
    place = lax.axis_index("tensor")
    copies = lax.axis_size("dp")
    bits = copies.bit_length() - 1
    _, chunks, rows, width = chain.shape
    unit = part.shape[1]
    halves = rows // unit
    units = chunks * halves
    half_width = late_met.shape[-1]
    lanes = wd.shape[1]
    valid = heads * HEAD
    columns = out_cols.shape[1]
    padded = -(-columns // LANES) * LANES
    inner = jnp.logical_and(place > 0, place < 3)
    outer = jnp.logical_not(inner)
    beside = place + 1 - 2 * lax.rem(place, 2)
    across = 3 - place

    def flipped(bit):
        return replica + (1 << bit) * (1 - 2 * lax.rem(replica // (1 << bit), 2))

    twin = {"section": 1 - section}
    mates = [{"dp": flipped(bit)} for bit in range(bits)]
    near = {"tensor": beside}
    far = {"tensor": across}
    friends = [twin, near, far] + mates

    def send(source, goal, sems, target):
        return pltpu.make_async_remote_copy(
            src_ref=source,
            dst_ref=goal,
            send_sem=sems[0],
            recv_sem=sems[1],
            device_id=target,
            device_id_type=MESH,
        )

    barrier = pltpu.get_barrier_semaphore()
    for friend in friends:
        pl.semaphore_signal(barrier, inc=1, device_id=friend, device_id_type=MESH)

    input_load = pltpu.make_async_copy(x_in.at[section], chain.at[0], load_sem.at[0])
    input_load.start()
    pairs = []
    for part_index in range(3):
        for h in range(heads):
            source = slice((3 * h + part_index) * HEAD, (3 * h + part_index + 1) * HEAD)
            goal = slice(part_index * lanes + h * HEAD, part_index * lanes + (h + 1) * HEAD)
            pairs.append((wq_in.at[source], wq.at[section, goal]))
    pairs += [(w1_in, w1.at[section]), (wd_in, wd.at[section, :valid]), (w2_in, w2.at[section])]
    loads = [
        pltpu.make_async_copy(source, goal, load_sem.at[4 + index])
        for index, (source, goal) in enumerate(pairs)
    ]
    for item in loads:
        item.start()
    target_load = pltpu.make_async_copy(target_in.at[section], chain.at[2], load_sem.at[3])
    target_load.start()

    for index, item in enumerate(vec_in):
        vec[section, index : index + 1] = item[...].astype(F32)
    vec[section, 4:5] = vec_in[4][...].astype(F32) + vec_in[5][...].astype(F32)
    line = qkv_bias[...].astype(F32)
    gap = [jnp.zeros((1, lanes - valid), F32)] if lanes > valid else []
    packed = []
    for part_index in range(3):
        for h in range(heads):
            packed.append(line[:, (3 * h + part_index) * HEAD : (3 * h + part_index + 1) * HEAD])
        packed += gap
    vec[section, 5:6] = jnp.concatenate(packed, axis=1)
    vec[section, 7:8] = jnp.zeros((1, width), F32)
    for layer in range(2):
        wd[layer, valid:] = jnp.zeros((lanes - valid, width), BF16)
        for part_index in range(3):
            pad = slice(part_index * lanes + valid, (part_index + 1) * lanes)
            wq[layer, pad] = jnp.zeros((lanes - valid, width), BF16)
    pl.semaphore_wait(barrier, len(friends))
    gifts = [
        send(source, goal, (give_sem.at[index], take_sem.at[index]), twin)
        for index, (source, goal) in enumerate(
            [(vec.at[section], vec.at[section])] + pairs
        )
    ]
    projection = 3 * heads
    for item in gifts[: 2 + projection]:
        item.start()

    small[...] = jnp.zeros_like(small)
    tissue_lane = lax.broadcasted_iota(jnp.int32, (8, LANES), 1)
    marks = [(tissue_lane == tissue[index]).astype(F32) for index in range(tissue.shape[0])]
    tally[...] = functools.reduce(lambda a, b: a + b, marks)

    def tally_step(bit):
        return send(
            tally, tally_got.at[bit], (tally_send.at[bit], tally_recv.at[bit]), mates[bit]
        )

    if bits:
        tally_step(0).start()

    def count_on(bit):
        step = tally_step(bit)
        step.wait()
        tally[...] += tally_got[bit]
        if bit + 1 < bits:
            tally_step(bit + 1).start()

    lane = lax.broadcasted_iota(jnp.int32, (1, lanes), 1) // HEAD
    head_masks = [lane == h for h in range(heads)]
    factor = HEAD ** (-0.5)

    left_half = lax.rem(lax.broadcasted_iota(jnp.int32, (1, lanes), 1), HEAD) < ROT // 2

    def wide(table, start):
        piece = tables[table, pl.ds(start, rows), :]
        return jnp.concatenate([piece] * (lanes // LANES), axis=1)

    def turned(value):
        ahead = pltpu.roll(value, lanes - ROT // 2, 1)
        behind = pltpu.roll(value, ROT // 2, 1)
        return jnp.where(left_half, ahead, behind)

    def turn(value, start):
        return value * wide(0, start) + turned(value) * wide(1, start)

    def turn_back(value, start):
        return value * wide(0, start) - turned(value) * wide(1, start)

    def only(mask, value):
        return jnp.where(mask, value, jnp.zeros_like(value))

    def put(goal, slot, value):
        for half in range(halves):
            piece = value[half * unit : (half + 1) * unit]
            goal[slot * halves + half] = piece.astype(BF16)

    def forward_chunk(layer, c):
        start = c * rows
        here = slice(start, start + rows)
        if c == 0:
            need(0, 1 + projection, layer)
            for item in gifts[2 + projection :]:
                pl.when(layer == 0)(item.start)
        spread, _ = normalise(chain[layer, c].astype(F32))
        first = (spread * vec[layer, 0:1] + vec[layer, 1:2]).astype(BF16)
        second = (spread * vec[layer, 2:3] + vec[layer, 3:4]).astype(BF16)
        projected = dot_nt(first, wq[layer]) + vec[layer, 5:6]
        query = turn(projected[:, :lanes], start).astype(BF16)
        qkv[layer, here, :lanes] = query
        qkv[layer, here, lanes : 2 * lanes] = turn(projected[:, lanes : 2 * lanes], start).astype(
            BF16
        )
        qkv[layer, here, 2 * lanes :] = projected[:, 2 * lanes :].astype(BF16)
        if c == 0:
            need(1 + projection, 2 + projection, layer)
        pre = dot_nn(second, w1[layer]) + vec[layer, 6:7]
        below = 0.5 * (1.0 + lax.erf(pre * (0.5**0.5)))
        active = (pre * below).astype(BF16)
        act[layer, here, :] = active
        slope = below + pre * (jnp.exp(-0.5 * pre * pre) * ((2.0 * np.pi) ** -0.5))
        gate[layer, here, :] = slope.astype(BF16)
        diagonal = lax.broadcasted_iota(jnp.int32, (rows, rows), 0) >= lax.broadcasted_iota(
            jnp.int32, (rows, rows), 1
        )
        context = jnp.zeros((rows, lanes), F32)
        for h in range(heads):
            asked = only(head_masks[h], query) * jnp.asarray(factor, BF16)
            near = dot_nt(asked, qkv[layer, here, lanes : 2 * lanes])
            near = jnp.where(diagonal, near, -1e30)
            highest = jnp.max(near, axis=-1, keepdims=True)
            if c > 0:
                far = dot_nt(asked, qkv[layer, :start, lanes : 2 * lanes])
                highest = jnp.maximum(highest, jnp.max(far, axis=-1, keepdims=True))
                far = jnp.exp(far - highest)
            near = jnp.exp(near - highest)
            total = jnp.sum(near, axis=-1, keepdims=True)
            if c > 0:
                total = total + jnp.sum(far, axis=-1, keepdims=True)
            inverse = 1.0 / total
            near = (near * inverse).astype(BF16)
            probs[c][layer, h, :, start:] = near
            mixed = dot_nn(near, qkv[layer, here, 2 * lanes :])
            if c > 0:
                far = (far * inverse).astype(BF16)
                probs[c][layer, h, :, :start] = far
                mixed = mixed + dot_nn(far, qkv[layer, :start, 2 * lanes :])
            context = jnp.where(head_masks[h], mixed, context)
        context = context.astype(BF16)
        ctx[layer, here, :] = context
        if c == 0:
            need(2 + projection, 4 + projection, layer)
        result = (dot_nn(context, wd[layer]) + dot_nn(active, w2[layer])).astype(BF16)
        for index, goal in enumerate((part, late_part)):
            pl.when(layer == index)(functools.partial(put, goal, c, result))
        return second

    def feed_back(c, second):
        here = slice(c * rows, (c + 1) * rows)
        cotangent = chain[2, c]
        pre_grad = (dot_nt(cotangent, w2[1]) * gate[1, here, :].astype(F32)).astype(BF16)
        gate[1, here, :] = pre_grad
        if c < chunks - 1:
            norm_rows[...] = second
            add_forward_grads(1, c, c == 0)

    def rows_of(c):
        return pl.ds(pl.multiple_of(c * rows, rows), rows)

    def backward_front(layer, c):
        here = rows_of(c)
        cotangent = chain[3 - layer, c]
        context_grad[...] = dot_nt(cotangent, wd[layer]).astype(BF16)

        @pl.when(layer == 0)
        def _():
            back = dot_nt(cotangent, w2[0]) * gate[0, here, :].astype(F32)
            gate[0, here, :] = back.astype(BF16)

    def backward_attention(layer, c):
        start = c * rows
        stop = start + rows
        here = slice(start, stop)
        own = context_grad[...]
        query = qkv[layer, here, :lanes]
        weighed = own.astype(F32) * ctx[layer, here, :].astype(F32)
        query_grad = jnp.zeros((rows, lanes), F32)
        key_sum = None
        value_sum = None
        for h in range(heads):
            mask = head_masks[h]
            own_grad = only(mask, own)
            asked = only(mask, query) * jnp.asarray(factor, BF16)
            row_dot = jnp.sum(only(mask, weighed), axis=-1, keepdims=True)
            prob = probs[c][layer, h]
            prob_grad = dot_nt(own_grad, qkv[layer, :stop, 2 * lanes :])
            score_grad = (prob.astype(F32) * (prob_grad - row_dot)).astype(BF16)
            query_grad = jnp.where(
                mask, dot_nn(score_grad, qkv[layer, :stop, lanes : 2 * lanes]), query_grad
            )
            key_part = dot_tn(score_grad, asked)
            value_part = dot_tn(prob, own_grad)
            key_sum = key_part if key_sum is None else key_sum + key_part
            value_sum = value_part if value_sum is None else value_sum + value_part
        query_back[...] = query_grad * factor
        if c == chunks - 1:
            key_grad[:stop] = key_sum
            value_grad[:stop] = value_sum
        else:
            key_grad[:stop] += key_sum
            value_grad[:stop] += value_sum

    def backward_rest(layer, c):
        here = rows_of(c)
        start = pl.multiple_of(c * rows, rows)
        pre_grad = gate[layer, here]
        second_back = dot_nt(pre_grad, w1[layer])
        qkv[layer, here, :lanes] = turn_back(query_back[...], start).astype(BF16)
        qkv[layer, here, lanes : 2 * lanes] = turn_back(key_grad[here], start).astype(BF16)
        qkv[layer, here, 2 * lanes :] = value_grad[here].astype(BF16)
        projected_grad = qkv[layer, here, :]
        first_back = dot_nn(projected_grad, wq[layer])
        spread, rstd = normalise(chain[layer, c].astype(F32))
        back = first_back * vec[layer, 0:1] + second_back * vec[layer, 2:3]
        middle = jnp.mean(back, axis=-1, keepdims=True)
        tilt = jnp.mean(back * spread, axis=-1, keepdims=True)
        put(part, chunks - 1 - c, rstd * (back - middle - spread * tilt))
        first = (spread * vec[layer, 0:1] + vec[layer, 1:2]).astype(BF16)
        norm_rows[...] = (spread * vec[layer, 2:3] + vec[layer, 3:4]).astype(BF16)
        sums = (
            first_back * spread,
            first_back,
            second_back * spread,
            second_back,
            projected_grad.astype(F32),
            chain[3 - layer, c].astype(F32),
            pre_grad.astype(F32),
        )
        for index, item in enumerate(sums):
            small[layer, index : index + 1] += jnp.sum(item, axis=0, keepdims=True)
        return first

    def add_piece_grads(layer, start, piece, first_turn):
        goal = slice(start, start + piece.shape[0])
        before = jnp.where(first_turn, 0.0, total[layer, goal].astype(F32))
        total[layer, goal] = (piece + before).astype(BF16)

    def add_forward_grads(layer, c, first_turn):
        here = rows_of(c)
        cotangent = chain.at[3 - layer, c]

        def add_block(index, carry):
            block = pl.ds(pl.multiple_of(index * lanes, lanes), lanes)
            goal = pl.ds(pl.multiple_of(width + index * lanes, lanes), lanes)
            pieces = (
                (block, dot_tn(norm_rows[:, block], gate[layer, here])),
                (goal, dot_tn(act[layer, here, block], cotangent[...])),
            )
            for at, piece in pieces:
                before = jnp.where(first_turn, 0.0, total[layer, at].astype(F32))
                total[layer, at] = (piece + before).astype(BF16)
            return carry

        lax.fori_loop(0, width // lanes, add_block, 0)

    def add_weight_grads(layer, c, first):
        base = width + act.shape[-1]
        here = rows_of(c)
        first_turn = c == chunks - 1
        for part_index in range(3):
            at = part_index * lanes
            piece = dot_tn(qkv[layer, here, at : at + lanes], first)
            for h in range(heads):
                row = base + (3 * h + part_index) * HEAD
                add_piece_grads(layer, row, piece[h * HEAD : (h + 1) * HEAD], first_turn)
        piece = dot_tn(ctx[layer, here], chain[3 - layer, c])[:valid]
        add_piece_grads(layer, base + 3 * valid, piece, first_turn)

    cut = width + act.shape[-1]
    jobs = ((0, cut), (cut, total.shape[1] - cut))
    folds = min(bits, 2)
    sum_steps = 2 + 2 * folds + (bits - folds)

    def spans(job, group):
        order = ((0, 1), (1, 0))[group][:folds]
        base, size = jobs[job]
        size = size // 4
        start = base + section * size * 2 + group * size
        steps = []
        for bit in order:
            size = size // 2
            upper = lax.rem(replica // (1 << bit), 2)
            steps.append((bit, start + upper * size, start + (1 - upper) * size, size))
            start = start + upper * size
        return steps, start, size

    groups = [[spans(job, group) for group in range(2)] for job in range(2)]

    def sums_of(layer, start, size):
        return total.at[layer, pl.ds(pl.multiple_of(start, 16), size)]

    def gathered(layer, job, group, start, size):
        base, job_rows = jobs[job]
        start = start - base - section * (job_rows // 2) - group * (job_rows // 4) + base // 4
        return (act, gate)[group].at[layer, pl.ds(pl.multiple_of(start, 16), size)]

    def sum_sems(layer, job, step, group):
        return sum_send.at[layer, job, step, group], sum_recv.at[layer, job, step, group]

    def landing_of(buffer, job, parts):
        base, job_rows = jobs[job]
        return buffer.at[base // parts : (base + job_rows) // parts]

    def sum_copies(layer, job, step):
        base, job_rows = jobs[job]
        if step == 0:
            source = sums_of(layer, base + (1 - section) * (job_rows // 2), job_rows // 2)
            goal = landing_of(half_got.at[layer], job, 2)
            return [send(source, goal, sum_sems(layer, job, 0, 0), twin)]
        copies_now = []
        for group, (steps, start, size) in enumerate(groups[job]):
            sems = sum_sems(layer, job, step, group)
            if step <= folds:
                bit, _, gone, size = steps[step - 1]
                goal = landing_of((first_got, second_got)[step - 1].at[group], job, 4 << step)
                copies_now.append(send(sums_of(layer, gone, size), goal, sems, mates[bit]))
            elif step <= bits:
                goal = landing_of(more_got.at[layer, step - 1 - folds, group], job, 16)
                source = gathered(layer, job, group, start, size)
                copies_now.append(send(source, goal, sems, mates[step - 1]))
            else:
                bit, start, _, size = steps[bits - step]
                piece = gathered(layer, job, group, start, size)
                copies_now.append(send(piece, piece, sems, mates[bit]))
        return copies_now

    def last_copies(layer, job):
        base, job_rows = jobs[job]
        size = job_rows // 4
        pieces = []
        for group in range(2):
            first_row = base + section * (job_rows // 2) + group * size
            piece = gathered(layer, job, group, first_row, size)
            goal = grads.at[pl.ds(pl.multiple_of(first_row, 16), size)]
            sems = sum_sems(layer, job, sum_steps - 1, group)
            other_row = base + (1 - section) * (job_rows // 2) + group * size
            other = grads.at[pl.ds(pl.multiple_of(other_row, 16), size)]
            pieces.append(
                (
                    send(piece, goal, sems, twin),
                    send(piece, other, sems, twin),
                    pltpu.make_async_copy(piece, goal, store_sem.at[job, group]),
                )
            )
        return pieces

    def sum_start(layer, job, step):
        if step < sum_steps - 1:
            if layer == 0 and 1 <= step <= folds:
                for group in range(2):
                    pl.semaphore_wait(free_sem.at[job, step - 1, group], 1)
            for item in sum_copies(layer, job, step):
                item.start()
            return
        for give, _, keep in last_copies(layer, job):
            pl.when(section != layer)(give.start)
            pl.when(section == layer)(keep.start)

    def add_rows(goal, base, source):
        size = source.shape[0]
        piece = math.gcd(size, 192)

        def add_piece(index, carry):
            here = pl.ds(pl.multiple_of(index * piece, 16), piece)
            goal[here] = (base[here].astype(F32) + source[here].astype(F32)).astype(BF16)
            return carry

        lax.fori_loop(0, size // piece, add_piece, 0)

    def sum_end(layer, job, step):
        if step == sum_steps - 1:
            for give, take, keep in last_copies(layer, job):
                pl.when(section != layer)(give.wait_send)
                pl.when(section == layer)(take.wait_recv)
                pl.when(section == layer)(keep.wait)
            return
        for item in sum_copies(layer, job, step):
            item.wait()
        if step == 0:
            base, job_rows = jobs[job]
            kept = sums_of(layer, base + section * (job_rows // 2), job_rows // 2)
            add_rows(kept, kept, landing_of(half_got.at[layer], job, 2))
            return
        if step > bits:
            return
        for group, (steps, start, size) in enumerate(groups[job]):
            goal = gathered(layer, job, group, start, size)
            if step < folds:
                base = sums_of(layer, steps[step - 1][1], steps[step - 1][3])
                add_rows(base, base, landing_of(first_got.at[group], job, 8))
            elif step == folds:
                add_rows(goal, sums_of(layer, start, size), landing_of(second_got.at[group], job, 16))
            else:
                landed = landing_of(more_got.at[layer, step - 1 - folds, group], job, 16)
                add_rows(goal, goal, landed)
            if layer == 1 and step <= folds:
                mate = mates[steps[step - 1][0]]
                pl.semaphore_signal(
                    free_sem.at[job, step - 1, group],
                    inc=1,
                    device_id=mate,
                    device_id_type=MESH,
                )

    steps_done = {(layer, job): 0 for layer in range(2) for job in range(2)}

    def move_sum(layer, job, step=None):
        step = steps_done[layer, job] if step is None else step
        if step < sum_steps:
            sum_end(layer, job, step)
            if step + 1 < sum_steps:
                sum_start(layer, job, step + 1)
            steps_done[layer, job] = max(steps_done[layer, job], step + 1)

    line_friends = [twin] + mates + [near, far]

    def line_copy(step):
        sems = (line_send.at[step], line_recv.at[step])
        return send(small, line_got.at[step], sems, line_friends[step])

    def line_end(step):
        line_copy(step).wait()
        if step <= bits:
            small[...] += line_got[step]
        else:
            small[:, 0:4] += line_got[step, :, 0:4]

    low_side = place < 2
    own_half = pl.multiple_of(jnp.where(low_side, 0, half_width), LANES)
    other_half = pl.multiple_of(jnp.where(low_side, half_width, 0), LANES)
    window = place * columns // LANES * LANES
    window = pl.multiple_of(window, LANES)
    end_window = pl.multiple_of(jnp.where(low_side, 0, width - padded), LANES)

    sent_width = width - LANES
    sent_lanes = pl.ds(pl.multiple_of(jnp.where(low_side, LANES, 0), LANES), sent_width)

    def spot(kind, u):
        chunk = u // halves if kind < 2 else chunks - 1 - u // halves
        return chunk, pl.ds(pl.multiple_of(lax.rem(u, halves) * unit, unit), unit)

    def buffers(kind, u):
        if kind == 1:
            return late_part.at[u], late_got.at[u], late_met.at[u]
        return part.at[u], got.at[u], met.at[u] if kind != 3 else met.at[u, :, :half_width]

    def hop_sems(kind, stage, u):
        return hop_send.at[int(kind == 1), stage, u], hop_recv.at[int(kind == 1), stage, u]

    def first_hop(kind, u):
        own, landing, _ = buffers(kind, u)
        if kind in (1, 3):
            own, landing = own.at[:, sent_lanes], landing.at[:, :sent_width]
        return send(own, landing, hop_sems(kind, 0, u), near)

    def second_hop(kind, u):
        own, _, landing = buffers(kind, u)
        if kind in (1, 3):
            own = own.at[:, pl.ds(other_half, half_width)]
        return send(own, landing, hop_sems(kind, 1, u), far)

    def third_hop(kind, u):
        own, _, landing = buffers(kind, u)
        if kind in (1, 3):
            own, landing = own.at[:, pl.ds(end_window, padded)], landing.at[:, :padded]
        else:
            chunk, here = spot(kind, u)
            own = landing = chain.at[kind + 1, chunk, here]
        return send(own, landing, hop_sems(kind, 2, u), near)

    def by_rows(count, work, step=32):
        def turn_rows(index, carry):
            work(pl.ds(pl.multiple_of(index * step, step), step))
            return carry

        lax.fori_loop(0, count // step, turn_rows, 0)

    def launch(kind, c):
        @pl.when(outer)
        def _():
            for half in range(halves):
                first_hop(kind, c * halves + half).start()

    def meet(kind, u):
        @pl.when(inner)
        def _():
            first_hop(kind, u).wait_recv()
            own, landed, _ = buffers(kind, u)
            if kind in (1, 3):
                own, landed = own.at[:, sent_lanes], landed.at[:, :sent_width]

            def add(here):
                own[here] = (own[here].astype(F32) + landed[here].astype(F32)).astype(BF16)

            by_rows(unit, add)
            second_hop(kind, u).start()

    def settle(kind, u):
        chunk, here = spot(kind, u)

        @pl.when(inner)
        def _():
            second_hop(kind, u).wait_recv()
            own, _, landed = buffers(kind, u)
            if kind in (1, 3):
                lanes_here = pl.ds(own_half, half_width)
                goal = own.at[:, lanes_here]
                source = goal
                base = chain.at[kind, chunk, here, lanes_here]
            else:
                lanes_here = slice(None)
                goal = chain.at[kind + 1, chunk, here]
                source = own
                base = chain.at[kind, chunk, here]

            def add(at):
                value = source[at].astype(F32) + landed[at].astype(F32) + base[at].astype(F32)
                if kind < 2:
                    value = value + vec[kind, 4:5, lanes_here]
                goal[at] = value.astype(BF16)

            by_rows(unit, add)
            if kind > 1:
                third_hop((0, 2)[kind - 2], u).wait_send()
            third_hop(kind, u).start()

    def arrive(kind, c):
        @pl.when(outer)
        def _():
            for half in range(halves):
                third_hop(kind, c * halves + half).wait_recv()

    def release(kind, c):
        for half in range(halves):
            u = c * halves + half
            pl.when(outer)(first_hop(kind, u).wait_send)
            pl.when(inner)(second_hop(kind, u).wait_send)

    def let_go(kind):
        for u in range(units):
            pl.when(inner)(third_hop(kind, u).wait_send)

    def serve(kind, meets, settles):
        for index in range(max(len(meets), len(settles))):
            if index < len(meets):
                meet(kind, meets[index])
            if index < len(settles):
                settle(kind, settles[index])

    def need(first, last, layer):
        @pl.when(section == layer)
        def _():
            for index in range(max(first, 1), last):
                loads[index - 1].wait()

        @pl.when(section != layer)
        def _():
            for index in range(first, last):
                gifts[index].wait_recv()

    input_load.wait()

    first_turns = (((), ()), ((), ()), ((0,), ()), ((1, 2), (0, 1)))
    second_turns = (
        (((3,), (2,)), ((4,), (3,))),
        (((5,), (4,)), ((6,), (5,))),
        (((7,), (6,)), ((), (7,))),
        (((), ()), ((), ())),
    )

    def weigh(c):
        chain[2, c] = (vec[0, 7:8] * chain[2, c].astype(F32)).astype(BF16)

    def find_share():
        own_mark = jnp.where(section == 0, marks[0], marks[1])[0:1]
        own_count = jnp.sum(own_mark * tally[0:1], axis=-1, keepdims=True)
        share = (tissue.shape[0] * copies / TISSUES) / own_count
        gifts[0].wait_send()
        vec[0, 7:8] = jnp.broadcast_to(share, (1, width))
        target_load.wait()

    def forward_layer(layer, carry):
        for c in range(chunks):
            pl.when(layer == 1)(functools.partial(arrive, 0, c))
            second = forward_chunk(layer, c)

            @pl.when(layer == 0)
            def _():
                launch(0, c)
                serve(0, *first_turns[c])
                for bit in range(bits):
                    if min(bit, chunks - 1) == c:
                        count_on(bit)

            @pl.when(layer == 1)
            def _():
                serve(0, *second_turns[c][0])
                if c in (1, 2):
                    launch(1, c - 1)
                if c == 0:
                    find_share()
                weigh(c)
                feed_back(c, second)
                serve(0, *second_turns[c][1])

        return carry

    lax.fori_loop(0, 2, forward_layer, 0)

    meets = {1: (1, 1, 3, 3), 2: (4, 5, 6, 7, 8, 9, 10, 11), 3: (13,)}
    settles = {1: (3, 3, 5, 5), 2: (6, 7, 8, 9, 10, 11, 12, 12), 3: ()}
    backward_points = [[] for _ in range(8 * 2)]
    for kind in (1, 2, 3):
        order = [(2 * u, meet, kind, u, meets[kind][u]) for u in range(len(meets[kind]))]
        order += [(2 * u + 3, settle, kind, u, settles[kind][u]) for u in range(len(settles[kind]))]
        for _, work, kind_now, u, point in sorted(order, key=lambda item: item[0]):
            backward_points[point].append((work, kind_now, u))

    def serve_point(point):
        for work, kind, u in backward_points[point]:
            work(kind, u)

    sum_moves = {
        5: ((0, 0),),
        8: ((1, 0),),
        9: ((0, 2),),
        10: ((1, 1),),
        11: ((1, 2), (0, 3)),
        12: ((1, 3),),
    }

    def serve_at(step, point):
        for index in range(2 * chunks):
            number = index * 2 + point

            @pl.when(step == index)
            def _():
                serve_point(number)
                for job, end in sum_moves.get(number, ()):
                    move_sum(1, job, end)

    def backward_step(step, carry):
        turn_index = step // chunks
        at = lax.rem(step, chunks)
        layer = 1 - turn_index
        c = chunks - 1 - at
        last_step = step == 2 * chunks - 1

        @pl.when(layer == 0)
        def _():
            pl.when(at == 0)(functools.partial(move_sum, 1, 0, 1))
            arrive(2, at)
            release(2, at)

        pl.when(layer == 1)(functools.partial(release, 0, at))
        backward_front(layer, c)

        @pl.when(last_step)
        def _():
            spread, _ = normalise(chain[0, 0].astype(F32))
            norm_rows[...] = (spread * vec[0, 2:3] + vec[0, 3:4]).astype(BF16)
            add_forward_grads(0, 0, False)
            sum_start(0, 0, 0)

        for index in range(chunks):
            pl.when(c == index)(functools.partial(backward_attention, layer, index))
        serve_at(step, 0)
        first = backward_rest(layer, c)
        for index in range(2):
            pl.when(turn_index == index)(functools.partial(launch, 2 + index, at))
        pl.when(last_step)(functools.partial(move_sum, 0, 0))
        add_weight_grads(layer, c, first)

        @pl.when(jnp.logical_or(step == 0, jnp.logical_and(layer == 0, c > 0)))
        def _():
            add_forward_grads(layer, c, step == chunks)

        @pl.when(step == 0)
        def _():
            sum_start(1, 0, 0)

        @pl.when(jnp.logical_and(layer == 0, at > 1))
        def _():
            launch(1, at)

        pl.when(step == chunks - 1)(functools.partial(sum_start, 1, 1, 0))
        pl.when(last_step)(functools.partial(sum_start, 0, 1, 0))
        serve_at(step, 1)
        return carry

    lax.fori_loop(0, 2 * chunks, backward_step, 0)

    shift = lax.rem(place * columns, LANES)

    def staged(index, layer):
        return probs[-1].at[layer, index, :columns]

    def stage(index, layer, row, value):
        turned_value = value.astype(F32).T
        low = turned_value[:columns]
        high = turned_value[LANES // 2 : LANES // 2 + columns]
        goal = pl.ds(pl.multiple_of(row, unit), unit)
        staged(index, layer)[:, goal] = jnp.where(shift == 0, low, high).astype(BF16)

    def stage_whole(index, layer, kind):
        def stage_unit(u, carry):
            rows_here = pl.ds(pl.multiple_of(lax.rem(u, halves) * unit, unit), unit)
            source = chain.at[kind + 1, u // halves, rows_here, pl.ds(window, padded)]
            stage(index, layer, u * unit, source[...])
            return carry

        lax.fori_loop(0, units, stage_unit, 0)

    def stage_own(index, layer, kind):
        for c in range(chunks):
            arrive(kind, c)
            release(kind, c)
        let_go(kind)
        tile = lax.broadcasted_iota(jnp.int32, (1, padded), 1) // LANES
        unsent = tile == jnp.where(low_side, 0, padded // LANES - 1)
        store, landing = (late_part, late_met) if kind == 1 else (part, met)

        def stage_unit(u, carry):
            chunk = u // halves if kind == 1 else chunks - 1 - u // halves
            row = chunk * rows + lax.rem(u, halves) * unit

            @pl.when(outer)
            def _():
                mine = store[u, :, pl.ds(end_window, padded)]
                value = landing[u, :, :padded].astype(F32) + only(unsent, mine.astype(F32))
                stage(index, layer, row, value)

            @pl.when(inner)
            def _():
                stage(index, layer, row, store[u, :, pl.ds(window, padded)])

            return carry

        lax.fori_loop(0, units, stage_unit, 0)

    def swap_columns(index, goal):
        sems = (swap_send.at[index], swap_recv.at[index])
        return [
            send(staged(index, 1 - section), goal.at[section], sems, twin),
            pltpu.make_async_copy(staged(index, section), goal.at[section], load_sem.at[1 + index]),
        ]

    def line_next(step):
        if step < len(line_friends):
            line_end(step)
            if step + 1 < len(line_friends):
                line_copy(step + 1).start()

    line_copy(0).start()
    for item in gifts[1:]:
        item.wait_send()
    serve(3, (1, 2), (0,))
    move_sum(0, 1)
    settle(3, 1)
    line_next(0)
    stage_whole(0, 0, 0)
    serve(3, (3, 4), (2, 3))
    stage_whole(1, 1, 2)
    meet(3, 5)
    move_sum(1, 0)
    settle(3, 4)
    meet(1, 4)
    move_sum(0, 0)
    settle(3, 5)
    meet(1, 5)
    move_sum(0, 1)
    line_next(1)
    settle(1, 4)
    meet(3, 6)
    move_sum(0, 0)
    settle(1, 5)
    meet(3, 7)
    move_sum(0, 1)
    line_next(2)
    settle(3, 6)
    meet(1, 6)
    move_sum(0, 0)
    settle(3, 7)
    meet(1, 7)
    move_sum(0, 1)
    line_next(3)
    stage_own(1, 0, 3)
    moves = swap_columns(1, grad_cols)
    for item in moves:
        item.start()
    settle(1, 6)
    settle(1, 7)
    move_sum(1, 1)
    move_sum(0, 0)
    for step in range(4, len(line_friends)):
        line_next(step)
    lines_store = pltpu.make_async_copy(small.at[section], lines, load_sem.at[0])
    lines_store.start()
    move_sum(0, 1)
    stage_own(0, 1, 1)
    late_moves = swap_columns(0, out_cols)
    for item in late_moves:
        item.start()
    for _ in range(sum_steps):
        for job in range(2):
            move_sum(0, job)
            move_sum(1, job)
    for item in moves + late_moves:
        item.wait()
    lines_store.wait()


def train(x, target, tissue, weights, qkv_bias, vec):
    wq, wd, w1, w2 = weights
    count, seq_len, width = x.shape
    rows = min(ROWS, seq_len)
    chunks = seq_len // rows
    unit = min(UNIT, rows)
    pieces = seq_len // unit
    valid = wd.shape[0]
    heads = valid // HEAD
    lanes = -(-valid // LANES) * LANES
    units = w1.shape[1]
    columns = width // lax.axis_size("tensor")
    bits = lax.axis_size("dp").bit_length() - 1
    tables = jnp.asarray(rotary_tables(seq_len))
    total_rows = 3 * valid + width + units + valid
    hbm = pl.BlockSpec(memory_space=pl.ANY)
    vmem = pl.BlockSpec(memory_space=pltpu.VMEM)
    smem = pl.BlockSpec(memory_space=pltpu.SMEM)
    scratch = [
        pltpu.VMEM((2, 8, width), F32),
        pltpu.VMEM((2, 3 * lanes, width), BF16),
        pltpu.VMEM((2, lanes, width), BF16),
        pltpu.VMEM((2,) + w1.shape, BF16),
        pltpu.VMEM((2,) + w2.shape, BF16),
        pltpu.VMEM((2, 8, width), F32),
        pltpu.VMEM((4, chunks, rows, width), BF16),
        pltpu.VMEM((2, seq_len, 3 * lanes), BF16),
        pltpu.VMEM((2, seq_len, lanes), BF16),
        pltpu.VMEM((2, seq_len, units), BF16),
        pltpu.VMEM((2, seq_len, units), BF16),
        pltpu.VMEM((seq_len, lanes), F32),
        pltpu.VMEM((seq_len, lanes), F32),
        pltpu.VMEM((pieces, unit, width), BF16),
        pltpu.VMEM((pieces, unit, width), BF16),
        pltpu.VMEM((pieces, unit, width), BF16),
        pltpu.VMEM((pieces, unit, width), BF16),
        pltpu.VMEM((pieces, unit, width - LANES), BF16),
        pltpu.VMEM((pieces, unit, width // 2), BF16),
        pltpu.VMEM((rows, width), BF16),
        pltpu.VMEM((rows, lanes), BF16),
        pltpu.VMEM((rows, lanes), F32),
        pltpu.VMEM((2, total_rows, width), BF16),
        pltpu.VMEM((2, total_rows // 2, width), BF16),
        pltpu.VMEM((2, total_rows // 8, width), BF16),
        pltpu.VMEM((2, total_rows // 16, width), BF16),
        pltpu.VMEM((2, max(bits - 2, 1), 2, total_rows // 16 if bits > 2 else 16, width), BF16),
        pltpu.VMEM((3 + bits, 2, 8, width), F32),
        pltpu.VMEM((8, LANES), F32),
        pltpu.VMEM((max(bits, 1), 8, LANES), F32),
    ]
    probs = [pltpu.VMEM((2, heads, rows, (c + 1) * rows), BF16) for c in range(chunks)]
    semaphores = [
        pltpu.SemaphoreType.DMA((4 + 3 * heads + 3,)),
        pltpu.SemaphoreType.DMA((4 + 3 * heads,)),
        pltpu.SemaphoreType.DMA((4 + 3 * heads,)),
        pltpu.SemaphoreType.DMA((2, 3, pieces)),
        pltpu.SemaphoreType.DMA((2, 3, pieces)),
        pltpu.SemaphoreType.DMA((2,)),
        pltpu.SemaphoreType.DMA((2,)),
        pltpu.SemaphoreType.DMA((2, 2, bits + 4, 2)),
        pltpu.SemaphoreType.DMA((2, 2, bits + 4, 2)),
        pltpu.SemaphoreType.DMA((3 + bits,)),
        pltpu.SemaphoreType.DMA((3 + bits,)),
        pltpu.SemaphoreType.DMA((max(bits, 1),)),
        pltpu.SemaphoreType.DMA((max(bits, 1),)),
        pltpu.SemaphoreType.DMA((2, 2)),
        pltpu.SemaphoreType.REGULAR((2, 2, 2)),
    ]

    def body(*refs):
        ends = np.cumsum([9, len(vec), 4 + len(scratch), chunks])
        head, lines, main, kept = (
            refs[start:stop] for start, stop in zip([0, *ends[:-1]], ends, strict=True)
        )
        train_kernel(heads, *head, lines, *main, kept, *refs[ends[-1] :])

    return pl.pallas_call(
        body,
        out_shape=(
            jax.ShapeDtypeStruct((count, columns, seq_len), BF16),
            jax.ShapeDtypeStruct((count, columns, seq_len), BF16),
            jax.ShapeDtypeStruct((total_rows, width), BF16),
            jax.ShapeDtypeStruct((8, width), F32),
        ),
        in_specs=[hbm, hbm, smem, vmem, hbm, hbm, hbm, hbm, vmem] + [vmem] * len(vec),
        out_specs=(hbm, hbm, hbm, hbm),
        scratch_shapes=scratch + probs + semaphores,
        compiler_params=pltpu.CompilerParams(
            collective_id=0, has_side_effects=True, vmem_limit_bytes=63 * 2**20
        ),
    )(
        x.reshape(count, chunks, rows, width),
        target.reshape(count, chunks, rows, width),
        tissue,
        tables,
        wq,
        wd,
        w1,
        w2,
        qkv_bias,
        *vec,
    )


def widen_kernel(
    heads,
    sizes,
    cols,
    grad_cols,
    total,
    lines,
    out_cols,
    out_grad_cols,
    goal0,
    goal1,
    goal2,
    goal3,
    gain1,
    bias1,
    gain2,
    bias2,
    out_bias,
    out_bias_again,
    fc1_bias,
    qkv_bias,
    cols_kept,
    cols_low,
    cols_wide,
    rows_low,
    rows_wide,
    pass_sem,
    load_sem,
    store_sem,
):
    block = sizes[-1]
    through = pltpu.make_async_copy(cols, cols_kept, pass_sem.at[0])
    onward = pltpu.make_async_copy(cols_kept, out_cols, pass_sem.at[1])
    moves = []
    for index in range(cols.shape[0]):
        moves.append(
            (grad_cols.at[index], cols_low.at[index], cols_wide.at[index], out_grad_cols.at[index])
        )
    start = 0
    for size, goal in zip(sizes, (goal0, goal1, goal2, goal3), strict=True):
        for at in range(0, size, block):
            here = slice(start + at, start + at + block)
            moves.append(
                (total.at[here], rows_low.at[here], rows_wide.at[here], goal.at[at : at + block])
            )
        start += size
    loads = [
        pltpu.make_async_copy(source, low, load_sem.at[index])
        for index, (source, low, _, _) in enumerate(moves)
    ]
    stores = [
        pltpu.make_async_copy(wide, goal, store_sem.at[index])
        for index, (_, _, wide, goal) in enumerate(moves)
    ]
    for item in loads:
        item.start()
    through.start()
    for index, goal in enumerate((gain1, bias1, gain2, bias2)):
        goal[...] = lines[index : index + 1]
    out_bias[...] = lines[5:6]
    out_bias_again[...] = lines[5:6]
    fc1_bias[...] = lines[6:7]
    line = lines[4:5]
    lanes = line.shape[1] // 3
    pieces = []
    for h in range(heads):
        for part_index in range(3):
            at = part_index * lanes + h * HEAD
            pieces.append(line[:, at : at + HEAD])
    qkv_bias[...] = jnp.concatenate(pieces, axis=1)
    for load, store, (_, low, wide, _) in zip(loads, stores, moves, strict=True):
        load.wait()
        wide[...] = low[...].astype(F32)
        store.start()
    through.wait()
    onward.start()
    for item in stores:
        item.wait()
    onward.wait()


def widen(out_cols, grad_cols, total, lines, heads, units):
    width = total.shape[1]
    sizes = (width, units, 3 * heads * HEAD, heads * HEAD)
    count = out_cols.shape[0] + sum(sizes) // sizes[-1]
    hbm = pl.BlockSpec(memory_space=pl.ANY)
    vmem = pl.BlockSpec(memory_space=pltpu.VMEM)
    line = jax.ShapeDtypeStruct((1, width), F32)
    return pl.pallas_call(
        functools.partial(widen_kernel, heads, sizes),
        in_specs=[hbm, hbm, hbm, vmem],
        out_specs=[hbm] * 6 + [vmem] * 8,
        out_shape=[
            jax.ShapeDtypeStruct(out_cols.shape, BF16),
            jax.ShapeDtypeStruct(out_cols.shape, F32),
        ]
        + [jax.ShapeDtypeStruct((size, width), F32) for size in sizes]
        + [line] * 7
        + [jax.ShapeDtypeStruct((1, sizes[2]), F32)],
        scratch_shapes=[
            pltpu.VMEM(out_cols.shape, BF16),
            pltpu.VMEM(out_cols.shape, BF16),
            pltpu.VMEM(out_cols.shape, F32),
            pltpu.VMEM(total.shape, BF16),
            pltpu.VMEM(total.shape, F32),
            pltpu.SemaphoreType.DMA((2,)),
            pltpu.SemaphoreType.DMA((count,)),
            pltpu.SemaphoreType.DMA((count,)),
        ],
        compiler_params=pltpu.CompilerParams(vmem_limit_bytes=60 * 2**20),
    )(out_cols, grad_cols, total, lines)


def per_device(
    hidden_in,
    target,
    tissue,
    ln1_gain,
    ln1_bias,
    ln2_gain,
    ln2_bias,
    qkv_weight,
    qkv_bias,
    dense_weight,
    dense_bias,
    fc1_weight,
    fc1_bias,
    fc2_weight,
    fc2_bias,
):
    heads = dense_weight.shape[1] // HEAD
    units = fc1_weight.shape[-1]
    weights = (qkv_weight[0].T, dense_weight[0], fc1_weight[0], fc2_weight[0])
    vec = (ln1_gain, ln1_bias, ln2_gain, ln2_bias, dense_bias, fc2_bias, fc1_bias)
    out_cols, grad_cols, total, lines = train(hidden_in, target, tissue, weights, qkv_bias, vec)
    out_cols, grad_cols, fc1_grad, fc2_grad, qkv_grad, dense_grad, *lines = widen(
        out_cols, grad_cols, total, lines, heads, units
    )
    gain1, bias1, gain2, bias2, dense_bias_grad, fc2_bias_grad, fc1_bias_grad, qkv_bias_grad = lines
    return (
        out_cols.transpose(0, 2, 1)[None],
        grad_cols.transpose(0, 2, 1)[None],
        gain1,
        bias1,
        gain2,
        bias2,
        qkv_grad.T[None],
        qkv_bias_grad,
        dense_grad[None],
        dense_bias_grad,
        fc1_grad[None],
        fc1_bias_grad,
        fc2_grad[None],
        fc2_bias_grad,
    )


def solution(mesh):
    return jax.shard_map(
        per_device,
        mesh=mesh,
        in_specs=(
            P("dp", None, None),
            P("dp", None, None),
            P("dp"),
            P("section", None),
            P("section", None),
            P("section", None),
            P("section", None),
            P("section", None, "tensor"),
            P("section", "tensor"),
            P("section", "tensor", None),
            P("section", None),
            P("section", None, "tensor"),
            P("section", "tensor"),
            P("section", "tensor", None),
            P("section", None),
        ),
        out_specs=(
            P("section", "dp", None, "tensor"),
            P("section", "dp", None, "tensor"),
            P("section", None),
            P("section", None),
            P("section", None),
            P("section", None),
            P("section", None, "tensor"),
            P("section", "tensor"),
            P("section", "tensor", None),
            P("section", None),
            P("section", None, "tensor"),
            P("section", "tensor"),
            P("section", "tensor", None),
            P("section", None),
        ),
        check_vma=False,
    )
```

```python
import functools
import math

import jax
import jax.numpy as jnp
import numpy as np
from jax import lax
from jax.experimental import pallas as pl
from jax.experimental.pallas import tpu as pltpu
from jax.sharding import PartitionSpec as P

HEAD = 64
ROT = 16
TISSUES = 16
ROWS = 256
UNIT = 128
LANES = 128
EPS = 1e-05
MESH = pl.DeviceIdType.MESH
F32 = jnp.float32
BF16 = jnp.bfloat16


def dot_nn(a, b):
    return lax.dot_general(a, b, (((1,), (0,)), ((), ())), preferred_element_type=F32)


def dot_nt(a, b):
    return lax.dot_general(a, b, (((1,), (1,)), ((), ())), preferred_element_type=F32)


def dot_tn(a, b):
    return lax.dot_general(a, b, (((0,), (0,)), ((), ())), preferred_element_type=F32)


def rotary_tables(seq_len):
    half = ROT // 2
    inverse = 10000.0 ** (-2.0 * np.arange(half) / ROT)
    angles = np.arange(seq_len)[:, None] * inverse[None, :]
    cosines = np.ones((seq_len, HEAD))
    sines = np.zeros((seq_len, HEAD))
    cosines[:, :half] = np.cos(angles)
    cosines[:, half:ROT] = np.cos(angles)
    sines[:, :half] = -np.sin(angles)
    sines[:, half:ROT] = np.sin(angles)
    tables = np.stack([np.tile(item, (1, LANES // HEAD)) for item in (cosines, sines)])
    return tables.astype(np.float32)


def normalise(value):
    center = value - jnp.mean(value, axis=-1, keepdims=True)
    rstd = lax.rsqrt(jnp.mean(center * center, axis=-1, keepdims=True) + EPS)
    return center * rstd, rstd


def train_kernel(
    heads,
    x_in,
    target_in,
    tissue,
    tables,
    wq_in,
    wd_in,
    w1_in,
    w2_in,
    qkv_bias,
    vec_in,
    out_cols,
    grad_cols,
    grads,
    lines,
    small,
    wq,
    wd,
    w1,
    w2,
    vec,
    chain,
    qkv,
    ctx,
    act,
    gate,
    key_grad,
    value_grad,
    part,
    late_part,
    got,
    met,
    late_got,
    late_met,
    norm_rows,
    context_grad,
    query_back,
    total,
    half_got,
    first_got,
    second_got,
    more_got,
    line_got,
    tally,
    tally_got,
    probs,
    load_sem,
    give_sem,
    take_sem,
    hop_send,
    hop_recv,
    swap_send,
    swap_recv,
    sum_send,
    sum_recv,
    line_send,
    line_recv,
    tally_send,
    tally_recv,
    store_sem,
    free_sem,
):
    section = lax.axis_index("section")
    replica = lax.axis_index("dp")
    place = lax.axis_index("tensor")
    copies = lax.axis_size("dp")
    bits = copies.bit_length() - 1
    _, chunks, rows, width = chain.shape
    unit = part.shape[1]
    halves = rows // unit
    units = chunks * halves
    half_width = late_met.shape[-1]
    lanes = wd.shape[1]
    valid = heads * HEAD
    columns = out_cols.shape[1]
    padded = -(-columns // LANES) * LANES
    inner = jnp.logical_and(place > 0, place < 3)
    outer = jnp.logical_not(inner)
    beside = place + 1 - 2 * lax.rem(place, 2)
    across = 3 - place

    def flipped(bit):
        return replica + (1 << bit) * (1 - 2 * lax.rem(replica // (1 << bit), 2))

    twin = {"section": 1 - section}
    mates = [{"dp": flipped(bit)} for bit in range(bits)]
    near = {"tensor": beside}
    far = {"tensor": across}
    friends = [twin, near, far] + mates

    def send(source, goal, sems, target):
        return pltpu.make_async_remote_copy(
            src_ref=source,
            dst_ref=goal,
            send_sem=sems[0],
            recv_sem=sems[1],
            device_id=target,
            device_id_type=MESH,
        )

    barrier = pltpu.get_barrier_semaphore()
    for friend in friends:
        pl.semaphore_signal(barrier, inc=1, device_id=friend, device_id_type=MESH)

    input_load = pltpu.make_async_copy(x_in.at[section], chain.at[0], load_sem.at[0])
    input_load.start()
    pairs = []
    for part_index in range(3):
        for h in range(heads):
            source = slice((3 * h + part_index) * HEAD, (3 * h + part_index + 1) * HEAD)
            goal = slice(part_index * lanes + h * HEAD, part_index * lanes + (h + 1) * HEAD)
            pairs.append((wq_in.at[source], wq.at[section, goal]))
    pairs += [(w1_in, w1.at[section]), (wd_in, wd.at[section, :valid]), (w2_in, w2.at[section])]
    loads = [
        pltpu.make_async_copy(source, goal, load_sem.at[4 + index])
        for index, (source, goal) in enumerate(pairs)
    ]
    for item in loads:
        item.start()
    target_load = pltpu.make_async_copy(target_in.at[section], chain.at[2], load_sem.at[3])
    target_load.start()

    for index, item in enumerate(vec_in):
        vec[section, index : index + 1] = item[...].astype(F32)
    vec[section, 4:5] = vec_in[4][...].astype(F32) + vec_in[5][...].astype(F32)
    line = qkv_bias[...].astype(F32)
    gap = [jnp.zeros((1, lanes - valid), F32)] if lanes > valid else []
    packed = []
    for part_index in range(3):
        for h in range(heads):
            packed.append(line[:, (3 * h + part_index) * HEAD : (3 * h + part_index + 1) * HEAD])
        packed += gap
    vec[section, 5:6] = jnp.concatenate(packed, axis=1)
    vec[section, 7:8] = jnp.zeros((1, width), F32)
    for layer in range(2):
        wd[layer, valid:] = jnp.zeros((lanes - valid, width), BF16)
        for part_index in range(3):
            pad = slice(part_index * lanes + valid, (part_index + 1) * lanes)
            wq[layer, pad] = jnp.zeros((lanes - valid, width), BF16)
    pl.semaphore_wait(barrier, len(friends))
    gifts = [
        send(source, goal, (give_sem.at[index], take_sem.at[index]), twin)
        for index, (source, goal) in enumerate(
            [(vec.at[section], vec.at[section])] + pairs
        )
    ]
    projection = 3 * heads
    for item in gifts[: 2 + projection]:
        item.start()

    small[...] = jnp.zeros_like(small)
    tissue_lane = lax.broadcasted_iota(jnp.int32, (8, LANES), 1)
    marks = [(tissue_lane == tissue[index]).astype(F32) for index in range(tissue.shape[0])]
    tally[...] = functools.reduce(lambda a, b: a + b, marks)

    def tally_step(bit):
        return send(
            tally, tally_got.at[bit], (tally_send.at[bit], tally_recv.at[bit]), mates[bit]
        )

    if bits:
        tally_step(0).start()

    def count_on(bit):
        step = tally_step(bit)
        step.wait()
        tally[...] += tally_got[bit]
        if bit + 1 < bits:
            tally_step(bit + 1).start()

    lane = lax.broadcasted_iota(jnp.int32, (1, lanes), 1) // HEAD
    head_masks = [lane == h for h in range(heads)]
    factor = HEAD ** (-0.5)

    left_half = lax.rem(lax.broadcasted_iota(jnp.int32, (1, lanes), 1), HEAD) < ROT // 2

    def wide(table, start):
        piece = tables[table, pl.ds(start, rows), :]
        return jnp.concatenate([piece] * (lanes // LANES), axis=1)

    def turned(value):
        ahead = pltpu.roll(value, lanes - ROT // 2, 1)
        behind = pltpu.roll(value, ROT // 2, 1)
        return jnp.where(left_half, ahead, behind)

    def turn(value, start):
        return value * wide(0, start) + turned(value) * wide(1, start)

    def turn_back(value, start):
        return value * wide(0, start) - turned(value) * wide(1, start)

    def only(mask, value):
        return jnp.where(mask, value, jnp.zeros_like(value))

    def put(goal, slot, value):
        for half in range(halves):
            piece = value[half * unit : (half + 1) * unit]
            goal[slot * halves + half] = piece.astype(BF16)

    def forward_chunk(layer, c):
        start = c * rows
        here = slice(start, start + rows)
        if c == 0:
            need(0, 1 + projection, layer)
            for item in gifts[2 + projection :]:
                pl.when(layer == 0)(item.start)
        spread, _ = normalise(chain[layer, c].astype(F32))
        first = (spread * vec[layer, 0:1] + vec[layer, 1:2]).astype(BF16)
        second = (spread * vec[layer, 2:3] + vec[layer, 3:4]).astype(BF16)
        projected = dot_nt(first, wq[layer]) + vec[layer, 5:6]
        query = turn(projected[:, :lanes], start).astype(BF16)
        qkv[layer, here, :lanes] = query
        qkv[layer, here, lanes : 2 * lanes] = turn(projected[:, lanes : 2 * lanes], start).astype(
            BF16
        )
        qkv[layer, here, 2 * lanes :] = projected[:, 2 * lanes :].astype(BF16)
        if c == 0:
            need(1 + projection, 2 + projection, layer)
        pre = dot_nn(second, w1[layer]) + vec[layer, 6:7]
        below = 0.5 * (1.0 + lax.erf(pre * (0.5**0.5)))
        active = (pre * below).astype(BF16)
        act[layer, here, :] = active
        slope = below + pre * (jnp.exp(-0.5 * pre * pre) * ((2.0 * np.pi) ** -0.5))
        gate[layer, here, :] = slope.astype(BF16)
        diagonal = lax.broadcasted_iota(jnp.int32, (rows, rows), 0) >= lax.broadcasted_iota(
            jnp.int32, (rows, rows), 1
        )
        context = jnp.zeros((rows, lanes), F32)
        for h in range(heads):
            asked = only(head_masks[h], query) * jnp.asarray(factor, BF16)
            near = dot_nt(asked, qkv[layer, here, lanes : 2 * lanes])
            near = jnp.where(diagonal, near, -1e30)
            highest = jnp.max(near, axis=-1, keepdims=True)
            if c > 0:
                far = dot_nt(asked, qkv[layer, :start, lanes : 2 * lanes])
                highest = jnp.maximum(highest, jnp.max(far, axis=-1, keepdims=True))
                far = jnp.exp(far - highest)
            near = jnp.exp(near - highest)
            total = jnp.sum(near, axis=-1, keepdims=True)
            if c > 0:
                total = total + jnp.sum(far, axis=-1, keepdims=True)
            inverse = 1.0 / total
            near = (near * inverse).astype(BF16)
            probs[c][layer, h, :, start:] = near
            mixed = dot_nn(near, qkv[layer, here, 2 * lanes :])
            if c > 0:
                far = (far * inverse).astype(BF16)
                probs[c][layer, h, :, :start] = far
                mixed = mixed + dot_nn(far, qkv[layer, :start, 2 * lanes :])
            context = jnp.where(head_masks[h], mixed, context)
        context = context.astype(BF16)
        ctx[layer, here, :] = context
        if c == 0:
            need(2 + projection, 4 + projection, layer)
        result = (dot_nn(context, wd[layer]) + dot_nn(active, w2[layer])).astype(BF16)
        for index, goal in enumerate((part, late_part)):
            pl.when(layer == index)(functools.partial(put, goal, c, result))
        return second

    def feed_back(c, second):
        here = slice(c * rows, (c + 1) * rows)
        cotangent = chain[2, c]
        pre_grad = (dot_nt(cotangent, w2[1]) * gate[1, here, :].astype(F32)).astype(BF16)
        gate[1, here, :] = pre_grad
        if c < chunks - 1:
            norm_rows[...] = second
            add_forward_grads(1, c, c == 0)

    def rows_of(c):
        return pl.ds(pl.multiple_of(c * rows, rows), rows)

    def backward_front(layer, c):
        here = rows_of(c)
        cotangent = chain[3 - layer, c]
        context_grad[...] = dot_nt(cotangent, wd[layer]).astype(BF16)

        @pl.when(layer == 0)
        def _():
            back = dot_nt(cotangent, w2[0]) * gate[0, here, :].astype(F32)
            gate[0, here, :] = back.astype(BF16)

    def backward_attention(layer, c):
        start = c * rows
        stop = start + rows
        here = slice(start, stop)
        own = context_grad[...]
        query = qkv[layer, here, :lanes]
        weighed = own.astype(F32) * ctx[layer, here, :].astype(F32)
        query_grad = jnp.zeros((rows, lanes), F32)
        key_sum = None
        value_sum = None
        for h in range(heads):
            mask = head_masks[h]
            own_grad = only(mask, own)
            asked = only(mask, query) * jnp.asarray(factor, BF16)
            row_dot = jnp.sum(only(mask, weighed), axis=-1, keepdims=True)
            prob = probs[c][layer, h]
            prob_grad = dot_nt(own_grad, qkv[layer, :stop, 2 * lanes :])
            score_grad = (prob.astype(F32) * (prob_grad - row_dot)).astype(BF16)
            query_grad = jnp.where(
                mask, dot_nn(score_grad, qkv[layer, :stop, lanes : 2 * lanes]), query_grad
            )
            key_part = dot_tn(score_grad, asked)
            value_part = dot_tn(prob, own_grad)
            key_sum = key_part if key_sum is None else key_sum + key_part
            value_sum = value_part if value_sum is None else value_sum + value_part
        query_back[...] = query_grad * factor
        if c == chunks - 1:
            key_grad[:stop] = key_sum
            value_grad[:stop] = value_sum
        else:
            key_grad[:stop] += key_sum
            value_grad[:stop] += value_sum

    def backward_rest(layer, c):
        here = rows_of(c)
        start = pl.multiple_of(c * rows, rows)
        pre_grad = gate[layer, here]
        second_back = dot_nt(pre_grad, w1[layer])
        qkv[layer, here, :lanes] = turn_back(query_back[...], start).astype(BF16)
        qkv[layer, here, lanes : 2 * lanes] = turn_back(key_grad[here], start).astype(BF16)
        qkv[layer, here, 2 * lanes :] = value_grad[here].astype(BF16)
        projected_grad = qkv[layer, here, :]
        first_back = dot_nn(projected_grad, wq[layer])
        spread, rstd = normalise(chain[layer, c].astype(F32))
        back = first_back * vec[layer, 0:1] + second_back * vec[layer, 2:3]
        middle = jnp.mean(back, axis=-1, keepdims=True)
        tilt = jnp.mean(back * spread, axis=-1, keepdims=True)
        put(part, chunks - 1 - c, rstd * (back - middle - spread * tilt))
        first = (spread * vec[layer, 0:1] + vec[layer, 1:2]).astype(BF16)
        norm_rows[...] = (spread * vec[layer, 2:3] + vec[layer, 3:4]).astype(BF16)
        sums = (
            first_back * spread,
            first_back,
            second_back * spread,
            second_back,
            projected_grad.astype(F32),
            chain[3 - layer, c].astype(F32),
            pre_grad.astype(F32),
        )
        for index, item in enumerate(sums):
            small[layer, index : index + 1] += jnp.sum(item, axis=0, keepdims=True)
        return first

    def add_piece_grads(layer, start, piece, first_turn):
        goal = slice(start, start + piece.shape[0])
        before = jnp.where(first_turn, 0.0, total[layer, goal].astype(F32))
        total[layer, goal] = (piece + before).astype(BF16)

    def add_forward_grads(layer, c, first_turn, parts=("fc1", "fc2")):
        here = rows_of(c)
        cotangent = chain.at[3 - layer, c]

        def add_block(index, carry):
            block = pl.ds(pl.multiple_of(index * lanes, lanes), lanes)
            goal = pl.ds(pl.multiple_of(width + index * lanes, lanes), lanes)
            pieces = []
            if "fc1" in parts:
                pieces.append((block, dot_tn(norm_rows[:, block], gate[layer, here])))
            if "fc2" in parts:
                pieces.append((goal, dot_tn(act[layer, here, block], cotangent[...])))
            for at, piece in pieces:
                before = jnp.where(first_turn, 0.0, total[layer, at].astype(F32))
                total[layer, at] = (piece + before).astype(BF16)
            return carry

        lax.fori_loop(0, width // lanes, add_block, 0)

    def add_weight_grads(layer, c, first):
        base = width + act.shape[-1]
        here = rows_of(c)
        first_turn = c == chunks - 1
        for part_index in range(3):
            at = part_index * lanes
            piece = dot_tn(qkv[layer, here, at : at + lanes], first)
            for h in range(heads):
                row = base + (3 * h + part_index) * HEAD
                add_piece_grads(layer, row, piece[h * HEAD : (h + 1) * HEAD], first_turn)
        piece = dot_tn(ctx[layer, here], chain[3 - layer, c])[:valid]
        add_piece_grads(layer, base + 3 * valid, piece, first_turn)

    cut = width + act.shape[-1]
    jobs = ((width, cut - width), (0, width), (cut, total.shape[1] - cut))
    folds = min(bits, 2)
    sum_steps = 2 + 2 * folds + (bits - folds)

    def spans(job, group):
        order = ((0, 1), (1, 0))[group][:folds]
        base, size = jobs[job]
        size = size // 4
        start = base + section * size * 2 + group * size
        steps = []
        for bit in order:
            size = size // 2
            upper = lax.rem(replica // (1 << bit), 2)
            steps.append((bit, start + upper * size, start + (1 - upper) * size, size))
            start = start + upper * size
        return steps, start, size

    groups = [[spans(job, group) for group in range(2)] for job in range(len(jobs))]

    def sums_of(layer, start, size):
        return total.at[layer, pl.ds(pl.multiple_of(start, 16), size)]

    def gathered(layer, job, group, start, size):
        base, job_rows = jobs[job]
        start = start - base - section * (job_rows // 2) - group * (job_rows // 4) + base // 4
        return (act, gate)[group].at[layer, pl.ds(pl.multiple_of(start, 16), size)]

    def sum_sems(layer, job, step, group):
        return sum_send.at[layer, job, step, group], sum_recv.at[layer, job, step, group]

    def landing_of(buffer, job, parts):
        base, job_rows = jobs[job]
        return buffer.at[base // parts : (base + job_rows) // parts]

    def sum_copies(layer, job, step):
        base, job_rows = jobs[job]
        if step == 0:
            source = sums_of(layer, base + (1 - section) * (job_rows // 2), job_rows // 2)
            goal = landing_of(half_got.at[layer], job, 2)
            return [send(source, goal, sum_sems(layer, job, 0, 0), twin)]
        copies_now = []
        for group, (steps, start, size) in enumerate(groups[job]):
            sems = sum_sems(layer, job, step, group)
            if step <= folds:
                bit, _, gone, size = steps[step - 1]
                goal = landing_of((first_got, second_got)[step - 1].at[group], job, 4 << step)
                copies_now.append(send(sums_of(layer, gone, size), goal, sems, mates[bit]))
            elif step <= bits:
                goal = landing_of(more_got.at[layer, step - 1 - folds, group], job, 16)
                source = gathered(layer, job, group, start, size)
                copies_now.append(send(source, goal, sems, mates[step - 1]))
            else:
                bit, start, _, size = steps[bits - step]
                piece = gathered(layer, job, group, start, size)
                copies_now.append(send(piece, piece, sems, mates[bit]))
        return copies_now

    def last_copies(layer, job):
        base, job_rows = jobs[job]
        size = job_rows // 4
        pieces = []
        for group in range(2):
            first_row = base + section * (job_rows // 2) + group * size
            piece = gathered(layer, job, group, first_row, size)
            goal = grads.at[pl.ds(pl.multiple_of(first_row, 16), size)]
            sems = sum_sems(layer, job, sum_steps - 1, group)
            other_row = base + (1 - section) * (job_rows // 2) + group * size
            other = grads.at[pl.ds(pl.multiple_of(other_row, 16), size)]
            pieces.append(
                (
                    send(piece, goal, sems, twin),
                    send(piece, other, sems, twin),
                    pltpu.make_async_copy(piece, goal, store_sem.at[job, group]),
                )
            )
        return pieces

    def sum_start(layer, job, step):
        if step < sum_steps - 1:
            if layer == 0 and 1 <= step <= folds:
                for group in range(2):
                    pl.semaphore_wait(free_sem.at[job, step - 1, group], 1)
            for item in sum_copies(layer, job, step):
                item.start()
            return
        for give, _, keep in last_copies(layer, job):
            pl.when(section != layer)(give.start)
            pl.when(section == layer)(keep.start)

    def add_rows(goal, base, source):
        size = source.shape[0]
        piece = math.gcd(size, 192)

        def add_piece(index, carry):
            here = pl.ds(pl.multiple_of(index * piece, 16), piece)
            goal[here] = (base[here].astype(F32) + source[here].astype(F32)).astype(BF16)
            return carry

        lax.fori_loop(0, size // piece, add_piece, 0)

    def sum_end(layer, job, step):
        if step == sum_steps - 1:
            for give, take, keep in last_copies(layer, job):
                pl.when(section != layer)(give.wait_send)
                pl.when(section == layer)(take.wait_recv)
                pl.when(section == layer)(keep.wait)
            return
        for item in sum_copies(layer, job, step):
            item.wait()
        if step == 0:
            base, job_rows = jobs[job]
            kept = sums_of(layer, base + section * (job_rows // 2), job_rows // 2)
            add_rows(kept, kept, landing_of(half_got.at[layer], job, 2))
            return
        if step > bits:
            return
        for group, (steps, start, size) in enumerate(groups[job]):
            goal = gathered(layer, job, group, start, size)
            if step < folds:
                base = sums_of(layer, steps[step - 1][1], steps[step - 1][3])
                add_rows(base, base, landing_of(first_got.at[group], job, 8))
            elif step == folds:
                add_rows(goal, sums_of(layer, start, size), landing_of(second_got.at[group], job, 16))
            else:
                landed = landing_of(more_got.at[layer, step - 1 - folds, group], job, 16)
                add_rows(goal, goal, landed)
            if layer == 1 and step <= folds:
                mate = mates[steps[step - 1][0]]
                pl.semaphore_signal(
                    free_sem.at[job, step - 1, group],
                    inc=1,
                    device_id=mate,
                    device_id_type=MESH,
                )

    steps_done = {(layer, job): 0 for layer in range(2) for job in range(len(jobs))}

    def move_sum(layer, job, step=None):
        step = steps_done[layer, job] if step is None else step
        if step < sum_steps:
            sum_end(layer, job, step)
            if step + 1 < sum_steps:
                sum_start(layer, job, step + 1)
            steps_done[layer, job] = max(steps_done[layer, job], step + 1)

    line_friends = [twin] + mates + [near, far]

    def line_copy(step):
        sems = (line_send.at[step], line_recv.at[step])
        return send(small, line_got.at[step], sems, line_friends[step])

    def line_end(step):
        line_copy(step).wait()
        if step <= bits:
            small[...] += line_got[step]
        else:
            small[:, 0:4] += line_got[step, :, 0:4]

    low_side = place < 2
    own_half = pl.multiple_of(jnp.where(low_side, 0, half_width), LANES)
    other_half = pl.multiple_of(jnp.where(low_side, half_width, 0), LANES)
    window = place * columns // LANES * LANES
    window = pl.multiple_of(window, LANES)
    end_window = pl.multiple_of(jnp.where(low_side, 0, width - padded), LANES)

    sent_width = width - LANES
    sent_lanes = pl.ds(pl.multiple_of(jnp.where(low_side, LANES, 0), LANES), sent_width)

    def spot(kind, u):
        chunk = u // halves if kind < 2 else chunks - 1 - u // halves
        return chunk, pl.ds(pl.multiple_of(lax.rem(u, halves) * unit, unit), unit)

    def buffers(kind, u):
        if kind == 1:
            return late_part.at[u], late_got.at[u], late_met.at[u]
        return part.at[u], got.at[u], met.at[u] if kind != 3 else met.at[u, :, :half_width]

    def hop_sems(kind, stage, u):
        return hop_send.at[int(kind == 1), stage, u], hop_recv.at[int(kind == 1), stage, u]

    def first_hop(kind, u):
        own, landing, _ = buffers(kind, u)
        if kind in (1, 3):
            own, landing = own.at[:, sent_lanes], landing.at[:, :sent_width]
        return send(own, landing, hop_sems(kind, 0, u), near)

    def second_hop(kind, u):
        own, _, landing = buffers(kind, u)
        if kind in (1, 3):
            own = own.at[:, pl.ds(other_half, half_width)]
        return send(own, landing, hop_sems(kind, 1, u), far)

    def third_hop(kind, u):
        own, _, landing = buffers(kind, u)
        if kind in (1, 3):
            own, landing = own.at[:, pl.ds(end_window, padded)], landing.at[:, :padded]
        else:
            chunk, here = spot(kind, u)
            own = landing = chain.at[kind + 1, chunk, here]
        return send(own, landing, hop_sems(kind, 2, u), near)

    def by_rows(count, work, step=32):
        def turn_rows(index, carry):
            work(pl.ds(pl.multiple_of(index * step, step), step))
            return carry

        lax.fori_loop(0, count // step, turn_rows, 0)

    def launch(kind, c, parts=(0, 1)):
        @pl.when(outer)
        def _():
            for half in parts:
                first_hop(kind, c * halves + half).start()

    def meet(kind, u):
        @pl.when(inner)
        def _():
            first_hop(kind, u).wait_recv()
            own, landed, _ = buffers(kind, u)
            if kind in (1, 3):
                own, landed = own.at[:, sent_lanes], landed.at[:, :sent_width]

            def add(here):
                own[here] = (own[here].astype(F32) + landed[here].astype(F32)).astype(BF16)

            by_rows(unit, add)
            second_hop(kind, u).start()

    def settle(kind, u):
        chunk, here = spot(kind, u)

        @pl.when(inner)
        def _():
            second_hop(kind, u).wait_recv()
            own, _, landed = buffers(kind, u)
            if kind in (1, 3):
                lanes_here = pl.ds(own_half, half_width)
                goal = own.at[:, lanes_here]
                source = goal
                base = chain.at[kind, chunk, here, lanes_here]
            else:
                lanes_here = slice(None)
                goal = chain.at[kind + 1, chunk, here]
                source = own
                base = chain.at[kind, chunk, here]

            def add(at):
                value = source[at].astype(F32) + landed[at].astype(F32) + base[at].astype(F32)
                if kind < 2:
                    value = value + vec[kind, 4:5, lanes_here]
                goal[at] = value.astype(BF16)

            by_rows(unit, add)
            if kind > 1:
                third_hop((0, 2)[kind - 2], u).wait_send()
            third_hop(kind, u).start()

    def arrive(kind, c):
        @pl.when(outer)
        def _():
            for half in range(halves):
                third_hop(kind, c * halves + half).wait_recv()

    def release(kind, c):
        for half in range(halves):
            u = c * halves + half
            pl.when(outer)(first_hop(kind, u).wait_send)
            pl.when(inner)(second_hop(kind, u).wait_send)

    def let_go(kind):
        for u in range(units):
            pl.when(inner)(third_hop(kind, u).wait_send)

    def serve(kind, meets, settles):
        for index in range(max(len(meets), len(settles))):
            if index < len(meets):
                meet(kind, meets[index])
            if index < len(settles):
                settle(kind, settles[index])

    def need(first, last, layer):
        @pl.when(section == layer)
        def _():
            for index in range(max(first, 1), last):
                loads[index - 1].wait()

        @pl.when(section != layer)
        def _():
            for index in range(first, last):
                gifts[index].wait_recv()

    input_load.wait()

    first_turns = (((), ()), ((), ()), ((0,), ()), ((1, 2), (0, 1)))
    second_turns = (
        (((3,), (2,)), ((4,), (3,))),
        (((5,), (4,)), ((6,), (5,))),
        (((7,), (6,)), ((), (7,))),
        (((), ()), ((), ())),
    )

    def weigh(c):
        chain[2, c] = (vec[0, 7:8] * chain[2, c].astype(F32)).astype(BF16)

    def find_share():
        own_mark = jnp.where(section == 0, marks[0], marks[1])[0:1]
        own_count = jnp.sum(own_mark * tally[0:1], axis=-1, keepdims=True)
        share = (tissue.shape[0] * copies / TISSUES) / own_count
        gifts[0].wait_send()
        vec[0, 7:8] = jnp.broadcast_to(share, (1, width))
        target_load.wait()

    def forward_layer(layer, carry):
        for c in range(chunks):
            pl.when(layer == 1)(functools.partial(arrive, 0, c))
            second = forward_chunk(layer, c)

            @pl.when(layer == 0)
            def _():
                launch(0, c)
                serve(0, *first_turns[c])
                for bit in range(bits):
                    if min(bit, chunks - 1) == c:
                        count_on(bit)

            @pl.when(layer == 1)
            def _():
                serve(0, *second_turns[c][0])
                if c in (1, 2):
                    launch(1, c - 1)
                if c == 2:
                    launch(1, 2, (0,))
                if c == 0:
                    find_share()
                weigh(c)
                feed_back(c, second)
                serve(0, *second_turns[c][1])

        return carry

    lax.fori_loop(0, 2, forward_layer, 0)

    meets = {1: (1, 1, 3, 3, 5), 2: (4, 5, 6, 7, 8, 9, 10, 11), 3: (13, 14, 14)}
    settles = {1: (3, 3, 5, 5, 7), 2: (6, 7, 8, 9, 10, 11, 12, 12), 3: (14,)}
    backward_points = [[] for _ in range(8 * 2)]
    for kind in (1, 2, 3):
        order = [(2 * u, meet, kind, u, meets[kind][u]) for u in range(len(meets[kind]))]
        order += [(2 * u + 3, settle, kind, u, settles[kind][u]) for u in range(len(settles[kind]))]
        for _, work, kind_now, u, point in sorted(order, key=lambda item: item[0]):
            backward_points[point].append((work, kind_now, u))

    def serve_point(point):
        for work, kind, u in backward_points[point]:
            work(kind, u)

    sum_moves = {
        5: ((1, 0, 0), (1, 1, 0)),
        8: ((1, 2, 0),),
        9: ((1, 0, 2), (1, 1, 2)),
        10: ((1, 2, 1),),
        12: ((1, 2, 2), (1, 0, 3), (1, 1, 3)),
        13: ((1, 2, 3),),
        14: ((0, 0, 0),),
    }

    def serve_at(step, point):
        for index in range(2 * chunks):
            number = index * 2 + point

            @pl.when(step == index)
            def _():
                serve_point(number)
                for moved in sum_moves.get(number, ()):
                    move_sum(*moved)

    def backward_step(step, carry):
        turn_index = step // chunks
        at = lax.rem(step, chunks)
        layer = 1 - turn_index
        c = chunks - 1 - at
        last_step = step == 2 * chunks - 1

        @pl.when(layer == 0)
        def _():

            @pl.when(at == 0)
            def _():
                move_sum(1, 0, 1)
                move_sum(1, 1, 1)

            arrive(2, at)
            release(2, at)

        pl.when(layer == 1)(functools.partial(release, 0, at))

        @pl.when(last_step)
        def _():
            add_forward_grads(0, 0, False, ("fc2",))
            sum_start(0, 0, 0)

        backward_front(layer, c)

        @pl.when(last_step)
        def _():
            spread, _ = normalise(chain[0, 0].astype(F32))
            norm_rows[...] = (spread * vec[0, 2:3] + vec[0, 3:4]).astype(BF16)
            add_forward_grads(0, 0, False, ("fc1",))
            sum_start(0, 1, 0)

        for index in range(chunks):
            pl.when(c == index)(functools.partial(backward_attention, layer, index))
        serve_at(step, 0)
        first = backward_rest(layer, c)
        for index in range(2):
            pl.when(turn_index == index)(functools.partial(launch, 2 + index, at))
        pl.when(last_step)(functools.partial(move_sum, 0, 1))
        add_weight_grads(layer, c, first)

        @pl.when(jnp.logical_or(step == 0, jnp.logical_and(layer == 0, c > 0)))
        def _():
            add_forward_grads(layer, c, step == chunks)

        @pl.when(step == 0)
        def _():
            sum_start(1, 0, 0)
            sum_start(1, 1, 0)

        @pl.when(jnp.logical_and(layer == 0, at > 1))
        def _():
            pl.when(at == 2)(functools.partial(launch, 1, 2, (1,)))
            pl.when(at == 3)(functools.partial(launch, 1, 3))

        pl.when(step == chunks - 1)(functools.partial(sum_start, 1, 2, 0))
        pl.when(last_step)(functools.partial(sum_start, 0, 2, 0))
        serve_at(step, 1)
        return carry

    lax.fori_loop(0, 2 * chunks, backward_step, 0)

    shift = lax.rem(place * columns, LANES)

    def staged(index, layer):
        return probs[-1].at[layer, index, :columns]

    def stage(index, layer, row, value):
        turned_value = value.astype(F32).T
        low = turned_value[:columns]
        high = turned_value[LANES // 2 : LANES // 2 + columns]
        goal = pl.ds(pl.multiple_of(row, unit), unit)
        staged(index, layer)[:, goal] = jnp.where(shift == 0, low, high).astype(BF16)

    def stage_whole(index, layer, kind):
        def stage_unit(u, carry):
            rows_here = pl.ds(pl.multiple_of(lax.rem(u, halves) * unit, unit), unit)
            source = chain.at[kind + 1, u // halves, rows_here, pl.ds(window, padded)]
            stage(index, layer, u * unit, source[...])
            return carry

        lax.fori_loop(0, units, stage_unit, 0)

    def stage_own(index, layer, kind):
        for c in range(chunks):
            arrive(kind, c)
            release(kind, c)
        let_go(kind)
        tile = lax.broadcasted_iota(jnp.int32, (1, padded), 1) // LANES
        unsent = tile == jnp.where(low_side, 0, padded // LANES - 1)
        store, landing = (late_part, late_met) if kind == 1 else (part, met)

        def stage_unit(u, carry):
            chunk = u // halves if kind == 1 else chunks - 1 - u // halves
            row = chunk * rows + lax.rem(u, halves) * unit

            @pl.when(outer)
            def _():
                mine = store[u, :, pl.ds(end_window, padded)]
                value = landing[u, :, :padded].astype(F32) + only(unsent, mine.astype(F32))
                stage(index, layer, row, value)

            @pl.when(inner)
            def _():
                stage(index, layer, row, store[u, :, pl.ds(window, padded)])

            return carry

        lax.fori_loop(0, units, stage_unit, 0)

    def swap_columns(index, goal):
        sems = (swap_send.at[index], swap_recv.at[index])
        return [
            send(staged(index, 1 - section), goal.at[section], sems, twin),
            pltpu.make_async_copy(staged(index, section), goal.at[section], load_sem.at[1 + index]),
        ]

    def line_next(step):
        if step < len(line_friends):
            line_end(step)
            if step + 1 < len(line_friends):
                line_copy(step + 1).start()

    line_copy(0).start()
    for item in gifts[1:]:
        item.wait_send()
    meet(3, 3)
    settle(3, 1)
    meet(3, 4)
    move_sum(0, 2)
    settle(3, 2)
    meet(3, 5)
    settle(3, 3)
    line_next(0)
    stage_whole(0, 0, 0)
    meet(1, 5)
    settle(3, 4)
    move_sum(0, 0)
    settle(3, 5)
    meet(3, 6)
    move_sum(0, 1)
    stage_whole(1, 1, 2)
    settle(1, 5)
    for job in range(2):
        move_sum(1, job)
    move_sum(0, 2)
    line_next(1)
    meet(3, 7)
    settle(3, 6)
    move_sum(0, 0)
    meet(1, 6)
    settle(3, 7)
    move_sum(0, 1)
    move_sum(0, 2)
    line_next(2)
    meet(1, 7)
    move_sum(0, 0)
    settle(1, 6)
    move_sum(0, 1)
    settle(1, 7)
    move_sum(0, 2)
    line_next(3)
    move_sum(1, 2)
    stage_own(1, 0, 3)
    moves = swap_columns(1, grad_cols)
    for item in moves:
        item.start()
    stage_own(0, 1, 1)
    late_moves = swap_columns(0, out_cols)
    for item in late_moves:
        item.start()
    move_sum(0, 0)
    move_sum(0, 1)
    for step in range(4, len(line_friends)):
        line_next(step)
    lines_store = pltpu.make_async_copy(small.at[section], lines, load_sem.at[0])
    lines_store.start()
    for _ in range(sum_steps):
        for job in range(len(jobs)):
            move_sum(0, job)
            move_sum(1, job)
    for item in moves + late_moves:
        item.wait()
    lines_store.wait()


def train(x, target, tissue, weights, qkv_bias, vec):
    wq, wd, w1, w2 = weights
    count, seq_len, width = x.shape
    rows = min(ROWS, seq_len)
    chunks = seq_len // rows
    unit = min(UNIT, rows)
    pieces = seq_len // unit
    valid = wd.shape[0]
    heads = valid // HEAD
    lanes = -(-valid // LANES) * LANES
    units = w1.shape[1]
    columns = width // lax.axis_size("tensor")
    bits = lax.axis_size("dp").bit_length() - 1
    tables = jnp.asarray(rotary_tables(seq_len))
    total_rows = 3 * valid + width + units + valid
    hbm = pl.BlockSpec(memory_space=pl.ANY)
    vmem = pl.BlockSpec(memory_space=pltpu.VMEM)
    smem = pl.BlockSpec(memory_space=pltpu.SMEM)
    scratch = [
        pltpu.VMEM((2, 8, width), F32),
        pltpu.VMEM((2, 3 * lanes, width), BF16),
        pltpu.VMEM((2, lanes, width), BF16),
        pltpu.VMEM((2,) + w1.shape, BF16),
        pltpu.VMEM((2,) + w2.shape, BF16),
        pltpu.VMEM((2, 8, width), F32),
        pltpu.VMEM((4, chunks, rows, width), BF16),
        pltpu.VMEM((2, seq_len, 3 * lanes), BF16),
        pltpu.VMEM((2, seq_len, lanes), BF16),
        pltpu.VMEM((2, seq_len, units), BF16),
        pltpu.VMEM((2, seq_len, units), BF16),
        pltpu.VMEM((seq_len, lanes), F32),
        pltpu.VMEM((seq_len, lanes), F32),
        pltpu.VMEM((pieces, unit, width), BF16),
        pltpu.VMEM((pieces, unit, width), BF16),
        pltpu.VMEM((pieces, unit, width), BF16),
        pltpu.VMEM((pieces, unit, width), BF16),
        pltpu.VMEM((pieces, unit, width - LANES), BF16),
        pltpu.VMEM((pieces, unit, width // 2), BF16),
        pltpu.VMEM((rows, width), BF16),
        pltpu.VMEM((rows, lanes), BF16),
        pltpu.VMEM((rows, lanes), F32),
        pltpu.VMEM((2, total_rows, width), BF16),
        pltpu.VMEM((2, total_rows // 2, width), BF16),
        pltpu.VMEM((2, total_rows // 8, width), BF16),
        pltpu.VMEM((2, total_rows // 16, width), BF16),
        pltpu.VMEM((2, max(bits - 2, 1), 2, total_rows // 16 if bits > 2 else 16, width), BF16),
        pltpu.VMEM((3 + bits, 2, 8, width), F32),
        pltpu.VMEM((8, LANES), F32),
        pltpu.VMEM((max(bits, 1), 8, LANES), F32),
    ]
    probs = [pltpu.VMEM((2, heads, rows, (c + 1) * rows), BF16) for c in range(chunks)]
    semaphores = [
        pltpu.SemaphoreType.DMA((4 + 3 * heads + 3,)),
        pltpu.SemaphoreType.DMA((4 + 3 * heads,)),
        pltpu.SemaphoreType.DMA((4 + 3 * heads,)),
        pltpu.SemaphoreType.DMA((2, 3, pieces)),
        pltpu.SemaphoreType.DMA((2, 3, pieces)),
        pltpu.SemaphoreType.DMA((2,)),
        pltpu.SemaphoreType.DMA((2,)),
        pltpu.SemaphoreType.DMA((2, 3, bits + 4, 2)),
        pltpu.SemaphoreType.DMA((2, 3, bits + 4, 2)),
        pltpu.SemaphoreType.DMA((3 + bits,)),
        pltpu.SemaphoreType.DMA((3 + bits,)),
        pltpu.SemaphoreType.DMA((max(bits, 1),)),
        pltpu.SemaphoreType.DMA((max(bits, 1),)),
        pltpu.SemaphoreType.DMA((3, 2)),
        pltpu.SemaphoreType.REGULAR((3, 2, 2)),
    ]

    def body(*refs):
        ends = np.cumsum([9, len(vec), 4 + len(scratch), chunks])
        head, lines, main, kept = (
            refs[start:stop] for start, stop in zip([0, *ends[:-1]], ends, strict=True)
        )
        train_kernel(heads, *head, lines, *main, kept, *refs[ends[-1] :])

    return pl.pallas_call(
        body,
        out_shape=(
            jax.ShapeDtypeStruct((count, columns, seq_len), BF16),
            jax.ShapeDtypeStruct((count, columns, seq_len), BF16),
            jax.ShapeDtypeStruct((total_rows, width), BF16),
            jax.ShapeDtypeStruct((8, width), F32),
        ),
        in_specs=[hbm, hbm, smem, vmem, hbm, hbm, hbm, hbm, vmem] + [vmem] * len(vec),
        out_specs=(hbm, hbm, hbm, hbm),
        scratch_shapes=scratch + probs + semaphores,
        compiler_params=pltpu.CompilerParams(
            collective_id=0, has_side_effects=True, vmem_limit_bytes=63 * 2**20
        ),
    )(
        x.reshape(count, chunks, rows, width),
        target.reshape(count, chunks, rows, width),
        tissue,
        tables,
        wq,
        wd,
        w1,
        w2,
        qkv_bias,
        *vec,
    )


def widen_kernel(
    heads,
    sizes,
    cols,
    grad_cols,
    total,
    lines,
    out_cols,
    out_grad_cols,
    goal0,
    goal1,
    goal2,
    goal3,
    gain1,
    bias1,
    gain2,
    bias2,
    out_bias,
    out_bias_again,
    fc1_bias,
    qkv_bias,
    cols_kept,
    cols_low,
    cols_wide,
    rows_low,
    rows_wide,
    pass_sem,
    load_sem,
    store_sem,
):
    block = sizes[-1]
    through = pltpu.make_async_copy(cols, cols_kept, pass_sem.at[0])
    onward = pltpu.make_async_copy(cols_kept, out_cols, pass_sem.at[1])
    moves = []
    for index in range(cols.shape[0]):
        moves.append(
            (grad_cols.at[index], cols_low.at[index], cols_wide.at[index], out_grad_cols.at[index])
        )
    start = 0
    for size, goal in zip(sizes, (goal0, goal1, goal2, goal3), strict=True):
        for at in range(0, size, block):
            here = slice(start + at, start + at + block)
            moves.append(
                (total.at[here], rows_low.at[here], rows_wide.at[here], goal.at[at : at + block])
            )
        start += size
    loads = [
        pltpu.make_async_copy(source, low, load_sem.at[index])
        for index, (source, low, _, _) in enumerate(moves)
    ]
    stores = [
        pltpu.make_async_copy(wide, goal, store_sem.at[index])
        for index, (_, _, wide, goal) in enumerate(moves)
    ]
    for item in loads:
        item.start()
    through.start()
    for index, goal in enumerate((gain1, bias1, gain2, bias2)):
        goal[...] = lines[index : index + 1]
    out_bias[...] = lines[5:6]
    out_bias_again[...] = lines[5:6]
    fc1_bias[...] = lines[6:7]
    line = lines[4:5]
    lanes = line.shape[1] // 3
    pieces = []
    for h in range(heads):
        for part_index in range(3):
            at = part_index * lanes + h * HEAD
            pieces.append(line[:, at : at + HEAD])
    qkv_bias[...] = jnp.concatenate(pieces, axis=1)
    for load, store, (_, low, wide, _) in zip(loads, stores, moves, strict=True):
        load.wait()
        wide[...] = low[...].astype(F32)
        store.start()
    through.wait()
    onward.start()
    for item in stores:
        item.wait()
    onward.wait()


def widen(out_cols, grad_cols, total, lines, heads, units):
    width = total.shape[1]
    sizes = (width, units, 3 * heads * HEAD, heads * HEAD)
    count = out_cols.shape[0] + sum(sizes) // sizes[-1]
    hbm = pl.BlockSpec(memory_space=pl.ANY)
    vmem = pl.BlockSpec(memory_space=pltpu.VMEM)
    line = jax.ShapeDtypeStruct((1, width), F32)
    return pl.pallas_call(
        functools.partial(widen_kernel, heads, sizes),
        in_specs=[hbm, hbm, hbm, vmem],
        out_specs=[hbm] * 6 + [vmem] * 8,
        out_shape=[
            jax.ShapeDtypeStruct(out_cols.shape, BF16),
            jax.ShapeDtypeStruct(out_cols.shape, F32),
        ]
        + [jax.ShapeDtypeStruct((size, width), F32) for size in sizes]
        + [line] * 7
        + [jax.ShapeDtypeStruct((1, sizes[2]), F32)],
        scratch_shapes=[
            pltpu.VMEM(out_cols.shape, BF16),
            pltpu.VMEM(out_cols.shape, BF16),
            pltpu.VMEM(out_cols.shape, F32),
            pltpu.VMEM(total.shape, BF16),
            pltpu.VMEM(total.shape, F32),
            pltpu.SemaphoreType.DMA((2,)),
            pltpu.SemaphoreType.DMA((count,)),
            pltpu.SemaphoreType.DMA((count,)),
        ],
        compiler_params=pltpu.CompilerParams(vmem_limit_bytes=60 * 2**20),
    )(out_cols, grad_cols, total, lines)


def per_device(
    hidden_in,
    target,
    tissue,
    ln1_gain,
    ln1_bias,
    ln2_gain,
    ln2_bias,
    qkv_weight,
    qkv_bias,
    dense_weight,
    dense_bias,
    fc1_weight,
    fc1_bias,
    fc2_weight,
    fc2_bias,
):
    heads = dense_weight.shape[1] // HEAD
    units = fc1_weight.shape[-1]
    weights = (qkv_weight[0].T, dense_weight[0], fc1_weight[0], fc2_weight[0])
    vec = (ln1_gain, ln1_bias, ln2_gain, ln2_bias, dense_bias, fc2_bias, fc1_bias)
    out_cols, grad_cols, total, lines = train(hidden_in, target, tissue, weights, qkv_bias, vec)
    out_cols, grad_cols, fc1_grad, fc2_grad, qkv_grad, dense_grad, *lines = widen(
        out_cols, grad_cols, total, lines, heads, units
    )
    gain1, bias1, gain2, bias2, dense_bias_grad, fc2_bias_grad, fc1_bias_grad, qkv_bias_grad = lines
    return (
        out_cols.transpose(0, 2, 1)[None],
        grad_cols.transpose(0, 2, 1)[None],
        gain1,
        bias1,
        gain2,
        bias2,
        qkv_grad.T[None],
        qkv_bias_grad,
        dense_grad[None],
        dense_bias_grad,
        fc1_grad[None],
        fc1_bias_grad,
        fc2_grad[None],
        fc2_bias_grad,
    )


def solution(mesh):
    return jax.shard_map(
        per_device,
        mesh=mesh,
        in_specs=(
            P("dp", None, None),
            P("dp", None, None),
            P("dp"),
            P("section", None),
            P("section", None),
            P("section", None),
            P("section", None),
            P("section", None, "tensor"),
            P("section", "tensor"),
            P("section", "tensor", None),
            P("section", None),
            P("section", None, "tensor"),
            P("section", "tensor"),
            P("section", "tensor", None),
            P("section", None),
        ),
        out_specs=(
            P("section", "dp", None, "tensor"),
            P("section", "dp", None, "tensor"),
            P("section", None),
            P("section", None),
            P("section", None),
            P("section", None),
            P("section", None, "tensor"),
            P("section", "tensor"),
            P("section", "tensor", None),
            P("section", None),
            P("section", None, "tensor"),
            P("section", "tensor"),
            P("section", "tensor", None),
            P("section", None),
        ),
        check_vma=False,
    )
```

```python
import functools
import math

import jax
import jax.numpy as jnp
import numpy as np
from jax import lax
from jax.experimental import pallas as pl
from jax.experimental.pallas import tpu as pltpu
from jax.sharding import PartitionSpec as P

HEAD = 64
ROT = 16
TISSUES = 16
ROWS = 256
UNIT = 128
LANES = 128
EPS = 1e-05
MESH = pl.DeviceIdType.MESH
F32 = jnp.float32
BF16 = jnp.bfloat16


def dot_nn(a, b):
    return lax.dot_general(a, b, (((1,), (0,)), ((), ())), preferred_element_type=F32)


def dot_nt(a, b):
    return lax.dot_general(a, b, (((1,), (1,)), ((), ())), preferred_element_type=F32)


def dot_tn(a, b):
    return lax.dot_general(a, b, (((0,), (0,)), ((), ())), preferred_element_type=F32)


def rotary_tables(seq_len):
    half = ROT // 2
    inverse = 10000.0 ** (-2.0 * np.arange(half) / ROT)
    angles = np.arange(seq_len)[:, None] * inverse[None, :]
    cosines = np.ones((seq_len, HEAD))
    sines = np.zeros((seq_len, HEAD))
    cosines[:, :half] = np.cos(angles)
    cosines[:, half:ROT] = np.cos(angles)
    sines[:, :half] = -np.sin(angles)
    sines[:, half:ROT] = np.sin(angles)
    tables = np.stack([np.tile(item, (1, LANES // HEAD)) for item in (cosines, sines)])
    return tables.astype(np.float32)


def normalise(value):
    center = value - jnp.mean(value, axis=-1, keepdims=True)
    rstd = lax.rsqrt(jnp.mean(center * center, axis=-1, keepdims=True) + EPS)
    return center * rstd, rstd


def train_kernel(
    heads,
    x_in,
    target_in,
    tissue,
    tables,
    wq_in,
    wd_in,
    w1_in,
    w2_in,
    qkv_bias,
    vec_in,
    out_cols,
    grad_cols,
    grads,
    lines,
    small,
    wq,
    wd,
    w1,
    w2,
    vec,
    chain,
    qkv,
    ctx,
    act,
    gate,
    key_grad,
    value_grad,
    part,
    late_part,
    got,
    met,
    late_got,
    late_met,
    norm_rows,
    context_grad,
    query_back,
    total,
    half_got,
    first_got,
    second_got,
    more_got,
    line_got,
    tally,
    tally_got,
    probs,
    load_sem,
    give_sem,
    take_sem,
    hop_send,
    hop_recv,
    swap_send,
    swap_recv,
    sum_send,
    sum_recv,
    line_send,
    line_recv,
    tally_send,
    tally_recv,
    store_sem,
    free_sem,
):
    section = lax.axis_index("section")
    replica = lax.axis_index("dp")
    place = lax.axis_index("tensor")
    copies = lax.axis_size("dp")
    bits = copies.bit_length() - 1
    _, chunks, rows, width = chain.shape
    unit = part.shape[1]
    halves = rows // unit
    units = chunks * halves
    half_width = late_met.shape[-1]
    lanes = wd.shape[1]
    valid = heads * HEAD
    columns = out_cols.shape[1]
    padded = -(-columns // LANES) * LANES
    inner = jnp.logical_and(place > 0, place < 3)
    outer = jnp.logical_not(inner)
    beside = place + 1 - 2 * lax.rem(place, 2)
    across = 3 - place

    def flipped(bit):
        return replica + (1 << bit) * (1 - 2 * lax.rem(replica // (1 << bit), 2))

    twin = {"section": 1 - section}
    mates = [{"dp": flipped(bit)} for bit in range(bits)]
    near = {"tensor": beside}
    far = {"tensor": across}
    friends = [twin, near, far] + mates

    def send(source, goal, sems, target):
        return pltpu.make_async_remote_copy(
            src_ref=source,
            dst_ref=goal,
            send_sem=sems[0],
            recv_sem=sems[1],
            device_id=target,
            device_id_type=MESH,
        )

    barrier = pltpu.get_barrier_semaphore()
    for friend in friends:
        pl.semaphore_signal(barrier, inc=1, device_id=friend, device_id_type=MESH)

    input_load = pltpu.make_async_copy(x_in.at[section], chain.at[0], load_sem.at[0])
    input_load.start()
    pairs = [(wq_in.at[:, index], wq.at[section, index, :heads]) for index in range(3)]
    pairs += [(w1_in, w1.at[section]), (wd_in, wd.at[section, :valid]), (w2_in, w2.at[section])]
    loads = [
        pltpu.make_async_copy(source, goal, load_sem.at[4 + index])
        for index, (source, goal) in enumerate(pairs)
    ]
    for item in loads:
        item.start()
    target_load = pltpu.make_async_copy(target_in.at[section], chain.at[2], load_sem.at[3])
    target_load.start()

    for index, item in enumerate(vec_in):
        vec[section, index : index + 1] = item[...].astype(F32)
    vec[section, 4:5] = vec_in[4][...].astype(F32) + vec_in[5][...].astype(F32)
    line = qkv_bias[...].astype(F32)
    gap = [jnp.zeros((1, lanes - valid), F32)] if lanes > valid else []
    packed = []
    for part_index in range(3):
        for h in range(heads):
            packed.append(line[:, (3 * h + part_index) * HEAD : (3 * h + part_index + 1) * HEAD])
        packed += gap
    vec[section, 5:6] = jnp.concatenate(packed, axis=1)
    vec[section, 7:8] = jnp.zeros((1, width), F32)
    for layer in range(2):
        wd[layer, valid:] = jnp.zeros((lanes - valid, width), BF16)
        wq[layer, :, heads:] = jnp.zeros((3, lanes // HEAD - heads, HEAD, width), BF16)
    pl.semaphore_wait(barrier, len(friends))
    gifts = [
        send(source, goal, (give_sem.at[index], take_sem.at[index]), twin)
        for index, (source, goal) in enumerate(
            [(vec.at[section], vec.at[section])] + pairs
        )
    ]
    projection = 3
    for item in gifts[: 2 + projection]:
        item.start()

    small[...] = jnp.zeros_like(small)
    tissue_lane = lax.broadcasted_iota(jnp.int32, (8, LANES), 1)
    marks = [(tissue_lane == tissue[index]).astype(F32) for index in range(tissue.shape[0])]
    tally[...] = functools.reduce(lambda a, b: a + b, marks)

    def tally_step(bit):
        return send(
            tally, tally_got.at[bit], (tally_send.at[0], tally_recv.at[bit]), mates[bit]
        )

    if bits:
        tally_step(0).start()

    def count_on(bit):
        step = tally_step(bit)
        step.wait()
        tally[...] += tally_got[bit]
        if bit + 1 < bits:
            tally_step(bit + 1).start()

    lane = lax.broadcasted_iota(jnp.int32, (1, lanes), 1) // HEAD
    head_masks = [lane == h for h in range(heads)]
    factor = HEAD ** (-0.5)

    left_half = lax.rem(lax.broadcasted_iota(jnp.int32, (1, lanes), 1), HEAD) < ROT // 2

    def wide(table, start):
        piece = tables[table, pl.ds(start, rows), :]
        return jnp.concatenate([piece] * (lanes // LANES), axis=1)

    def turned(value):
        ahead = pltpu.roll(value, lanes - ROT // 2, 1)
        behind = pltpu.roll(value, ROT // 2, 1)
        return jnp.where(left_half, ahead, behind)

    def turn(value, start):
        return value * wide(0, start) + turned(value) * wide(1, start)

    def turn_back(value, start):
        return value * wide(0, start) - turned(value) * wide(1, start)

    def only(mask, value):
        return jnp.where(mask, value, jnp.zeros_like(value))

    def put(goal, slot, value):
        for half in range(halves):
            piece = value[half * unit : (half + 1) * unit]
            goal[slot * halves + half] = piece.astype(BF16)

    def forward_chunk(layer, c):
        start = c * rows
        here = slice(start, start + rows)
        if c == 0:
            need(0, 1 + projection, layer)
            for item in gifts[2 + projection :]:
                pl.when(layer == 0)(item.start)
        spread, _ = normalise(chain[layer, c].astype(F32))
        first = (spread * vec[layer, 0:1] + vec[layer, 1:2]).astype(BF16)
        second = (spread * vec[layer, 2:3] + vec[layer, 3:4]).astype(BF16)
        projected = dot_nt(first, wq[layer].reshape(3 * lanes, width)) + vec[layer, 5:6]
        query = turn(projected[:, :lanes], start).astype(BF16)
        qkv[layer, here, :lanes] = query
        qkv[layer, here, lanes : 2 * lanes] = turn(projected[:, lanes : 2 * lanes], start).astype(
            BF16
        )
        qkv[layer, here, 2 * lanes :] = projected[:, 2 * lanes :].astype(BF16)
        if c == 0:
            need(1 + projection, 2 + projection, layer)
        pre = dot_nn(second, w1[layer]) + vec[layer, 6:7]
        below = 0.5 * (1.0 + lax.erf(pre * (0.5**0.5)))
        active = (pre * below).astype(BF16)
        act[layer, here, :] = active
        slope = below + pre * (jnp.exp(-0.5 * pre * pre) * ((2.0 * np.pi) ** -0.5))
        gate[layer, here, :] = slope.astype(BF16)
        diagonal = lax.broadcasted_iota(jnp.int32, (rows, rows), 0) >= lax.broadcasted_iota(
            jnp.int32, (rows, rows), 1
        )
        context = jnp.zeros((rows, lanes), F32)
        for h in range(heads):
            asked = only(head_masks[h], query) * jnp.asarray(factor, BF16)
            near = dot_nt(asked, qkv[layer, here, lanes : 2 * lanes])
            near = jnp.where(diagonal, near, -1e30)
            highest = jnp.max(near, axis=-1, keepdims=True)
            if c > 0:
                far = dot_nt(asked, qkv[layer, :start, lanes : 2 * lanes])
                highest = jnp.maximum(highest, jnp.max(far, axis=-1, keepdims=True))
                far = jnp.exp(far - highest)
            near = jnp.exp(near - highest)
            total = jnp.sum(near, axis=-1, keepdims=True)
            if c > 0:
                total = total + jnp.sum(far, axis=-1, keepdims=True)
            inverse = 1.0 / total
            near = (near * inverse).astype(BF16)
            probs[c][layer, h, :, start:] = near
            mixed = dot_nn(near, qkv[layer, here, 2 * lanes :])
            if c > 0:
                far = (far * inverse).astype(BF16)
                probs[c][layer, h, :, :start] = far
                mixed = mixed + dot_nn(far, qkv[layer, :start, 2 * lanes :])
            context = jnp.where(head_masks[h], mixed, context)
        context = context.astype(BF16)
        ctx[layer, here, :] = context
        if c == 0:
            need(2 + projection, 4 + projection, layer)
        result = (dot_nn(context, wd[layer]) + dot_nn(active, w2[layer])).astype(BF16)
        for index, goal in enumerate((part, late_part)):
            pl.when(layer == index)(functools.partial(put, goal, c, result))
        return second

    def feed_back(c, second):
        here = slice(c * rows, (c + 1) * rows)
        cotangent = chain[2, c]
        pre_grad = (dot_nt(cotangent, w2[1]) * gate[1, here, :].astype(F32)).astype(BF16)
        gate[1, here, :] = pre_grad
        if c < chunks - 1:
            norm_rows[...] = second
            add_forward_grads(1, c, c == 0)

    def rows_of(c):
        return pl.ds(pl.multiple_of(c * rows, rows), rows)

    def backward_front(layer, c):
        here = rows_of(c)
        cotangent = chain[3 - layer, c]
        context_grad[...] = dot_nt(cotangent, wd[layer]).astype(BF16)

        @pl.when(layer == 0)
        def _():
            back = dot_nt(cotangent, w2[0]) * gate[0, here, :].astype(F32)
            gate[0, here, :] = back.astype(BF16)

    def backward_attention(layer, c):
        start = c * rows
        stop = start + rows
        here = slice(start, stop)
        own = context_grad[...]
        query = qkv[layer, here, :lanes]
        weighed = own.astype(F32) * ctx[layer, here, :].astype(F32)
        query_grad = jnp.zeros((rows, lanes), F32)
        key_sum = None
        value_sum = None
        for h in range(heads):
            mask = head_masks[h]
            own_grad = only(mask, own)
            asked = only(mask, query) * jnp.asarray(factor, BF16)
            row_dot = jnp.sum(only(mask, weighed), axis=-1, keepdims=True)
            prob = probs[c][layer, h]
            prob_grad = dot_nt(own_grad, qkv[layer, :stop, 2 * lanes :])
            score_grad = (prob.astype(F32) * (prob_grad - row_dot)).astype(BF16)
            query_grad = jnp.where(
                mask, dot_nn(score_grad, qkv[layer, :stop, lanes : 2 * lanes]), query_grad
            )
            key_part = dot_tn(score_grad, asked)
            value_part = dot_tn(prob, own_grad)
            key_sum = key_part if key_sum is None else key_sum + key_part
            value_sum = value_part if value_sum is None else value_sum + value_part
        query_back[...] = query_grad * factor
        if c == chunks - 1:
            key_grad[:stop] = key_sum
            value_grad[:stop] = value_sum
        else:
            key_grad[:stop] += key_sum
            value_grad[:stop] += value_sum

    def backward_rest(layer, c):
        here = rows_of(c)
        start = pl.multiple_of(c * rows, rows)
        pre_grad = gate[layer, here]
        second_back = dot_nt(pre_grad, w1[layer])
        qkv[layer, here, :lanes] = turn_back(query_back[...], start).astype(BF16)
        qkv[layer, here, lanes : 2 * lanes] = turn_back(key_grad[here], start).astype(BF16)
        qkv[layer, here, 2 * lanes :] = value_grad[here].astype(BF16)
        projected_grad = qkv[layer, here, :]
        first_back = dot_nn(projected_grad, wq[layer].reshape(3 * lanes, width))
        spread, rstd = normalise(chain[layer, c].astype(F32))
        back = first_back * vec[layer, 0:1] + second_back * vec[layer, 2:3]
        middle = jnp.mean(back, axis=-1, keepdims=True)
        tilt = jnp.mean(back * spread, axis=-1, keepdims=True)
        put(part, chunks - 1 - c, rstd * (back - middle - spread * tilt))
        first = (spread * vec[layer, 0:1] + vec[layer, 1:2]).astype(BF16)
        norm_rows[...] = (spread * vec[layer, 2:3] + vec[layer, 3:4]).astype(BF16)
        sums = (
            first_back * spread,
            first_back,
            second_back * spread,
            second_back,
            projected_grad.astype(F32),
            chain[3 - layer, c].astype(F32),
            pre_grad.astype(F32),
        )
        for index, item in enumerate(sums):
            small[layer, index : index + 1] += jnp.sum(item, axis=0, keepdims=True)
        return first

    def add_piece_grads(layer, start, piece, first_turn):
        goal = slice(start, start + piece.shape[0])
        before = jnp.where(first_turn, 0.0, total[layer, goal].astype(F32))
        total[layer, goal] = (piece + before).astype(BF16)

    def add_forward_grads(layer, c, first_turn, parts=("fc1", "fc2")):
        here = rows_of(c)
        cotangent = chain.at[3 - layer, c]

        def add_block(index, carry):
            block = pl.ds(pl.multiple_of(index * lanes, lanes), lanes)
            goal = pl.ds(pl.multiple_of(width + index * lanes, lanes), lanes)
            pieces = []
            if "fc1" in parts:
                pieces.append((block, dot_tn(norm_rows[:, block], gate[layer, here])))
            if "fc2" in parts:
                pieces.append((goal, dot_tn(act[layer, here, block], cotangent[...])))
            for at, piece in pieces:
                before = jnp.where(first_turn, 0.0, total[layer, at].astype(F32))
                total[layer, at] = (piece + before).astype(BF16)
            return carry

        lax.fori_loop(0, width // lanes, add_block, 0)

    def add_weight_grads(layer, c, first):
        base = width + act.shape[-1]
        here = rows_of(c)
        first_turn = c == chunks - 1
        for part_index in range(3):
            at = part_index * lanes
            piece = dot_tn(qkv[layer, here, at : at + lanes], first)
            for h in range(heads):
                row = base + (3 * h + part_index) * HEAD
                add_piece_grads(layer, row, piece[h * HEAD : (h + 1) * HEAD], first_turn)
        piece = dot_tn(ctx[layer, here], chain[3 - layer, c])[:valid]
        add_piece_grads(layer, base + 3 * valid, piece, first_turn)

    cut = width + act.shape[-1]
    jobs = ((width, cut - width), (0, width), (cut, total.shape[1] - cut))
    folds = min(bits, 2)
    sum_steps = 2 + 2 * folds + (bits - folds)

    def spans(job, group):
        order = ((0, 1), (1, 0))[group][:folds]
        base, size = jobs[job]
        size = size // 4
        start = base + section * size * 2 + group * size
        steps = []
        for bit in order:
            size = size // 2
            upper = lax.rem(replica // (1 << bit), 2)
            steps.append((bit, start + upper * size, start + (1 - upper) * size, size))
            start = start + upper * size
        return steps, start, size

    groups = [[spans(job, group) for group in range(2)] for job in range(len(jobs))]

    def sums_of(layer, start, size):
        return total.at[layer, pl.ds(pl.multiple_of(start, 16), size)]

    def gathered(layer, job, group, start, size):
        base, job_rows = jobs[job]
        start = start - base - section * (job_rows // 2) - group * (job_rows // 4) + base // 4
        return (act, gate)[group].at[layer, pl.ds(pl.multiple_of(start, 16), size)]

    def sum_sems(layer, job, step, group):
        return sum_send.at[layer, job, group], sum_recv.at[layer, job, step, group]

    def landing_of(buffer, job, parts):
        base, job_rows = jobs[job]
        return buffer.at[base // parts : (base + job_rows) // parts]

    def sum_copies(layer, job, step):
        base, job_rows = jobs[job]
        if step == 0:
            source = sums_of(layer, base + (1 - section) * (job_rows // 2), job_rows // 2)
            goal = landing_of(half_got.at[layer], job, 2)
            return [send(source, goal, sum_sems(layer, job, 0, 0), twin)]
        copies_now = []
        for group, (steps, start, size) in enumerate(groups[job]):
            sems = sum_sems(layer, job, step, group)
            if step <= folds:
                bit, _, gone, size = steps[step - 1]
                goal = landing_of((first_got, second_got)[step - 1].at[group], job, 4 << step)
                copies_now.append(send(sums_of(layer, gone, size), goal, sems, mates[bit]))
            elif step <= bits:
                goal = landing_of(more_got.at[layer, step - 1 - folds, group], job, 16)
                source = gathered(layer, job, group, start, size)
                copies_now.append(send(source, goal, sems, mates[step - 1]))
            else:
                bit, start, _, size = steps[bits - step]
                piece = gathered(layer, job, group, start, size)
                copies_now.append(send(piece, piece, sems, mates[bit]))
        return copies_now

    def last_copies(layer, job):
        base, job_rows = jobs[job]
        size = job_rows // 4
        pieces = []
        for group in range(2):
            first_row = base + section * (job_rows // 2) + group * size
            piece = gathered(layer, job, group, first_row, size)
            goal = grads.at[pl.ds(pl.multiple_of(first_row, 16), size)]
            sems = sum_sems(layer, job, sum_steps - 1, group)
            other_row = base + (1 - section) * (job_rows // 2) + group * size
            other = grads.at[pl.ds(pl.multiple_of(other_row, 16), size)]
            pieces.append(
                (
                    send(piece, goal, sems, twin),
                    send(piece, other, sems, twin),
                    pltpu.make_async_copy(piece, goal, store_sem.at[job, group]),
                )
            )
        return pieces

    def sum_start(layer, job, step):
        if step < sum_steps - 1:
            if layer == 0 and 1 <= step <= folds:
                pl.semaphore_wait(free_sem.at[job, step - 1], 2)
            for item in sum_copies(layer, job, step):
                item.start()
            return
        for give, _, keep in last_copies(layer, job):
            pl.when(section != layer)(give.start)
            pl.when(section == layer)(keep.start)

    def add_rows(goal, base, source):
        size = source.shape[0]
        piece = math.gcd(size, 192)

        def add_piece(index, carry):
            here = pl.ds(pl.multiple_of(index * piece, 16), piece)
            goal[here] = (base[here].astype(F32) + source[here].astype(F32)).astype(BF16)
            return carry

        lax.fori_loop(0, size // piece, add_piece, 0)

    def sum_end(layer, job, step):
        if step == sum_steps - 1:
            for give, take, keep in last_copies(layer, job):
                pl.when(section != layer)(give.wait_send)
                pl.when(section == layer)(take.wait_recv)
                pl.when(section == layer)(keep.wait)
            return
        for item in sum_copies(layer, job, step):
            item.wait()
        if step == 0:
            base, job_rows = jobs[job]
            kept = sums_of(layer, base + section * (job_rows // 2), job_rows // 2)
            add_rows(kept, kept, landing_of(half_got.at[layer], job, 2))
            return
        if step > bits:
            return
        for group, (steps, start, size) in enumerate(groups[job]):
            goal = gathered(layer, job, group, start, size)
            if step < folds:
                base = sums_of(layer, steps[step - 1][1], steps[step - 1][3])
                add_rows(base, base, landing_of(first_got.at[group], job, 8))
            elif step == folds:
                add_rows(goal, sums_of(layer, start, size), landing_of(second_got.at[group], job, 16))
            else:
                landed = landing_of(more_got.at[layer, step - 1 - folds, group], job, 16)
                add_rows(goal, goal, landed)
            if layer == 1 and step <= folds:
                mate = mates[steps[step - 1][0]]
                pl.semaphore_signal(
                    free_sem.at[job, step - 1],
                    inc=1,
                    device_id=mate,
                    device_id_type=MESH,
                )

    steps_done = {(layer, job): 0 for layer in range(2) for job in range(len(jobs))}

    def move_sum(layer, job, step=None):
        step = steps_done[layer, job] if step is None else step
        if step < sum_steps:
            sum_end(layer, job, step)
            if step + 1 < sum_steps:
                sum_start(layer, job, step + 1)
            steps_done[layer, job] = max(steps_done[layer, job], step + 1)

    line_friends = [twin] + mates + [near, far]

    def line_copy(step):
        sems = (line_send.at[0], line_recv.at[step])
        return send(small, line_got.at[step], sems, line_friends[step])

    def line_end(step):
        line_copy(step).wait()
        if step <= bits:
            small[...] += line_got[step]
        else:
            small[:, 0:4] += line_got[step, :, 0:4]

    low_side = place < 2
    own_half = pl.multiple_of(jnp.where(low_side, 0, half_width), LANES)
    other_half = pl.multiple_of(jnp.where(low_side, half_width, 0), LANES)
    window = place * columns // LANES * LANES
    window = pl.multiple_of(window, LANES)
    end_window = pl.multiple_of(jnp.where(low_side, 0, width - padded), LANES)

    sent_width = width - LANES
    sent_lanes = pl.ds(pl.multiple_of(jnp.where(low_side, LANES, 0), LANES), sent_width)

    def spot(kind, u):
        chunk = u // halves if kind < 2 else chunks - 1 - u // halves
        return chunk, pl.ds(pl.multiple_of(lax.rem(u, halves) * unit, unit), unit)

    def buffers(kind, u):
        if kind == 1:
            return late_part.at[u], late_got.at[u], late_met.at[u]
        return part.at[u], got.at[u], met.at[u] if kind != 3 else met.at[u, :, :half_width]

    def hop_sems(kind, stage, u):
        late = int(kind == 1)
        return hop_send.at[late, (0, 0, 1)[stage], u], hop_recv.at[late, (0, 1, 0)[stage], u]

    def first_hop(kind, u):
        own, landing, _ = buffers(kind, u)
        if kind in (1, 3):
            own, landing = own.at[:, sent_lanes], landing.at[:, :sent_width]
        return send(own, landing, hop_sems(kind, 0, u), near)

    def second_hop(kind, u):
        own, _, landing = buffers(kind, u)
        if kind in (1, 3):
            own = own.at[:, pl.ds(other_half, half_width)]
        return send(own, landing, hop_sems(kind, 1, u), far)

    def third_hop(kind, u):
        own, _, landing = buffers(kind, u)
        if kind in (1, 3):
            own, landing = own.at[:, pl.ds(end_window, padded)], landing.at[:, :padded]
        else:
            chunk, here = spot(kind, u)
            own = landing = chain.at[kind + 1, chunk, here]
        return send(own, landing, hop_sems(kind, 2, u), near)

    def by_rows(count, work, step=32):
        def turn_rows(index, carry):
            work(pl.ds(pl.multiple_of(index * step, step), step))
            return carry

        lax.fori_loop(0, count // step, turn_rows, 0)

    def launch(kind, c, parts=(0, 1)):
        @pl.when(outer)
        def _():
            for half in parts:
                first_hop(kind, c * halves + half).start()

    def meet(kind, u):
        @pl.when(inner)
        def _():
            first_hop(kind, u).wait_recv()
            own, landed, _ = buffers(kind, u)
            if kind in (1, 3):
                own, landed = own.at[:, sent_lanes], landed.at[:, :sent_width]

            def add(here):
                own[here] = (own[here].astype(F32) + landed[here].astype(F32)).astype(BF16)

            by_rows(unit, add)
            second_hop(kind, u).start()

    def settle(kind, u):
        chunk, here = spot(kind, u)

        @pl.when(inner)
        def _():
            second_hop(kind, u).wait_recv()
            own, _, landed = buffers(kind, u)
            if kind in (1, 3):
                lanes_here = pl.ds(own_half, half_width)
                goal = own.at[:, lanes_here]
                source = goal
                base = chain.at[kind, chunk, here, lanes_here]
            else:
                lanes_here = slice(None)
                goal = chain.at[kind + 1, chunk, here]
                source = own
                base = chain.at[kind, chunk, here]

            def add(at):
                value = source[at].astype(F32) + landed[at].astype(F32) + base[at].astype(F32)
                if kind < 2:
                    value = value + vec[kind, 4:5, lanes_here]
                goal[at] = value.astype(BF16)

            by_rows(unit, add)
            if kind > 1:
                third_hop((0, 2)[kind - 2], u).wait_send()
            third_hop(kind, u).start()

    def arrive(kind, c):
        @pl.when(outer)
        def _():
            for half in range(halves):
                third_hop(kind, c * halves + half).wait_recv()

    def release(kind, c):
        for half in range(halves):
            u = c * halves + half
            pl.when(outer)(first_hop(kind, u).wait_send)
            pl.when(inner)(second_hop(kind, u).wait_send)

    def let_go(kind):
        for u in range(units):
            pl.when(inner)(third_hop(kind, u).wait_send)

    def serve(kind, meets, settles):
        for index in range(max(len(meets), len(settles))):
            if index < len(meets):
                meet(kind, meets[index])
            if index < len(settles):
                settle(kind, settles[index])

    def need(first, last, layer):
        @pl.when(section == layer)
        def _():
            for index in range(max(first, 1), last):
                loads[index - 1].wait()

        @pl.when(section != layer)
        def _():
            for index in range(first, last):
                gifts[index].wait_recv()

    input_load.wait()

    first_turns = (((), ()), ((), ()), ((0,), ()), ((1, 2), (0, 1)))
    second_turns = (
        (((3,), (2,)), ((4,), (3,))),
        (((5,), (4,)), ((6,), (5,))),
        (((7,), (6,)), ((), (7,))),
        (((), ()), ((), ())),
    )

    def weigh(c):
        chain[2, c] = (vec[0, 7:8] * chain[2, c].astype(F32)).astype(BF16)

    def find_share():
        own_mark = jnp.where(section == 0, marks[0], marks[1])[0:1]
        own_count = jnp.sum(own_mark * tally[0:1], axis=-1, keepdims=True)
        share = (tissue.shape[0] * copies / TISSUES) / own_count
        gifts[0].wait_send()
        vec[0, 7:8] = jnp.broadcast_to(share, (1, width))
        target_load.wait()

    def forward_layer(layer, carry):
        for c in range(chunks):
            pl.when(layer == 1)(functools.partial(arrive, 0, c))
            second = forward_chunk(layer, c)

            @pl.when(layer == 0)
            def _():
                launch(0, c)
                serve(0, *first_turns[c])
                for bit in range(bits):
                    if min(bit, chunks - 1) == c:
                        count_on(bit)

            @pl.when(layer == 1)
            def _():
                serve(0, *second_turns[c][0])
                if c in (1, 2):
                    launch(1, c - 1)
                if c == 2:
                    launch(1, 2, (0,))
                if c == 0:
                    find_share()
                weigh(c)
                feed_back(c, second)
                serve(0, *second_turns[c][1])

        return carry

    lax.fori_loop(0, 2, forward_layer, 0)

    meets = {1: (1, 1, 3, 3, 5), 2: (4, 5, 6, 7, 8, 9, 10, 11), 3: (13, 14, 14)}
    settles = {1: (3, 3, 5, 5, 7), 2: (6, 7, 8, 9, 10, 11, 12, 12), 3: (14,)}
    backward_points = [[] for _ in range(8 * 2)]
    for kind in (1, 2, 3):
        order = [(2 * u, meet, kind, u, meets[kind][u]) for u in range(len(meets[kind]))]
        order += [(2 * u + 3, settle, kind, u, settles[kind][u]) for u in range(len(settles[kind]))]
        for _, work, kind_now, u, point in sorted(order, key=lambda item: item[0]):
            backward_points[point].append((work, kind_now, u))

    def serve_point(point):
        for work, kind, u in backward_points[point]:
            work(kind, u)

    sum_moves = {
        5: ((1, 0, 0), (1, 1, 0)),
        8: ((1, 2, 0),),
        9: ((1, 0, 2), (1, 1, 2)),
        10: ((1, 2, 1),),
        11: ((1, 2, 2),),
        12: ((1, 0, 3), (1, 1, 3)),
        13: ((1, 2, 3),),
        14: ((0, 0, 0),),
    }

    def serve_at(step, point):
        for index in range(2 * chunks):
            number = index * 2 + point

            @pl.when(step == index)
            def _():
                serve_point(number)
                for moved in sum_moves.get(number, ()):
                    move_sum(*moved)

    def backward_step(step, carry):
        turn_index = step // chunks
        at = lax.rem(step, chunks)
        layer = 1 - turn_index
        c = chunks - 1 - at
        last_step = step == 2 * chunks - 1

        @pl.when(layer == 0)
        def _():

            @pl.when(at == 0)
            def _():
                move_sum(1, 0, 1)
                move_sum(1, 1, 1)

            arrive(2, at)
            release(2, at)

        pl.when(layer == 1)(functools.partial(release, 0, at))

        @pl.when(last_step)
        def _():
            add_forward_grads(0, 0, False, ("fc2",))
            sum_start(0, 0, 0)

        backward_front(layer, c)

        @pl.when(last_step)
        def _():
            spread, _ = normalise(chain[0, 0].astype(F32))
            norm_rows[...] = (spread * vec[0, 2:3] + vec[0, 3:4]).astype(BF16)
            add_forward_grads(0, 0, False, ("fc1",))
            sum_start(0, 1, 0)

        for index in range(chunks):
            pl.when(c == index)(functools.partial(backward_attention, layer, index))
        serve_at(step, 0)
        first = backward_rest(layer, c)
        for index in range(2):
            pl.when(turn_index == index)(functools.partial(launch, 2 + index, at))
        pl.when(last_step)(functools.partial(move_sum, 0, 1))
        add_weight_grads(layer, c, first)

        @pl.when(jnp.logical_or(step == 0, jnp.logical_and(layer == 0, c > 0)))
        def _():
            add_forward_grads(layer, c, step == chunks)

        @pl.when(step == 0)
        def _():
            sum_start(1, 0, 0)
            sum_start(1, 1, 0)

        @pl.when(jnp.logical_and(layer == 0, at > 1))
        def _():
            pl.when(at == 2)(functools.partial(launch, 1, 2, (1,)))
            pl.when(at == 3)(functools.partial(launch, 1, 3))

        pl.when(step == chunks - 1)(functools.partial(sum_start, 1, 2, 0))
        pl.when(last_step)(functools.partial(sum_start, 0, 2, 0))
        serve_at(step, 1)
        return carry

    lax.fori_loop(0, 2 * chunks, backward_step, 0)

    shift = lax.rem(place * columns, LANES)

    def staged(index, layer):
        return probs[-1].at[layer, index, :columns]

    def stage(index, layer, row, value):
        turned_value = value.astype(F32).T
        low = turned_value[:columns]
        high = turned_value[LANES // 2 : LANES // 2 + columns]
        goal = pl.ds(pl.multiple_of(row, unit), unit)
        staged(index, layer)[:, goal] = jnp.where(shift == 0, low, high).astype(BF16)

    def stage_whole(index, layer, kind):
        def stage_unit(u, carry):
            rows_here = pl.ds(pl.multiple_of(lax.rem(u, halves) * unit, unit), unit)
            source = chain.at[kind + 1, u // halves, rows_here, pl.ds(window, padded)]
            stage(index, layer, u * unit, source[...])
            return carry

        lax.fori_loop(0, units, stage_unit, 0)

    def stage_own(index, layer, kind):
        for c in range(chunks):
            arrive(kind, c)
            release(kind, c)
        let_go(kind)
        tile = lax.broadcasted_iota(jnp.int32, (1, padded), 1) // LANES
        unsent = tile == jnp.where(low_side, 0, padded // LANES - 1)
        store, landing = (late_part, late_met) if kind == 1 else (part, met)

        def stage_unit(u, carry):
            chunk = u // halves if kind == 1 else chunks - 1 - u // halves
            row = chunk * rows + lax.rem(u, halves) * unit

            @pl.when(outer)
            def _():
                mine = store[u, :, pl.ds(end_window, padded)]
                value = landing[u, :, :padded].astype(F32) + only(unsent, mine.astype(F32))
                stage(index, layer, row, value)

            @pl.when(inner)
            def _():
                stage(index, layer, row, store[u, :, pl.ds(window, padded)])

            return carry

        lax.fori_loop(0, units, stage_unit, 0)

    def swap_columns(index, goal):
        sems = (swap_send.at[index], swap_recv.at[index])
        return [
            send(staged(index, 1 - section), goal.at[section], sems, twin),
            pltpu.make_async_copy(staged(index, section), goal.at[section], load_sem.at[1 + index]),
        ]

    def line_next(step):
        if step < len(line_friends):
            line_end(step)
            if step + 1 < len(line_friends):
                line_copy(step + 1).start()

    line_copy(0).start()
    for item in gifts[1:]:
        item.wait_send()
    meet(3, 3)
    settle(3, 1)
    meet(3, 4)
    move_sum(0, 2)
    settle(3, 2)
    meet(3, 5)
    settle(3, 3)
    line_next(0)
    move_sum(0, 0)
    meet(1, 5)
    settle(3, 4)
    move_sum(0, 1)
    settle(3, 5)
    meet(3, 6)
    settle(1, 5)
    for job in range(2):
        move_sum(1, job)
    move_sum(0, 2)
    stage_whole(0, 0, 0)
    meet(3, 7)
    settle(3, 6)
    move_sum(0, 0)
    move_sum(0, 1)
    line_next(1)
    meet(1, 6)
    settle(3, 7)
    move_sum(0, 2)
    stage_whole(1, 1, 2)
    meet(1, 7)
    move_sum(0, 0)
    settle(1, 6)
    move_sum(0, 1)
    line_next(2)
    settle(1, 7)
    move_sum(0, 2)
    move_sum(1, 2)
    stage_own(1, 0, 3)
    moves = swap_columns(1, grad_cols)
    for item in moves:
        item.start()
    line_next(3)
    stage_own(0, 1, 1)
    late_moves = swap_columns(0, out_cols)
    for item in late_moves:
        item.start()
    move_sum(0, 0)
    move_sum(0, 1)
    for step in range(4, len(line_friends)):
        line_next(step)
    lines_store = pltpu.make_async_copy(small.at[section], lines, load_sem.at[0])
    lines_store.start()
    for _ in range(sum_steps):
        for job in range(len(jobs)):
            move_sum(0, job)
            move_sum(1, job)
    for item in moves + late_moves:
        item.wait()
    lines_store.wait()


def train(x, target, tissue, weights, qkv_bias, vec):
    wq, wd, w1, w2 = weights
    count, seq_len, width = x.shape
    rows = min(ROWS, seq_len)
    chunks = seq_len // rows
    unit = min(UNIT, rows)
    pieces = seq_len // unit
    valid = wd.shape[0]
    heads = valid // HEAD
    lanes = -(-valid // LANES) * LANES
    units = w1.shape[1]
    columns = width // lax.axis_size("tensor")
    bits = lax.axis_size("dp").bit_length() - 1
    tables = jnp.asarray(rotary_tables(seq_len))
    total_rows = 3 * valid + width + units + valid
    hbm = pl.BlockSpec(memory_space=pl.ANY)
    vmem = pl.BlockSpec(memory_space=pltpu.VMEM)
    smem = pl.BlockSpec(memory_space=pltpu.SMEM)
    scratch = [
        pltpu.VMEM((2, 8, width), F32),
        pltpu.VMEM((2, 3, lanes // HEAD, HEAD, width), BF16),
        pltpu.VMEM((2, lanes, width), BF16),
        pltpu.VMEM((2,) + w1.shape, BF16),
        pltpu.VMEM((2,) + w2.shape, BF16),
        pltpu.VMEM((2, 8, width), F32),
        pltpu.VMEM((4, chunks, rows, width), BF16),
        pltpu.VMEM((2, seq_len, 3 * lanes), BF16),
        pltpu.VMEM((2, seq_len, lanes), BF16),
        pltpu.VMEM((2, seq_len, units), BF16),
        pltpu.VMEM((2, seq_len, units), BF16),
        pltpu.VMEM((seq_len, lanes), F32),
        pltpu.VMEM((seq_len, lanes), F32),
        pltpu.VMEM((pieces, unit, width), BF16),
        pltpu.VMEM((pieces, unit, width), BF16),
        pltpu.VMEM((pieces, unit, width), BF16),
        pltpu.VMEM((pieces, unit, width), BF16),
        pltpu.VMEM((pieces, unit, width - LANES), BF16),
        pltpu.VMEM((pieces, unit, width // 2), BF16),
        pltpu.VMEM((rows, width), BF16),
        pltpu.VMEM((rows, lanes), BF16),
        pltpu.VMEM((rows, lanes), F32),
        pltpu.VMEM((2, total_rows, width), BF16),
        pltpu.VMEM((2, total_rows // 2, width), BF16),
        pltpu.VMEM((2, total_rows // 8, width), BF16),
        pltpu.VMEM((2, total_rows // 16, width), BF16),
        pltpu.VMEM((2, max(bits - 2, 1), 2, total_rows // 16 if bits > 2 else 16, width), BF16),
        pltpu.VMEM((3 + bits, 2, 8, width), F32),
        pltpu.VMEM((8, LANES), F32),
        pltpu.VMEM((max(bits, 1), 8, LANES), F32),
    ]
    probs = [pltpu.VMEM((2, heads, rows, (c + 1) * rows), BF16) for c in range(chunks)]
    semaphores = [
        pltpu.SemaphoreType.DMA((10,)),
        pltpu.SemaphoreType.DMA((7,)),
        pltpu.SemaphoreType.DMA((7,)),
        pltpu.SemaphoreType.DMA((2, 2, pieces)),
        pltpu.SemaphoreType.DMA((2, 2, pieces)),
        pltpu.SemaphoreType.DMA((2,)),
        pltpu.SemaphoreType.DMA((2,)),
        pltpu.SemaphoreType.DMA((2, 3, 2)),
        pltpu.SemaphoreType.DMA((2, 3, bits + 4, 2)),
        pltpu.SemaphoreType.DMA((1,)),
        pltpu.SemaphoreType.DMA((3 + bits,)),
        pltpu.SemaphoreType.DMA((1,)),
        pltpu.SemaphoreType.DMA((max(bits, 1),)),
        pltpu.SemaphoreType.DMA((3, 2)),
        pltpu.SemaphoreType.REGULAR((3, 2)),
    ]

    def body(*refs):
        ends = np.cumsum([9, len(vec), 4 + len(scratch), chunks])
        head, lines, main, kept = (
            refs[start:stop] for start, stop in zip([0, *ends[:-1]], ends, strict=True)
        )
        train_kernel(heads, *head, lines, *main, kept, *refs[ends[-1] :])

    return pl.pallas_call(
        body,
        out_shape=(
            jax.ShapeDtypeStruct((count, columns, seq_len), BF16),
            jax.ShapeDtypeStruct((count, columns, seq_len), BF16),
            jax.ShapeDtypeStruct((total_rows, width), BF16),
            jax.ShapeDtypeStruct((8, width), F32),
        ),
        in_specs=[hbm, hbm, smem, vmem, hbm, hbm, hbm, hbm, vmem] + [vmem] * len(vec),
        out_specs=(hbm, hbm, hbm, hbm),
        scratch_shapes=scratch + probs + semaphores,
        compiler_params=pltpu.CompilerParams(
            collective_id=0, has_side_effects=True, vmem_limit_bytes=63 * 2**20
        ),
    )(
        x.reshape(count, chunks, rows, width),
        target.reshape(count, chunks, rows, width),
        tissue,
        tables,
        wq.reshape(heads, 3, HEAD, width),
        wd,
        w1,
        w2,
        qkv_bias,
        *vec,
    )


def widen_kernel(
    heads,
    sizes,
    cols,
    grad_cols,
    total,
    lines,
    out_cols,
    out_grad_cols,
    goal0,
    goal1,
    goal2,
    goal3,
    gain1,
    bias1,
    gain2,
    bias2,
    out_bias,
    out_bias_again,
    fc1_bias,
    qkv_bias,
    cols_kept,
    cols_low,
    cols_wide,
    rows_low,
    rows_wide,
    pass_sem,
    load_sem,
    store_sem,
):
    block = sizes[-1]
    through = pltpu.make_async_copy(cols, cols_kept, pass_sem.at[0])
    onward = pltpu.make_async_copy(cols_kept, out_cols, pass_sem.at[1])
    moves = []
    for index in range(cols.shape[0]):
        moves.append(
            (grad_cols.at[index], cols_low.at[index], cols_wide.at[index], out_grad_cols.at[index])
        )
    start = 0
    for size, goal in zip(sizes, (goal0, goal1, goal2, goal3), strict=True):
        for at in range(0, size, block):
            here = slice(start + at, start + at + block)
            moves.append(
                (total.at[here], rows_low.at[here], rows_wide.at[here], goal.at[at : at + block])
            )
        start += size
    loads = [
        pltpu.make_async_copy(source, low, load_sem.at[index])
        for index, (source, low, _, _) in enumerate(moves)
    ]
    stores = [
        pltpu.make_async_copy(wide, goal, store_sem.at[index])
        for index, (_, _, wide, goal) in enumerate(moves)
    ]
    for item in loads:
        item.start()
    through.start()
    for index, goal in enumerate((gain1, bias1, gain2, bias2)):
        goal[...] = lines[index : index + 1]
    out_bias[...] = lines[5:6]
    out_bias_again[...] = lines[5:6]
    fc1_bias[...] = lines[6:7]
    line = lines[4:5]
    lanes = line.shape[1] // 3
    pieces = []
    for h in range(heads):
        for part_index in range(3):
            at = part_index * lanes + h * HEAD
            pieces.append(line[:, at : at + HEAD])
    qkv_bias[...] = jnp.concatenate(pieces, axis=1)
    for load, store, (_, low, wide, _) in zip(loads, stores, moves, strict=True):
        load.wait()
        wide[...] = low[...].astype(F32)
        store.start()
    through.wait()
    onward.start()
    for item in stores:
        item.wait()
    onward.wait()


def widen(out_cols, grad_cols, total, lines, heads, units):
    width = total.shape[1]
    sizes = (width, units, 3 * heads * HEAD, heads * HEAD)
    count = out_cols.shape[0] + sum(sizes) // sizes[-1]
    hbm = pl.BlockSpec(memory_space=pl.ANY)
    vmem = pl.BlockSpec(memory_space=pltpu.VMEM)
    line = jax.ShapeDtypeStruct((1, width), F32)
    return pl.pallas_call(
        functools.partial(widen_kernel, heads, sizes),
        in_specs=[hbm, hbm, hbm, vmem],
        out_specs=[hbm] * 6 + [vmem] * 8,
        out_shape=[
            jax.ShapeDtypeStruct(out_cols.shape, BF16),
            jax.ShapeDtypeStruct(out_cols.shape, F32),
        ]
        + [jax.ShapeDtypeStruct((size, width), F32) for size in sizes]
        + [line] * 7
        + [jax.ShapeDtypeStruct((1, sizes[2]), F32)],
        scratch_shapes=[
            pltpu.VMEM(out_cols.shape, BF16),
            pltpu.VMEM(out_cols.shape, BF16),
            pltpu.VMEM(out_cols.shape, F32),
            pltpu.VMEM(total.shape, BF16),
            pltpu.VMEM(total.shape, F32),
            pltpu.SemaphoreType.DMA((2,)),
            pltpu.SemaphoreType.DMA((count,)),
            pltpu.SemaphoreType.DMA((count,)),
        ],
        compiler_params=pltpu.CompilerParams(vmem_limit_bytes=60 * 2**20),
    )(out_cols, grad_cols, total, lines)


def per_device(
    hidden_in,
    target,
    tissue,
    ln1_gain,
    ln1_bias,
    ln2_gain,
    ln2_bias,
    qkv_weight,
    qkv_bias,
    dense_weight,
    dense_bias,
    fc1_weight,
    fc1_bias,
    fc2_weight,
    fc2_bias,
):
    heads = dense_weight.shape[1] // HEAD
    units = fc1_weight.shape[-1]
    weights = (qkv_weight[0].T, dense_weight[0], fc1_weight[0], fc2_weight[0])
    vec = (ln1_gain, ln1_bias, ln2_gain, ln2_bias, dense_bias, fc2_bias, fc1_bias)
    out_cols, grad_cols, total, lines = train(hidden_in, target, tissue, weights, qkv_bias, vec)
    out_cols, grad_cols, fc1_grad, fc2_grad, qkv_grad, dense_grad, *lines = widen(
        out_cols, grad_cols, total, lines, heads, units
    )
    gain1, bias1, gain2, bias2, dense_bias_grad, fc2_bias_grad, fc1_bias_grad, qkv_bias_grad = lines
    return (
        out_cols.transpose(0, 2, 1)[None],
        grad_cols.transpose(0, 2, 1)[None],
        gain1,
        bias1,
        gain2,
        bias2,
        qkv_grad.T[None],
        qkv_bias_grad,
        dense_grad[None],
        dense_bias_grad,
        fc1_grad[None],
        fc1_bias_grad,
        fc2_grad[None],
        fc2_bias_grad,
    )


def solution(mesh):
    return jax.shard_map(
        per_device,
        mesh=mesh,
        in_specs=(
            P("dp", None, None),
            P("dp", None, None),
            P("dp"),
            P("section", None),
            P("section", None),
            P("section", None),
            P("section", None),
            P("section", None, "tensor"),
            P("section", "tensor"),
            P("section", "tensor", None),
            P("section", None),
            P("section", None, "tensor"),
            P("section", "tensor"),
            P("section", "tensor", None),
            P("section", None),
        ),
        out_specs=(
            P("section", "dp", None, "tensor"),
            P("section", "dp", None, "tensor"),
            P("section", None),
            P("section", None),
            P("section", None),
            P("section", None),
            P("section", None, "tensor"),
            P("section", "tensor"),
            P("section", "tensor", None),
            P("section", None),
            P("section", None, "tensor"),
            P("section", "tensor"),
            P("section", "tensor", None),
            P("section", None),
        ),
        check_vma=False,
    )
```

```python
import functools
import math

import jax
import jax.numpy as jnp
import numpy as np
from jax import lax
from jax.experimental import pallas as pl
from jax.experimental.pallas import tpu as pltpu
from jax.sharding import PartitionSpec as P

HEAD = 64
ROT = 16
TISSUES = 16
ROWS = 256
UNIT = 128
LANES = 128
EPS = 1e-05
MESH = pl.DeviceIdType.MESH
F32 = jnp.float32
BF16 = jnp.bfloat16


def dot_nn(a, b):
    return lax.dot_general(a, b, (((1,), (0,)), ((), ())), preferred_element_type=F32)


def dot_nt(a, b):
    return lax.dot_general(a, b, (((1,), (1,)), ((), ())), preferred_element_type=F32)


def dot_tn(a, b):
    return lax.dot_general(a, b, (((0,), (0,)), ((), ())), preferred_element_type=F32)


def rotary_tables(seq_len):
    half = ROT // 2
    inverse = 10000.0 ** (-2.0 * np.arange(half) / ROT)
    angles = np.arange(seq_len)[:, None] * inverse[None, :]
    cosines = np.ones((seq_len, HEAD))
    sines = np.zeros((seq_len, HEAD))
    cosines[:, :half] = np.cos(angles)
    cosines[:, half:ROT] = np.cos(angles)
    sines[:, :half] = -np.sin(angles)
    sines[:, half:ROT] = np.sin(angles)
    tables = np.stack([np.tile(item, (1, LANES // HEAD)) for item in (cosines, sines)])
    return tables.astype(np.float32)


def normalise(value):
    center = value - jnp.mean(value, axis=-1, keepdims=True)
    rstd = lax.rsqrt(jnp.mean(center * center, axis=-1, keepdims=True) + EPS)
    return center * rstd, rstd


def train_kernel(
    heads,
    x_in,
    target_in,
    tissue,
    tables,
    wq_in,
    wd_in,
    w1_in,
    w2_in,
    qkv_bias,
    vec_in,
    out_cols,
    grad_cols,
    grads,
    lines,
    small,
    wq,
    wd,
    w1,
    w2,
    vec,
    chain,
    qkv,
    ctx,
    act,
    gate,
    key_grad,
    value_grad,
    part,
    late_part,
    got,
    met,
    late_got,
    late_met,
    norm_rows,
    context_grad,
    query_back,
    total,
    half_got,
    first_got,
    second_got,
    more_got,
    line_got,
    tally,
    tally_got,
    probs,
    load_sem,
    give_sem,
    take_sem,
    hop_send,
    hop_recv,
    swap_send,
    swap_recv,
    sum_send,
    sum_recv,
    line_send,
    line_recv,
    tally_send,
    tally_recv,
    store_sem,
    free_sem,
):
    section = lax.axis_index("section")
    replica = lax.axis_index("dp")
    place = lax.axis_index("tensor")
    copies = lax.axis_size("dp")
    bits = copies.bit_length() - 1
    _, chunks, rows, width = chain.shape
    unit = part.shape[1]
    halves = rows // unit
    units = chunks * halves
    half_width = late_met.shape[-1]
    lanes = wd.shape[1]
    valid = heads * HEAD
    columns = out_cols.shape[1]
    padded = -(-columns // LANES) * LANES
    inner = jnp.logical_and(place > 0, place < 3)
    outer = jnp.logical_not(inner)
    beside = place + 1 - 2 * lax.rem(place, 2)
    across = 3 - place

    def flipped(bit):
        return replica + (1 << bit) * (1 - 2 * lax.rem(replica // (1 << bit), 2))

    twin = {"section": 1 - section}
    mates = [{"dp": flipped(bit)} for bit in range(bits)]
    near = {"tensor": beside}
    far = {"tensor": across}
    friends = [twin, near, far] + mates

    def send(source, goal, sems, target):
        return pltpu.make_async_remote_copy(
            src_ref=source,
            dst_ref=goal,
            send_sem=sems[0],
            recv_sem=sems[1],
            device_id=target,
            device_id_type=MESH,
        )

    barrier = pltpu.get_barrier_semaphore()
    for friend in friends:
        pl.semaphore_signal(barrier, inc=1, device_id=friend, device_id_type=MESH)

    input_load = pltpu.make_async_copy(x_in.at[section], chain.at[0], load_sem.at[0])
    input_load.start()
    pairs = [(wq_in.at[:, index], wq.at[section, index, :heads]) for index in range(3)]
    pairs += [(w1_in, w1.at[section]), (wd_in, wd.at[section, :valid]), (w2_in, w2.at[section])]
    loads = [
        pltpu.make_async_copy(source, goal, load_sem.at[4 + index])
        for index, (source, goal) in enumerate(pairs)
    ]
    for item in loads:
        item.start()
    target_load = pltpu.make_async_copy(target_in.at[section], chain.at[2], load_sem.at[3])
    target_load.start()

    for index, item in enumerate(vec_in):
        vec[section, index : index + 1] = item[...].astype(F32)
    vec[section, 4:5] = vec_in[4][...].astype(F32) + vec_in[5][...].astype(F32)
    line = qkv_bias[...].astype(F32)
    gap = [jnp.zeros((1, lanes - valid), F32)] if lanes > valid else []
    packed = []
    for part_index in range(3):
        for h in range(heads):
            packed.append(line[:, (3 * h + part_index) * HEAD : (3 * h + part_index + 1) * HEAD])
        packed += gap
    vec[section, 5:6] = jnp.concatenate(packed, axis=1)
    vec[section, 7:8] = jnp.zeros((1, width), F32)
    for layer in range(2):
        wd[layer, valid:] = jnp.zeros((lanes - valid, width), BF16)
        wq[layer, :, heads:] = jnp.zeros((3, lanes // HEAD - heads, HEAD, width), BF16)
    pl.semaphore_wait(barrier, len(friends))
    gifts = [
        send(source, goal, (give_sem.at[index], take_sem.at[index]), twin)
        for index, (source, goal) in enumerate(
            [(vec.at[section], vec.at[section])] + pairs
        )
    ]
    projection = 3
    for item in gifts[: 2 + projection]:
        item.start()

    small[...] = jnp.zeros_like(small)
    tissue_lane = lax.broadcasted_iota(jnp.int32, (8, LANES), 1)
    marks = [(tissue_lane == tissue[index]).astype(F32) for index in range(tissue.shape[0])]
    tally[...] = functools.reduce(lambda a, b: a + b, marks)

    def tally_step(bit):
        return send(
            tally, tally_got.at[bit], (tally_send.at[0], tally_recv.at[bit]), mates[bit]
        )

    if bits:
        tally_step(0).start()

    def count_on(bit):
        step = tally_step(bit)
        step.wait()
        tally[...] += tally_got[bit]
        if bit + 1 < bits:
            tally_step(bit + 1).start()

    lane = lax.broadcasted_iota(jnp.int32, (1, lanes), 1) // HEAD
    head_masks = [lane == h for h in range(heads)]
    factor = HEAD ** (-0.5)

    left_half = lax.rem(lax.broadcasted_iota(jnp.int32, (1, lanes), 1), HEAD) < ROT // 2

    def wide(table, start):
        piece = tables[table, pl.ds(start, rows), :]
        return jnp.concatenate([piece] * (lanes // LANES), axis=1)

    def turned(value):
        ahead = pltpu.roll(value, lanes - ROT // 2, 1)
        behind = pltpu.roll(value, ROT // 2, 1)
        return jnp.where(left_half, ahead, behind)

    def turn(value, start):
        return value * wide(0, start) + turned(value) * wide(1, start)

    def turn_back(value, start):
        return value * wide(0, start) - turned(value) * wide(1, start)

    def only(mask, value):
        return jnp.where(mask, value, jnp.zeros_like(value))

    def put(goal, slot, value):
        for half in range(halves):
            piece = value[half * unit : (half + 1) * unit]
            goal[slot * halves + half] = piece.astype(BF16)

    def forward_chunk(layer, c):
        start = c * rows
        here = slice(start, start + rows)
        if c == 0:
            need(0, 1 + projection, layer)
            for item in gifts[2 + projection :]:
                pl.when(layer == 0)(item.start)
        spread, _ = normalise(chain[layer, c].astype(F32))
        first = (spread * vec[layer, 0:1] + vec[layer, 1:2]).astype(BF16)
        second = (spread * vec[layer, 2:3] + vec[layer, 3:4]).astype(BF16)
        projected = dot_nt(first, wq[layer].reshape(3 * lanes, width)) + vec[layer, 5:6]
        query = turn(projected[:, :lanes], start).astype(BF16)
        qkv[layer, here, :lanes] = query
        qkv[layer, here, lanes : 2 * lanes] = turn(projected[:, lanes : 2 * lanes], start).astype(
            BF16
        )
        qkv[layer, here, 2 * lanes :] = projected[:, 2 * lanes :].astype(BF16)
        if c == 0:
            need(1 + projection, 2 + projection, layer)
        pre = dot_nn(second, w1[layer]) + vec[layer, 6:7]
        below = 0.5 * (1.0 + lax.erf(pre * (0.5**0.5)))
        active = (pre * below).astype(BF16)
        act[layer, here, :] = active
        slope = below + pre * (jnp.exp(-0.5 * pre * pre) * ((2.0 * np.pi) ** -0.5))
        gate[layer, here, :] = slope.astype(BF16)
        diagonal = lax.broadcasted_iota(jnp.int32, (rows, rows), 0) >= lax.broadcasted_iota(
            jnp.int32, (rows, rows), 1
        )
        context = jnp.zeros((rows, lanes), F32)
        for h in range(heads):
            asked = only(head_masks[h], query) * jnp.asarray(factor, BF16)
            near = dot_nt(asked, qkv[layer, here, lanes : 2 * lanes])
            near = jnp.where(diagonal, near, -1e30)
            highest = jnp.max(near, axis=-1, keepdims=True)
            if c > 0:
                far = dot_nt(asked, qkv[layer, :start, lanes : 2 * lanes])
                highest = jnp.maximum(highest, jnp.max(far, axis=-1, keepdims=True))
                far = jnp.exp(far - highest)
            near = jnp.exp(near - highest)
            total = jnp.sum(near, axis=-1, keepdims=True)
            if c > 0:
                total = total + jnp.sum(far, axis=-1, keepdims=True)
            inverse = 1.0 / total
            near = (near * inverse).astype(BF16)
            probs[c][layer, h, :, start:] = near
            mixed = dot_nn(near, qkv[layer, here, 2 * lanes :])
            if c > 0:
                far = (far * inverse).astype(BF16)
                probs[c][layer, h, :, :start] = far
                mixed = mixed + dot_nn(far, qkv[layer, :start, 2 * lanes :])
            context = jnp.where(head_masks[h], mixed, context)
        context = context.astype(BF16)
        ctx[layer, here, :] = context
        if c == 0:
            need(2 + projection, 4 + projection, layer)
        result = (dot_nn(context, wd[layer]) + dot_nn(active, w2[layer])).astype(BF16)
        for index, goal in enumerate((part, late_part)):
            pl.when(layer == index)(functools.partial(put, goal, c, result))
        return second

    def feed_back(c, second):
        here = slice(c * rows, (c + 1) * rows)
        cotangent = chain[2, c]
        pre_grad = (dot_nt(cotangent, w2[1]) * gate[1, here, :].astype(F32)).astype(BF16)
        gate[1, here, :] = pre_grad
        if c < chunks - 1:
            norm_rows[...] = second
            add_forward_grads(1, c, c == 0)

    def rows_of(c):
        return pl.ds(pl.multiple_of(c * rows, rows), rows)

    def backward_front(layer, c):
        here = rows_of(c)
        cotangent = chain[3 - layer, c]
        context_grad[...] = dot_nt(cotangent, wd[layer]).astype(BF16)

        @pl.when(layer == 0)
        def _():
            back = dot_nt(cotangent, w2[0]) * gate[0, here, :].astype(F32)
            gate[0, here, :] = back.astype(BF16)

    def backward_attention(layer, c):
        start = c * rows
        stop = start + rows
        here = slice(start, stop)
        own = context_grad[...]
        query = qkv[layer, here, :lanes]
        weighed = own.astype(F32) * ctx[layer, here, :].astype(F32)
        query_grad = jnp.zeros((rows, lanes), F32)
        key_sum = None
        value_sum = None
        for h in range(heads):
            mask = head_masks[h]
            own_grad = only(mask, own)
            asked = only(mask, query) * jnp.asarray(factor, BF16)
            row_dot = jnp.sum(only(mask, weighed), axis=-1, keepdims=True)
            prob = probs[c][layer, h]
            prob_grad = dot_nt(own_grad, qkv[layer, :stop, 2 * lanes :])
            score_grad = (prob.astype(F32) * (prob_grad - row_dot)).astype(BF16)
            query_grad = jnp.where(
                mask, dot_nn(score_grad, qkv[layer, :stop, lanes : 2 * lanes]), query_grad
            )
            key_part = dot_tn(score_grad, asked)
            value_part = dot_tn(prob, own_grad)
            key_sum = key_part if key_sum is None else key_sum + key_part
            value_sum = value_part if value_sum is None else value_sum + value_part
        query_back[...] = query_grad * factor
        if c == chunks - 1:
            key_grad[:stop] = key_sum
            value_grad[:stop] = value_sum
        else:
            key_grad[:stop] += key_sum
            value_grad[:stop] += value_sum

    def backward_rest(layer, c):
        here = rows_of(c)
        start = pl.multiple_of(c * rows, rows)
        pre_grad = gate[layer, here]
        second_back = dot_nt(pre_grad, w1[layer])
        qkv[layer, here, :lanes] = turn_back(query_back[...], start).astype(BF16)
        qkv[layer, here, lanes : 2 * lanes] = turn_back(key_grad[here], start).astype(BF16)
        qkv[layer, here, 2 * lanes :] = value_grad[here].astype(BF16)
        projected_grad = qkv[layer, here, :]
        first_back = dot_nn(projected_grad, wq[layer].reshape(3 * lanes, width))
        spread, rstd = normalise(chain[layer, c].astype(F32))
        back = first_back * vec[layer, 0:1] + second_back * vec[layer, 2:3]
        middle = jnp.mean(back, axis=-1, keepdims=True)
        tilt = jnp.mean(back * spread, axis=-1, keepdims=True)
        put(part, chunks - 1 - c, rstd * (back - middle - spread * tilt))
        first = (spread * vec[layer, 0:1] + vec[layer, 1:2]).astype(BF16)
        norm_rows[...] = (spread * vec[layer, 2:3] + vec[layer, 3:4]).astype(BF16)
        sums = (
            first_back * spread,
            first_back,
            second_back * spread,
            second_back,
            projected_grad.astype(F32),
            chain[3 - layer, c].astype(F32),
            pre_grad.astype(F32),
        )
        for index, item in enumerate(sums):
            small[layer, index : index + 1] += jnp.sum(item, axis=0, keepdims=True)
        return first

    def add_piece_grads(layer, start, piece, first_turn):
        goal = slice(start, start + piece.shape[0])
        before = jnp.where(first_turn, 0.0, total[layer, goal].astype(F32))
        total[layer, goal] = (piece + before).astype(BF16)

    def add_forward_grads(layer, c, first_turn, parts=("fc1", "fc2")):
        here = rows_of(c)
        cotangent = chain.at[3 - layer, c]

        def add_block(index, carry):
            block = pl.ds(pl.multiple_of(index * lanes, lanes), lanes)
            goal = pl.ds(pl.multiple_of(width + index * lanes, lanes), lanes)
            pieces = []
            if "fc1" in parts:
                pieces.append((block, dot_tn(norm_rows[:, block], gate[layer, here])))
            if "fc2" in parts:
                pieces.append((goal, dot_tn(act[layer, here, block], cotangent[...])))
            for at, piece in pieces:
                before = jnp.where(first_turn, 0.0, total[layer, at].astype(F32))
                total[layer, at] = (piece + before).astype(BF16)
            return carry

        lax.fori_loop(0, width // lanes, add_block, 0)

    def add_weight_grads(layer, c, first):
        base = width + act.shape[-1]
        here = rows_of(c)
        first_turn = c == chunks - 1
        for part_index in range(3):
            at = part_index * lanes
            piece = dot_tn(qkv[layer, here, at : at + lanes], first)
            for h in range(heads):
                row = base + (3 * h + part_index) * HEAD
                add_piece_grads(layer, row, piece[h * HEAD : (h + 1) * HEAD], first_turn)
        piece = dot_tn(ctx[layer, here], chain[3 - layer, c])[:valid]
        add_piece_grads(layer, base + 3 * valid, piece, first_turn)

    cut = width + act.shape[-1]
    jobs = ((width, cut - width), (0, width), (cut, total.shape[1] - cut))
    folds = min(bits, 2)
    sum_steps = 2 + 2 * folds + (bits - folds)

    def spans(job, group):
        order = ((0, 1), (1, 0))[group][:folds]
        base, size = jobs[job]
        size = size // 4
        start = base + section * size * 2 + group * size
        steps = []
        for bit in order:
            size = size // 2
            upper = lax.rem(replica // (1 << bit), 2)
            steps.append((bit, start + upper * size, start + (1 - upper) * size, size))
            start = start + upper * size
        return steps, start, size

    groups = [[spans(job, group) for group in range(2)] for job in range(len(jobs))]

    def sums_of(layer, start, size):
        return total.at[layer, pl.ds(pl.multiple_of(start, 16), size)]

    def gathered(layer, job, group, start, size):
        base, job_rows = jobs[job]
        start = start - base - section * (job_rows // 2) - group * (job_rows // 4) + base // 4
        return (act, gate)[group].at[layer, pl.ds(pl.multiple_of(start, 16), size)]

    def sum_sems(layer, job, step, group):
        return sum_send.at[layer, job, group], sum_recv.at[layer, job, step, group]

    def landing_of(buffer, job, parts):
        base, job_rows = jobs[job]
        return buffer.at[base // parts : (base + job_rows) // parts]

    def sum_copies(layer, job, step):
        base, job_rows = jobs[job]
        if step == 0:
            source = sums_of(layer, base + (1 - section) * (job_rows // 2), job_rows // 2)
            goal = landing_of(half_got.at[layer], job, 2)
            return [send(source, goal, sum_sems(layer, job, 0, 0), twin)]
        copies_now = []
        for group, (steps, start, size) in enumerate(groups[job]):
            sems = sum_sems(layer, job, step, group)
            if step <= folds:
                bit, _, gone, size = steps[step - 1]
                goal = landing_of((first_got, second_got)[step - 1].at[group], job, 4 << step)
                copies_now.append(send(sums_of(layer, gone, size), goal, sems, mates[bit]))
            elif step <= bits:
                goal = landing_of(more_got.at[layer, step - 1 - folds, group], job, 16)
                source = gathered(layer, job, group, start, size)
                copies_now.append(send(source, goal, sems, mates[step - 1]))
            else:
                bit, start, _, size = steps[bits - step]
                piece = gathered(layer, job, group, start, size)
                copies_now.append(send(piece, piece, sems, mates[bit]))
        return copies_now

    def last_copies(layer, job):
        base, job_rows = jobs[job]
        size = job_rows // 4
        pieces = []
        for group in range(2):
            first_row = base + section * (job_rows // 2) + group * size
            piece = gathered(layer, job, group, first_row, size)
            goal = grads.at[pl.ds(pl.multiple_of(first_row, 16), size)]
            sems = sum_sems(layer, job, sum_steps - 1, group)
            other_row = base + (1 - section) * (job_rows // 2) + group * size
            other = grads.at[pl.ds(pl.multiple_of(other_row, 16), size)]
            pieces.append(
                (
                    send(piece, goal, sems, twin),
                    send(piece, other, sems, twin),
                    pltpu.make_async_copy(piece, goal, store_sem.at[job, group]),
                )
            )
        return pieces

    def sum_start(layer, job, step):
        if step < sum_steps - 1:
            if layer == 0 and 1 <= step <= folds:
                pl.semaphore_wait(free_sem.at[job, step - 1], 2)
            for item in sum_copies(layer, job, step):
                item.start()
            return
        for give, _, keep in last_copies(layer, job):
            pl.when(section != layer)(give.start)
            pl.when(section == layer)(keep.start)

    def add_rows(goal, base, source):
        size = source.shape[0]
        piece = math.gcd(size, 192)

        def add_piece(index, carry):
            here = pl.ds(pl.multiple_of(index * piece, 16), piece)
            goal[here] = (base[here].astype(F32) + source[here].astype(F32)).astype(BF16)
            return carry

        lax.fori_loop(0, size // piece, add_piece, 0)

    def sum_end(layer, job, step):
        if step == sum_steps - 1:
            for give, take, keep in last_copies(layer, job):
                pl.when(section != layer)(give.wait_send)
                pl.when(section == layer)(take.wait_recv)
                pl.when(section == layer)(keep.wait)
            return
        for item in sum_copies(layer, job, step):
            item.wait()
        if step == 0:
            base, job_rows = jobs[job]
            kept = sums_of(layer, base + section * (job_rows // 2), job_rows // 2)
            add_rows(kept, kept, landing_of(half_got.at[layer], job, 2))
            return
        if step > bits:
            return
        for group, (steps, start, size) in enumerate(groups[job]):
            goal = gathered(layer, job, group, start, size)
            if step < folds:
                base = sums_of(layer, steps[step - 1][1], steps[step - 1][3])
                add_rows(base, base, landing_of(first_got.at[group], job, 8))
            elif step == folds:
                add_rows(goal, sums_of(layer, start, size), landing_of(second_got.at[group], job, 16))
            else:
                landed = landing_of(more_got.at[layer, step - 1 - folds, group], job, 16)
                add_rows(goal, goal, landed)
            if layer == 1 and step <= folds:
                mate = mates[steps[step - 1][0]]
                pl.semaphore_signal(
                    free_sem.at[job, step - 1],
                    inc=1,
                    device_id=mate,
                    device_id_type=MESH,
                )

    steps_done = {(layer, job): 0 for layer in range(2) for job in range(len(jobs))}

    def move_sum(layer, job, step=None):
        step = steps_done[layer, job] if step is None else step
        if step < sum_steps:
            sum_end(layer, job, step)
            if step + 1 < sum_steps:
                sum_start(layer, job, step + 1)
            steps_done[layer, job] = max(steps_done[layer, job], step + 1)

    line_friends = [twin] + mates + [near, far]

    def line_copy(step):
        sems = (line_send.at[0], line_recv.at[step])
        return send(small, line_got.at[step], sems, line_friends[step])

    def line_end(step):
        line_copy(step).wait()
        if step <= bits:
            small[...] += line_got[step]
        else:
            small[:, 0:4] += line_got[step, :, 0:4]

    low_side = place < 2
    own_half = pl.multiple_of(jnp.where(low_side, 0, half_width), LANES)
    other_half = pl.multiple_of(jnp.where(low_side, half_width, 0), LANES)
    window = place * columns // LANES * LANES
    window = pl.multiple_of(window, LANES)
    end_window = pl.multiple_of(jnp.where(low_side, 0, width - padded), LANES)

    sent_width = width - LANES
    sent_lanes = pl.ds(pl.multiple_of(jnp.where(low_side, LANES, 0), LANES), sent_width)

    def spot(kind, u):
        chunk = u // halves if kind < 2 else chunks - 1 - u // halves
        return chunk, pl.ds(pl.multiple_of(lax.rem(u, halves) * unit, unit), unit)

    def buffers(kind, u):
        if kind == 1:
            return late_part.at[u], late_got.at[u], late_met.at[u]
        return part.at[u], got.at[u], met.at[u] if kind != 3 else met.at[u, :, :half_width]

    def hop_sems(kind, stage, u):
        late = int(kind == 1)
        return hop_send.at[late, (0, 0, 1)[stage], u], hop_recv.at[late, (0, 1, 0)[stage], u]

    def first_hop(kind, u):
        own, landing, _ = buffers(kind, u)
        if kind in (1, 3):
            own, landing = own.at[:, sent_lanes], landing.at[:, :sent_width]
        return send(own, landing, hop_sems(kind, 0, u), near)

    def second_hop(kind, u):
        own, _, landing = buffers(kind, u)
        if kind in (1, 3):
            own = own.at[:, pl.ds(other_half, half_width)]
        return send(own, landing, hop_sems(kind, 1, u), far)

    def third_hop(kind, u):
        own, _, landing = buffers(kind, u)
        if kind in (1, 3):
            own, landing = own.at[:, pl.ds(end_window, padded)], landing.at[:, :padded]
        else:
            chunk, here = spot(kind, u)
            own = landing = chain.at[kind + 1, chunk, here]
        return send(own, landing, hop_sems(kind, 2, u), near)

    def by_rows(count, work, step=32):
        def turn_rows(index, carry):
            work(pl.ds(pl.multiple_of(index * step, step), step))
            return carry

        lax.fori_loop(0, count // step, turn_rows, 0)

    def launch(kind, c, parts=(0, 1)):
        @pl.when(outer)
        def _():
            for half in parts:
                first_hop(kind, c * halves + half).start()

    def meet(kind, u):
        @pl.when(inner)
        def _():
            first_hop(kind, u).wait_recv()
            own, landed, _ = buffers(kind, u)
            if kind in (1, 3):
                own, landed = own.at[:, sent_lanes], landed.at[:, :sent_width]

            def add(here):
                own[here] = (own[here].astype(F32) + landed[here].astype(F32)).astype(BF16)

            by_rows(unit, add)
            second_hop(kind, u).start()

    def settle(kind, u):
        chunk, here = spot(kind, u)

        @pl.when(inner)
        def _():
            second_hop(kind, u).wait_recv()
            own, _, landed = buffers(kind, u)
            if kind in (1, 3):
                lanes_here = pl.ds(own_half, half_width)
                goal = own.at[:, lanes_here]
                source = goal
                base = chain.at[kind, chunk, here, lanes_here]
            else:
                lanes_here = slice(None)
                goal = chain.at[kind + 1, chunk, here]
                source = own
                base = chain.at[kind, chunk, here]

            def add(at):
                value = source[at].astype(F32) + landed[at].astype(F32) + base[at].astype(F32)
                if kind < 2:
                    value = value + vec[kind, 4:5, lanes_here]
                goal[at] = value.astype(BF16)

            by_rows(unit, add)
            if kind > 1:
                third_hop((0, 2)[kind - 2], u).wait_send()
            third_hop(kind, u).start()

    def arrive(kind, c):
        @pl.when(outer)
        def _():
            for half in range(halves):
                third_hop(kind, c * halves + half).wait_recv()

    def release(kind, c):
        for half in range(halves):
            u = c * halves + half
            pl.when(outer)(first_hop(kind, u).wait_send)
            pl.when(inner)(second_hop(kind, u).wait_send)

    def let_go(kind):
        for u in range(units):
            pl.when(inner)(third_hop(kind, u).wait_send)

    def serve(kind, meets, settles):
        for index in range(max(len(meets), len(settles))):
            if index < len(meets):
                meet(kind, meets[index])
            if index < len(settles):
                settle(kind, settles[index])

    def need(first, last, layer):
        @pl.when(section == layer)
        def _():
            for index in range(max(first, 1), last):
                loads[index - 1].wait()

        @pl.when(section != layer)
        def _():
            for index in range(first, last):
                gifts[index].wait_recv()

    input_load.wait()

    first_turns = (((), ()), ((), ()), ((0,), ()), ((1, 2), (0, 1)))
    second_turns = (
        (((3,), (2,)), ((4,), (3,))),
        (((5,), (4,)), ((6,), (5,))),
        (((7,), (6,)), ((), (7,))),
        (((), ()), ((), ())),
    )

    def weigh(c):
        chain[2, c] = (vec[0, 7:8] * chain[2, c].astype(F32)).astype(BF16)

    def find_share():
        own_mark = jnp.where(section == 0, marks[0], marks[1])[0:1]
        own_count = jnp.sum(own_mark * tally[0:1], axis=-1, keepdims=True)
        share = (tissue.shape[0] * copies / TISSUES) / own_count
        gifts[0].wait_send()
        vec[0, 7:8] = jnp.broadcast_to(share, (1, width))
        target_load.wait()

    def forward_layer(layer, carry):
        for c in range(chunks):
            pl.when(layer == 1)(functools.partial(arrive, 0, c))
            second = forward_chunk(layer, c)

            @pl.when(layer == 0)
            def _():
                launch(0, c)
                serve(0, *first_turns[c])
                for bit in range(bits):
                    if min(bit, chunks - 1) == c:
                        count_on(bit)

            @pl.when(layer == 1)
            def _():
                serve(0, *second_turns[c][0])
                if c in (1, 2):
                    launch(1, c - 1)
                if c == 2:
                    launch(1, 2, (0,))
                if c == 0:
                    find_share()
                weigh(c)
                feed_back(c, second)
                serve(0, *second_turns[c][1])

        return carry

    lax.fori_loop(0, 2, forward_layer, 0)

    meets = {1: (1, 1, 3, 3, 5), 2: (4, 5, 6, 7, 8, 9, 10, 11), 3: (13, 14, 14)}
    settles = {1: (3, 3, 5, 5, 7), 2: (6, 7, 8, 9, 10, 11, 12, 12), 3: (14,)}
    backward_points = [[] for _ in range(8 * 2)]
    for kind in (1, 2, 3):
        order = [(2 * u, meet, kind, u, meets[kind][u]) for u in range(len(meets[kind]))]
        order += [(2 * u + 3, settle, kind, u, settles[kind][u]) for u in range(len(settles[kind]))]
        for _, work, kind_now, u, point in sorted(order, key=lambda item: item[0]):
            backward_points[point].append((work, kind_now, u))

    def serve_point(point):
        for work, kind, u in backward_points[point]:
            work(kind, u)

    sum_moves = {
        5: ((1, 0, 0), (1, 1, 0)),
        8: ((1, 2, 0),),
        9: ((1, 0, 2), (1, 1, 2)),
        10: ((1, 2, 1),),
        12: ((1, 2, 2), (1, 0, 3), (1, 1, 3)),
        13: ((1, 2, 3),),
        14: ((0, 0, 0),),
    }

    def serve_at(step, point):
        for index in range(2 * chunks):
            number = index * 2 + point

            @pl.when(step == index)
            def _():
                serve_point(number)
                for moved in sum_moves.get(number, ()):
                    move_sum(*moved)

    def backward_step(step, carry):
        turn_index = step // chunks
        at = lax.rem(step, chunks)
        layer = 1 - turn_index
        c = chunks - 1 - at
        last_step = step == 2 * chunks - 1

        @pl.when(layer == 0)
        def _():

            @pl.when(at == 0)
            def _():
                move_sum(1, 0, 1)
                move_sum(1, 1, 1)

            arrive(2, at)
            release(2, at)

        pl.when(layer == 1)(functools.partial(release, 0, at))

        @pl.when(last_step)
        def _():
            add_forward_grads(0, 0, False, ("fc2",))
            sum_start(0, 0, 0)

        backward_front(layer, c)

        @pl.when(last_step)
        def _():
            spread, _ = normalise(chain[0, 0].astype(F32))
            norm_rows[...] = (spread * vec[0, 2:3] + vec[0, 3:4]).astype(BF16)
            add_forward_grads(0, 0, False, ("fc1",))
            sum_start(0, 1, 0)

        for index in range(chunks):
            pl.when(c == index)(functools.partial(backward_attention, layer, index))
        serve_at(step, 0)
        first = backward_rest(layer, c)
        for index in range(2):
            pl.when(turn_index == index)(functools.partial(launch, 2 + index, at))
        pl.when(last_step)(functools.partial(move_sum, 0, 1))
        add_weight_grads(layer, c, first)

        @pl.when(jnp.logical_or(step == 0, jnp.logical_and(layer == 0, c > 0)))
        def _():
            add_forward_grads(layer, c, step == chunks)

        @pl.when(step == 0)
        def _():
            sum_start(1, 0, 0)
            sum_start(1, 1, 0)

        @pl.when(jnp.logical_and(layer == 0, at > 1))
        def _():
            pl.when(at == 2)(functools.partial(launch, 1, 2, (1,)))
            pl.when(at == 3)(functools.partial(launch, 1, 3))

        pl.when(step == chunks - 1)(functools.partial(sum_start, 1, 2, 0))
        pl.when(last_step)(functools.partial(sum_start, 0, 2, 0))
        serve_at(step, 1)
        return carry

    lax.fori_loop(0, 2 * chunks, backward_step, 0)

    shift = lax.rem(place * columns, LANES)

    def staged(index, layer):
        return probs[-1].at[layer, index, :columns]

    def stage(index, layer, row, value):
        turned_value = value.astype(F32).T
        low = turned_value[:columns]
        high = turned_value[LANES // 2 : LANES // 2 + columns]
        goal = pl.ds(pl.multiple_of(row, unit), unit)
        staged(index, layer)[:, goal] = jnp.where(shift == 0, low, high).astype(BF16)

    def stage_whole(index, layer, kind):
        def stage_unit(u, carry):
            rows_here = pl.ds(pl.multiple_of(lax.rem(u, halves) * unit, unit), unit)
            source = chain.at[kind + 1, u // halves, rows_here, pl.ds(window, padded)]
            stage(index, layer, u * unit, source[...])
            return carry

        lax.fori_loop(0, units, stage_unit, 0)

    def stage_own(index, layer, kind):
        for c in range(chunks):
            arrive(kind, c)
            release(kind, c)
        let_go(kind)
        tile = lax.broadcasted_iota(jnp.int32, (1, padded), 1) // LANES
        unsent = tile == jnp.where(low_side, 0, padded // LANES - 1)
        store, landing = (late_part, late_met) if kind == 1 else (part, met)

        def stage_unit(u, carry):
            chunk = u // halves if kind == 1 else chunks - 1 - u // halves
            row = chunk * rows + lax.rem(u, halves) * unit

            @pl.when(outer)
            def _():
                mine = store[u, :, pl.ds(end_window, padded)]
                value = landing[u, :, :padded].astype(F32) + only(unsent, mine.astype(F32))
                stage(index, layer, row, value)

            @pl.when(inner)
            def _():
                stage(index, layer, row, store[u, :, pl.ds(window, padded)])

            return carry

        lax.fori_loop(0, units, stage_unit, 0)

    def swap_columns(index, goal):
        sems = (swap_send.at[index], swap_recv.at[index])
        return [
            send(staged(index, 1 - section), goal.at[section], sems, twin),
            pltpu.make_async_copy(staged(index, section), goal.at[section], load_sem.at[1 + index]),
        ]

    def line_next(step):
        if step < len(line_friends):
            line_end(step)
            if step + 1 < len(line_friends):
                line_copy(step + 1).start()

    line_copy(0).start()
    for item in gifts[1:]:
        item.wait_send()
    meet(3, 3)
    settle(3, 1)
    meet(3, 4)
    move_sum(0, 2)
    settle(3, 2)
    meet(3, 5)
    settle(3, 3)
    line_next(0)
    stage_whole(0, 0, 0)
    meet(1, 5)
    settle(3, 4)
    move_sum(0, 0)
    settle(3, 5)
    meet(3, 6)
    move_sum(0, 1)
    stage_whole(1, 1, 2)
    settle(1, 5)
    for job in range(2):
        move_sum(1, job)
    move_sum(0, 2)
    line_next(1)
    meet(3, 7)
    settle(3, 6)
    move_sum(0, 0)
    meet(1, 6)
    settle(3, 7)
    move_sum(0, 1)
    move_sum(0, 2)
    line_next(2)
    meet(1, 7)
    move_sum(0, 0)
    settle(1, 6)
    move_sum(0, 1)
    settle(1, 7)
    move_sum(0, 2)
    line_next(3)
    move_sum(1, 2)
    stage_own(1, 0, 3)
    moves = swap_columns(1, grad_cols)
    for item in moves:
        item.start()
    stage_own(0, 1, 1)
    late_moves = swap_columns(0, out_cols)
    for item in late_moves:
        item.start()
    move_sum(0, 0)
    move_sum(0, 1)
    for step in range(4, len(line_friends)):
        line_next(step)
    lines_store = pltpu.make_async_copy(small.at[section], lines, load_sem.at[0])
    lines_store.start()
    for _ in range(sum_steps):
        for job in range(len(jobs)):
            move_sum(0, job)
            move_sum(1, job)
    for item in moves + late_moves:
        item.wait()
    lines_store.wait()


def train(x, target, tissue, weights, qkv_bias, vec):
    wq, wd, w1, w2 = weights
    count, seq_len, width = x.shape
    rows = min(ROWS, seq_len)
    chunks = seq_len // rows
    unit = min(UNIT, rows)
    pieces = seq_len // unit
    valid = wd.shape[0]
    heads = valid // HEAD
    lanes = -(-valid // LANES) * LANES
    units = w1.shape[1]
    columns = width // lax.axis_size("tensor")
    bits = lax.axis_size("dp").bit_length() - 1
    tables = jnp.asarray(rotary_tables(seq_len))
    total_rows = 3 * valid + width + units + valid
    hbm = pl.BlockSpec(memory_space=pl.ANY)
    vmem = pl.BlockSpec(memory_space=pltpu.VMEM)
    smem = pl.BlockSpec(memory_space=pltpu.SMEM)
    scratch = [
        pltpu.VMEM((2, 8, width), F32),
        pltpu.VMEM((2, 3, lanes // HEAD, HEAD, width), BF16),
        pltpu.VMEM((2, lanes, width), BF16),
        pltpu.VMEM((2,) + w1.shape, BF16),
        pltpu.VMEM((2,) + w2.shape, BF16),
        pltpu.VMEM((2, 8, width), F32),
        pltpu.VMEM((4, chunks, rows, width), BF16),
        pltpu.VMEM((2, seq_len, 3 * lanes), BF16),
        pltpu.VMEM((2, seq_len, lanes), BF16),
        pltpu.VMEM((2, seq_len, units), BF16),
        pltpu.VMEM((2, seq_len, units), BF16),
        pltpu.VMEM((seq_len, lanes), F32),
        pltpu.VMEM((seq_len, lanes), F32),
        pltpu.VMEM((pieces, unit, width), BF16),
        pltpu.VMEM((pieces, unit, width), BF16),
        pltpu.VMEM((pieces, unit, width), BF16),
        pltpu.VMEM((pieces, unit, width), BF16),
        pltpu.VMEM((pieces, unit, width - LANES), BF16),
        pltpu.VMEM((pieces, unit, width // 2), BF16),
        pltpu.VMEM((rows, width), BF16),
        pltpu.VMEM((rows, lanes), BF16),
        pltpu.VMEM((rows, lanes), F32),
        pltpu.VMEM((2, total_rows, width), BF16),
        pltpu.VMEM((2, total_rows // 2, width), BF16),
        pltpu.VMEM((2, total_rows // 8, width), BF16),
        pltpu.VMEM((2, total_rows // 16, width), BF16),
        pltpu.VMEM((2, max(bits - 2, 1), 2, total_rows // 16 if bits > 2 else 16, width), BF16),
        pltpu.VMEM((3 + bits, 2, 8, width), F32),
        pltpu.VMEM((8, LANES), F32),
        pltpu.VMEM((max(bits, 1), 8, LANES), F32),
    ]
    probs = [pltpu.VMEM((2, heads, rows, (c + 1) * rows), BF16) for c in range(chunks)]
    semaphores = [
        pltpu.SemaphoreType.DMA((10,)),
        pltpu.SemaphoreType.DMA((7,)),
        pltpu.SemaphoreType.DMA((7,)),
        pltpu.SemaphoreType.DMA((2, 2, pieces)),
        pltpu.SemaphoreType.DMA((2, 2, pieces)),
        pltpu.SemaphoreType.DMA((2,)),
        pltpu.SemaphoreType.DMA((2,)),
        pltpu.SemaphoreType.DMA((2, 3, 2)),
        pltpu.SemaphoreType.DMA((2, 3, bits + 4, 2)),
        pltpu.SemaphoreType.DMA((1,)),
        pltpu.SemaphoreType.DMA((3 + bits,)),
        pltpu.SemaphoreType.DMA((1,)),
        pltpu.SemaphoreType.DMA((max(bits, 1),)),
        pltpu.SemaphoreType.DMA((3, 2)),
        pltpu.SemaphoreType.REGULAR((3, 2)),
    ]

    def body(*refs):
        ends = np.cumsum([9, len(vec), 4 + len(scratch), chunks])
        head, lines, main, kept = (
            refs[start:stop] for start, stop in zip([0, *ends[:-1]], ends, strict=True)
        )
        train_kernel(heads, *head, lines, *main, kept, *refs[ends[-1] :])

    return pl.pallas_call(
        body,
        out_shape=(
            jax.ShapeDtypeStruct((count, columns, seq_len), BF16),
            jax.ShapeDtypeStruct((count, columns, seq_len), BF16),
            jax.ShapeDtypeStruct((total_rows, width), BF16),
            jax.ShapeDtypeStruct((8, width), F32),
        ),
        in_specs=[hbm, hbm, smem, vmem, hbm, hbm, hbm, hbm, vmem] + [vmem] * len(vec),
        out_specs=(hbm, hbm, hbm, hbm),
        scratch_shapes=scratch + probs + semaphores,
        compiler_params=pltpu.CompilerParams(
            collective_id=0, has_side_effects=True, vmem_limit_bytes=63 * 2**20
        ),
    )(
        x.reshape(count, chunks, rows, width),
        target.reshape(count, chunks, rows, width),
        tissue,
        tables,
        wq.reshape(heads, 3, HEAD, width),
        wd,
        w1,
        w2,
        qkv_bias,
        *vec,
    )


def widen_kernel(
    heads,
    sizes,
    cols,
    grad_cols,
    total,
    lines,
    out_cols,
    out_grad_cols,
    goal0,
    goal1,
    goal2,
    goal3,
    gain1,
    bias1,
    gain2,
    bias2,
    out_bias,
    out_bias_again,
    fc1_bias,
    qkv_bias,
    cols_kept,
    cols_low,
    cols_wide,
    rows_low,
    rows_wide,
    pass_sem,
    load_sem,
    store_sem,
):
    block = sizes[-1]
    through = pltpu.make_async_copy(cols, cols_kept, pass_sem.at[0])
    onward = pltpu.make_async_copy(cols_kept, out_cols, pass_sem.at[1])
    moves = []
    for index in range(cols.shape[0]):
        moves.append(
            (grad_cols.at[index], cols_low.at[index], cols_wide.at[index], out_grad_cols.at[index])
        )
    start = 0
    for size, goal in zip(sizes, (goal0, goal1, goal2, goal3), strict=True):
        for at in range(0, size, block):
            here = slice(start + at, start + at + block)
            moves.append(
                (total.at[here], rows_low.at[here], rows_wide.at[here], goal.at[at : at + block])
            )
        start += size
    loads = [
        pltpu.make_async_copy(source, low, load_sem.at[index])
        for index, (source, low, _, _) in enumerate(moves)
    ]
    stores = [
        pltpu.make_async_copy(wide, goal, store_sem.at[index])
        for index, (_, _, wide, goal) in enumerate(moves)
    ]
    for item in loads:
        item.start()
    through.start()
    for index, goal in enumerate((gain1, bias1, gain2, bias2)):
        goal[...] = lines[index : index + 1]
    out_bias[...] = lines[5:6]
    out_bias_again[...] = lines[5:6]
    fc1_bias[...] = lines[6:7]
    line = lines[4:5]
    lanes = line.shape[1] // 3
    pieces = []
    for h in range(heads):
        for part_index in range(3):
            at = part_index * lanes + h * HEAD
            pieces.append(line[:, at : at + HEAD])
    qkv_bias[...] = jnp.concatenate(pieces, axis=1)
    for load, store, (_, low, wide, _) in zip(loads, stores, moves, strict=True):
        load.wait()
        wide[...] = low[...].astype(F32)
        store.start()
    through.wait()
    onward.start()
    for item in stores:
        item.wait()
    onward.wait()


def widen(out_cols, grad_cols, total, lines, heads, units):
    width = total.shape[1]
    sizes = (width, units, 3 * heads * HEAD, heads * HEAD)
    count = out_cols.shape[0] + sum(sizes) // sizes[-1]
    hbm = pl.BlockSpec(memory_space=pl.ANY)
    vmem = pl.BlockSpec(memory_space=pltpu.VMEM)
    line = jax.ShapeDtypeStruct((1, width), F32)
    return pl.pallas_call(
        functools.partial(widen_kernel, heads, sizes),
        in_specs=[hbm, hbm, hbm, vmem],
        out_specs=[hbm] * 6 + [vmem] * 8,
        out_shape=[
            jax.ShapeDtypeStruct(out_cols.shape, BF16),
            jax.ShapeDtypeStruct(out_cols.shape, F32),
        ]
        + [jax.ShapeDtypeStruct((size, width), F32) for size in sizes]
        + [line] * 7
        + [jax.ShapeDtypeStruct((1, sizes[2]), F32)],
        scratch_shapes=[
            pltpu.VMEM(out_cols.shape, BF16),
            pltpu.VMEM(out_cols.shape, BF16),
            pltpu.VMEM(out_cols.shape, F32),
            pltpu.VMEM(total.shape, BF16),
            pltpu.VMEM(total.shape, F32),
            pltpu.SemaphoreType.DMA((2,)),
            pltpu.SemaphoreType.DMA((count,)),
            pltpu.SemaphoreType.DMA((count,)),
        ],
        compiler_params=pltpu.CompilerParams(vmem_limit_bytes=60 * 2**20),
    )(out_cols, grad_cols, total, lines)


def per_device(
    hidden_in,
    target,
    tissue,
    ln1_gain,
    ln1_bias,
    ln2_gain,
    ln2_bias,
    qkv_weight,
    qkv_bias,
    dense_weight,
    dense_bias,
    fc1_weight,
    fc1_bias,
    fc2_weight,
    fc2_bias,
):
    heads = dense_weight.shape[1] // HEAD
    units = fc1_weight.shape[-1]
    weights = (qkv_weight[0].T, dense_weight[0], fc1_weight[0], fc2_weight[0])
    vec = (ln1_gain, ln1_bias, ln2_gain, ln2_bias, dense_bias, fc2_bias, fc1_bias)
    out_cols, grad_cols, total, lines = train(hidden_in, target, tissue, weights, qkv_bias, vec)
    out_cols, grad_cols, fc1_grad, fc2_grad, qkv_grad, dense_grad, *lines = widen(
        out_cols, grad_cols, total, lines, heads, units
    )
    gain1, bias1, gain2, bias2, dense_bias_grad, fc2_bias_grad, fc1_bias_grad, qkv_bias_grad = lines
    return (
        out_cols.transpose(0, 2, 1)[None],
        grad_cols.transpose(0, 2, 1)[None],
        gain1,
        bias1,
        gain2,
        bias2,
        qkv_grad.T[None],
        qkv_bias_grad,
        dense_grad[None],
        dense_bias_grad,
        fc1_grad[None],
        fc1_bias_grad,
        fc2_grad[None],
        fc2_bias_grad,
    )


def solution(mesh):
    return jax.shard_map(
        per_device,
        mesh=mesh,
        in_specs=(
            P("dp", None, None),
            P("dp", None, None),
            P("dp"),
            P("section", None),
            P("section", None),
            P("section", None),
            P("section", None),
            P("section", None, "tensor"),
            P("section", "tensor"),
            P("section", "tensor", None),
            P("section", None),
            P("section", None, "tensor"),
            P("section", "tensor"),
            P("section", "tensor", None),
            P("section", None),
        ),
        out_specs=(
            P("section", "dp", None, "tensor"),
            P("section", "dp", None, "tensor"),
            P("section", None),
            P("section", None),
            P("section", None),
            P("section", None),
            P("section", None, "tensor"),
            P("section", "tensor"),
            P("section", "tensor", None),
            P("section", None),
            P("section", None, "tensor"),
            P("section", "tensor"),
            P("section", "tensor", None),
            P("section", None),
        ),
        check_vma=False,
    )
```

```python
import functools
import math

import jax
import jax.numpy as jnp
import numpy as np
from jax import lax
from jax.experimental import pallas as pl
from jax.experimental.pallas import tpu as pltpu
from jax.sharding import PartitionSpec as P

HEAD = 64
ROT = 16
TISSUES = 16
ROWS = 256
UNIT = 128
LANES = 128
EPS = 1e-05
MESH = pl.DeviceIdType.MESH
F32 = jnp.float32
BF16 = jnp.bfloat16


def dot_nn(a, b):
    return lax.dot_general(a, b, (((1,), (0,)), ((), ())), preferred_element_type=F32)


def dot_nt(a, b):
    return lax.dot_general(a, b, (((1,), (1,)), ((), ())), preferred_element_type=F32)


def dot_tn(a, b):
    return lax.dot_general(a, b, (((0,), (0,)), ((), ())), preferred_element_type=F32)


def rotary_tables(seq_len):
    half = ROT // 2
    inverse = 10000.0 ** (-2.0 * np.arange(half) / ROT)
    angles = np.arange(seq_len)[:, None] * inverse[None, :]
    cosines = np.ones((seq_len, HEAD))
    sines = np.zeros((seq_len, HEAD))
    cosines[:, :half] = np.cos(angles)
    cosines[:, half:ROT] = np.cos(angles)
    sines[:, :half] = -np.sin(angles)
    sines[:, half:ROT] = np.sin(angles)
    tables = np.stack([np.tile(item, (1, LANES // HEAD)) for item in (cosines, sines)])
    return tables.astype(np.float32)


def normalise(value):
    center = value - jnp.mean(value, axis=-1, keepdims=True)
    rstd = lax.rsqrt(jnp.mean(center * center, axis=-1, keepdims=True) + EPS)
    return center * rstd, rstd


def train_kernel(
    heads,
    x_in,
    target_in,
    tissue,
    tables,
    wq_in,
    wd_in,
    w1_in,
    w2_in,
    qkv_bias,
    vec_in,
    out_cols,
    grad_cols,
    grads,
    lines,
    small,
    wq,
    wd,
    w1,
    w2,
    vec,
    chain,
    qkv,
    ctx,
    act,
    gate,
    key_grad,
    value_grad,
    part,
    late_part,
    got,
    met,
    late_got,
    late_met,
    norm_rows,
    context_grad,
    query_back,
    total,
    half_got,
    first_got,
    second_got,
    more_got,
    line_got,
    tally,
    tally_got,
    probs,
    load_sem,
    give_sem,
    take_sem,
    hop_send,
    hop_recv,
    swap_send,
    swap_recv,
    sum_send,
    sum_recv,
    line_send,
    line_recv,
    tally_send,
    tally_recv,
    store_sem,
    free_sem,
):
    section = lax.axis_index("section")
    replica = lax.axis_index("dp")
    place = lax.axis_index("tensor")
    copies = lax.axis_size("dp")
    bits = copies.bit_length() - 1
    _, chunks, rows, width = chain.shape
    unit = part.shape[1]
    halves = rows // unit
    units = chunks * halves
    half_width = late_met.shape[-1]
    lanes = wd.shape[1]
    valid = heads * HEAD
    columns = out_cols.shape[1]
    padded = -(-columns // LANES) * LANES
    inner = jnp.logical_and(place > 0, place < 3)
    outer = jnp.logical_not(inner)
    beside = place + 1 - 2 * lax.rem(place, 2)
    across = 3 - place

    def flipped(bit):
        return replica + (1 << bit) * (1 - 2 * lax.rem(replica // (1 << bit), 2))

    twin = {"section": 1 - section}
    mates = [{"dp": flipped(bit)} for bit in range(bits)]
    near = {"tensor": beside}
    far = {"tensor": across}
    friends = [twin, near, far] + mates

    def send(source, goal, sems, target):
        return pltpu.make_async_remote_copy(
            src_ref=source,
            dst_ref=goal,
            send_sem=sems[0],
            recv_sem=sems[1],
            device_id=target,
            device_id_type=MESH,
        )

    barrier = pltpu.get_barrier_semaphore()
    for friend in friends:
        pl.semaphore_signal(barrier, inc=1, device_id=friend, device_id_type=MESH)

    input_load = pltpu.make_async_copy(x_in.at[section], chain.at[0], load_sem.at[0])
    input_load.start()
    pairs = [(wq_in.at[:, index], wq.at[section, index, :heads]) for index in range(3)]
    pairs += [(w1_in, w1.at[section]), (wd_in, wd.at[section, :valid]), (w2_in, w2.at[section])]
    loads = [
        pltpu.make_async_copy(source, goal, load_sem.at[4 + index])
        for index, (source, goal) in enumerate(pairs)
    ]
    for item in loads:
        item.start()
    target_load = pltpu.make_async_copy(target_in.at[section], chain.at[2], load_sem.at[3])
    target_load.start()

    for index, item in enumerate(vec_in):
        vec[section, index : index + 1] = item[...].astype(F32)
    vec[section, 4:5] = vec_in[4][...].astype(F32) + vec_in[5][...].astype(F32)
    line = qkv_bias[...].astype(F32)
    gap = [jnp.zeros((1, lanes - valid), F32)] if lanes > valid else []
    packed = []
    for part_index in range(3):
        for h in range(heads):
            packed.append(line[:, (3 * h + part_index) * HEAD : (3 * h + part_index + 1) * HEAD])
        packed += gap
    vec[section, 5:6] = jnp.concatenate(packed, axis=1)
    vec[section, 7:8] = jnp.zeros((1, width), F32)
    for layer in range(2):
        wd[layer, valid:] = jnp.zeros((lanes - valid, width), BF16)
        wq[layer, :, heads:] = jnp.zeros((3, lanes // HEAD - heads, HEAD, width), BF16)
    pl.semaphore_wait(barrier, len(friends))
    gifts = [
        send(source, goal, (give_sem.at[index], take_sem.at[index]), twin)
        for index, (source, goal) in enumerate(
            [(vec.at[section], vec.at[section])] + pairs
        )
    ]
    projection = 3
    for item in gifts[: 2 + projection]:
        item.start()

    small[...] = jnp.zeros_like(small)
    tissue_lane = lax.broadcasted_iota(jnp.int32, (8, LANES), 1)
    marks = [(tissue_lane == tissue[index]).astype(F32) for index in range(tissue.shape[0])]
    tally[...] = functools.reduce(lambda a, b: a + b, marks)

    def tally_step(bit):
        return send(
            tally, tally_got.at[bit], (tally_send.at[0], tally_recv.at[bit]), mates[bit]
        )

    if bits:
        tally_step(0).start()

    def count_on(bit):
        step = tally_step(bit)
        step.wait()
        tally[...] += tally_got[bit]
        if bit + 1 < bits:
            tally_step(bit + 1).start()

    lane = lax.broadcasted_iota(jnp.int32, (1, lanes), 1) // HEAD
    head_masks = [lane == h for h in range(heads)]
    factor = HEAD ** (-0.5)

    left_half = lax.rem(lax.broadcasted_iota(jnp.int32, (1, lanes), 1), HEAD) < ROT // 2

    def wide(table, start):
        piece = tables[table, pl.ds(start, rows), :]
        return jnp.concatenate([piece] * (lanes // LANES), axis=1)

    def turned(value):
        ahead = pltpu.roll(value, lanes - ROT // 2, 1)
        behind = pltpu.roll(value, ROT // 2, 1)
        return jnp.where(left_half, ahead, behind)

    def turn(value, start):
        return value * wide(0, start) + turned(value) * wide(1, start)

    def turn_back(value, start):
        return value * wide(0, start) - turned(value) * wide(1, start)

    def only(mask, value):
        return jnp.where(mask, value, jnp.zeros_like(value))

    def put(goal, slot, value):
        for half in range(halves):
            piece = value[half * unit : (half + 1) * unit]
            goal[slot * halves + half] = piece.astype(BF16)

    def forward_chunk(layer, c):
        start = c * rows
        here = slice(start, start + rows)
        if c == 0:
            need(0, 1 + projection, layer)
            for item in gifts[2 + projection :]:
                pl.when(layer == 0)(item.start)
        spread, _ = normalise(chain[layer, c].astype(F32))
        first = (spread * vec[layer, 0:1] + vec[layer, 1:2]).astype(BF16)
        second = (spread * vec[layer, 2:3] + vec[layer, 3:4]).astype(BF16)
        projected = dot_nt(first, wq[layer].reshape(3 * lanes, width)) + vec[layer, 5:6]
        query = turn(projected[:, :lanes], start).astype(BF16)
        qkv[layer, here, :lanes] = query
        qkv[layer, here, lanes : 2 * lanes] = turn(projected[:, lanes : 2 * lanes], start).astype(
            BF16
        )
        qkv[layer, here, 2 * lanes :] = projected[:, 2 * lanes :].astype(BF16)
        if c == 0:
            need(1 + projection, 2 + projection, layer)
        pre = dot_nn(second, w1[layer]) + vec[layer, 6:7]
        below = 0.5 * (1.0 + lax.erf(pre * (0.5**0.5)))
        active = (pre * below).astype(BF16)
        act[layer, here, :] = active
        slope = below + pre * (jnp.exp(-0.5 * pre * pre) * ((2.0 * np.pi) ** -0.5))
        gate[layer, here, :] = slope.astype(BF16)
        diagonal = lax.broadcasted_iota(jnp.int32, (rows, rows), 0) >= lax.broadcasted_iota(
            jnp.int32, (rows, rows), 1
        )
        context = jnp.zeros((rows, lanes), F32)
        for h in range(heads):
            asked = only(head_masks[h], query) * jnp.asarray(factor, BF16)
            near = dot_nt(asked, qkv[layer, here, lanes : 2 * lanes])
            near = jnp.where(diagonal, near, -1e30)
            highest = jnp.max(near, axis=-1, keepdims=True)
            if c > 0:
                far = dot_nt(asked, qkv[layer, :start, lanes : 2 * lanes])
                highest = jnp.maximum(highest, jnp.max(far, axis=-1, keepdims=True))
                far = jnp.exp(far - highest)
            near = jnp.exp(near - highest)
            total = jnp.sum(near, axis=-1, keepdims=True)
            if c > 0:
                total = total + jnp.sum(far, axis=-1, keepdims=True)
            inverse = 1.0 / total
            near = (near * inverse).astype(BF16)
            probs[c][layer, h, :, start:] = near
            mixed = dot_nn(near, qkv[layer, here, 2 * lanes :])
            if c > 0:
                far = (far * inverse).astype(BF16)
                probs[c][layer, h, :, :start] = far
                mixed = mixed + dot_nn(far, qkv[layer, :start, 2 * lanes :])
            context = jnp.where(head_masks[h], mixed, context)
        context = context.astype(BF16)
        ctx[layer, here, :] = context
        if c == 0:
            need(2 + projection, 4 + projection, layer)
        result = (dot_nn(context, wd[layer]) + dot_nn(active, w2[layer])).astype(BF16)
        for index, goal in enumerate((part, late_part)):
            pl.when(layer == index)(functools.partial(put, goal, c, result))
        return second

    def feed_back(c, second):
        here = slice(c * rows, (c + 1) * rows)
        cotangent = chain[2, c]
        pre_grad = (dot_nt(cotangent, w2[1]) * gate[1, here, :].astype(F32)).astype(BF16)
        gate[1, here, :] = pre_grad
        if c < chunks - 1:
            norm_rows[...] = second
            add_forward_grads(1, c, c == 0)

    def rows_of(c):
        return pl.ds(pl.multiple_of(c * rows, rows), rows)

    def backward_front(layer, c):
        here = rows_of(c)
        cotangent = chain[3 - layer, c]
        context_grad[...] = dot_nt(cotangent, wd[layer]).astype(BF16)

        @pl.when(layer == 0)
        def _():
            back = dot_nt(cotangent, w2[0]) * gate[0, here, :].astype(F32)
            gate[0, here, :] = back.astype(BF16)

    def backward_attention(layer, c):
        start = c * rows
        stop = start + rows
        here = slice(start, stop)
        own = context_grad[...]
        query = qkv[layer, here, :lanes]
        weighed = own.astype(F32) * ctx[layer, here, :].astype(F32)
        query_grad = jnp.zeros((rows, lanes), F32)
        key_sum = None
        value_sum = None
        for h in range(heads):
            mask = head_masks[h]
            own_grad = only(mask, own)
            asked = only(mask, query) * jnp.asarray(factor, BF16)
            row_dot = jnp.sum(only(mask, weighed), axis=-1, keepdims=True)
            prob = probs[c][layer, h]
            prob_grad = dot_nt(own_grad, qkv[layer, :stop, 2 * lanes :])
            score_grad = (prob.astype(F32) * (prob_grad - row_dot)).astype(BF16)
            query_grad = jnp.where(
                mask, dot_nn(score_grad, qkv[layer, :stop, lanes : 2 * lanes]), query_grad
            )
            key_part = dot_tn(score_grad, asked)
            value_part = dot_tn(prob, own_grad)
            key_sum = key_part if key_sum is None else key_sum + key_part
            value_sum = value_part if value_sum is None else value_sum + value_part
        query_back[...] = query_grad * factor
        if c == chunks - 1:
            key_grad[:stop] = key_sum
            value_grad[:stop] = value_sum
        else:
            key_grad[:stop] += key_sum
            value_grad[:stop] += value_sum

    def backward_rest(layer, c):
        here = rows_of(c)
        start = pl.multiple_of(c * rows, rows)
        pre_grad = gate[layer, here]
        second_back = dot_nt(pre_grad, w1[layer])
        qkv[layer, here, :lanes] = turn_back(query_back[...], start).astype(BF16)
        qkv[layer, here, lanes : 2 * lanes] = turn_back(key_grad[here], start).astype(BF16)
        qkv[layer, here, 2 * lanes :] = value_grad[here].astype(BF16)
        projected_grad = qkv[layer, here, :]
        first_back = dot_nn(projected_grad, wq[layer].reshape(3 * lanes, width))
        spread, rstd = normalise(chain[layer, c].astype(F32))
        back = first_back * vec[layer, 0:1] + second_back * vec[layer, 2:3]
        middle = jnp.mean(back, axis=-1, keepdims=True)
        tilt = jnp.mean(back * spread, axis=-1, keepdims=True)
        put(part, chunks - 1 - c, rstd * (back - middle - spread * tilt))
        first = (spread * vec[layer, 0:1] + vec[layer, 1:2]).astype(BF16)
        norm_rows[...] = (spread * vec[layer, 2:3] + vec[layer, 3:4]).astype(BF16)
        sums = (
            first_back * spread,
            first_back,
            second_back * spread,
            second_back,
            projected_grad.astype(F32),
            chain[3 - layer, c].astype(F32),
            pre_grad.astype(F32),
        )
        for index, item in enumerate(sums):
            small[layer, index : index + 1] += jnp.sum(item, axis=0, keepdims=True)
        return first

    def add_piece_grads(layer, start, piece, first_turn):
        goal = slice(start, start + piece.shape[0])
        before = jnp.where(first_turn, 0.0, total[layer, goal].astype(F32))
        total[layer, goal] = (piece + before).astype(BF16)

    def add_forward_grads(layer, c, first_turn, parts=("fc1", "fc2")):
        here = rows_of(c)
        cotangent = chain.at[3 - layer, c]

        def add_block(index, carry):
            block = pl.ds(pl.multiple_of(index * lanes, lanes), lanes)
            goal = pl.ds(pl.multiple_of(width + index * lanes, lanes), lanes)
            pieces = []
            if "fc1" in parts:
                pieces.append((block, dot_tn(norm_rows[:, block], gate[layer, here])))
            if "fc2" in parts:
                pieces.append((goal, dot_tn(act[layer, here, block], cotangent[...])))
            for at, piece in pieces:
                before = jnp.where(first_turn, 0.0, total[layer, at].astype(F32))
                total[layer, at] = (piece + before).astype(BF16)
            return carry

        lax.fori_loop(0, width // lanes, add_block, 0)

    def add_weight_grads(layer, c, first):
        base = width + act.shape[-1]
        here = rows_of(c)
        first_turn = c == chunks - 1
        for part_index in range(3):
            at = part_index * lanes
            piece = dot_tn(qkv[layer, here, at : at + lanes], first)
            for h in range(heads):
                row = base + (3 * h + part_index) * HEAD
                add_piece_grads(layer, row, piece[h * HEAD : (h + 1) * HEAD], first_turn)
        piece = dot_tn(ctx[layer, here], chain[3 - layer, c])[:valid]
        add_piece_grads(layer, base + 3 * valid, piece, first_turn)

    cut = width + act.shape[-1]
    jobs = ((width, cut - width), (0, width), (cut, total.shape[1] - cut))
    folds = min(bits, 2)
    sum_steps = 2 + 2 * folds + (bits - folds)

    def spans(job, group):
        order = ((0, 1), (1, 0))[group][:folds]
        base, size = jobs[job]
        size = size // 4
        start = base + section * size * 2 + group * size
        steps = []
        for bit in order:
            size = size // 2
            upper = lax.rem(replica // (1 << bit), 2)
            steps.append((bit, start + upper * size, start + (1 - upper) * size, size))
            start = start + upper * size
        return steps, start, size

    groups = [[spans(job, group) for group in range(2)] for job in range(len(jobs))]

    def sums_of(layer, start, size):
        return total.at[layer, pl.ds(pl.multiple_of(start, 16), size)]

    def gathered(layer, job, group, start, size):
        base, job_rows = jobs[job]
        start = start - base - section * (job_rows // 2) - group * (job_rows // 4) + base // 4
        return (act, gate)[group].at[layer, pl.ds(pl.multiple_of(start, 16), size)]

    def sum_sems(layer, job, step, group):
        if 1 <= step <= folds:
            slot = step - 1
        else:
            slot = folds + layer + 2 * (step if step == 0 else step - folds)
        return sum_send.at[layer, job, group], sum_recv.at[job, slot, group]

    def landing_of(buffer, job, parts):
        base, job_rows = jobs[job]
        return buffer.at[base // parts : (base + job_rows) // parts]

    def sum_copies(layer, job, step):
        base, job_rows = jobs[job]
        if step == 0:
            source = sums_of(layer, base + (1 - section) * (job_rows // 2), job_rows // 2)
            goal = landing_of(half_got.at[layer], job, 2)
            return [send(source, goal, sum_sems(layer, job, 0, 0), twin)]
        copies_now = []
        for group, (steps, start, size) in enumerate(groups[job]):
            sems = sum_sems(layer, job, step, group)
            if step <= folds:
                bit, _, gone, size = steps[step - 1]
                goal = landing_of((first_got, second_got)[step - 1].at[group], job, 4 << step)
                copies_now.append(send(sums_of(layer, gone, size), goal, sems, mates[bit]))
            elif step <= bits:
                goal = landing_of(more_got.at[layer, step - 1 - folds, group], job, 16)
                source = gathered(layer, job, group, start, size)
                copies_now.append(send(source, goal, sems, mates[step - 1]))
            else:
                bit, start, _, size = steps[bits - step]
                piece = gathered(layer, job, group, start, size)
                copies_now.append(send(piece, piece, sems, mates[bit]))
        return copies_now

    def last_copies(layer, job):
        base, job_rows = jobs[job]
        size = job_rows // 4
        pieces = []
        for group in range(2):
            first_row = base + section * (job_rows // 2) + group * size
            piece = gathered(layer, job, group, first_row, size)
            goal = grads.at[pl.ds(pl.multiple_of(first_row, 16), size)]
            sems = sum_sems(layer, job, sum_steps - 1, group)
            other_row = base + (1 - section) * (job_rows // 2) + group * size
            other = grads.at[pl.ds(pl.multiple_of(other_row, 16), size)]
            pieces.append(
                (
                    send(piece, goal, sems, twin),
                    send(piece, other, sems, twin),
                    pltpu.make_async_copy(piece, goal, store_sem.at[job, group]),
                )
            )
        return pieces

    def sum_start(layer, job, step):
        if step < sum_steps - 1:
            if layer == 0 and 1 <= step <= folds:
                pl.semaphore_wait(free_sem.at[job, step - 1], 2)
            for item in sum_copies(layer, job, step):
                item.start()
            return
        for give, _, keep in last_copies(layer, job):
            pl.when(section != layer)(give.start)
            pl.when(section == layer)(keep.start)

    def add_rows(goal, base, source):
        size = source.shape[0]
        piece = math.gcd(size, 192)

        def add_piece(index, carry):
            here = pl.ds(pl.multiple_of(index * piece, 16), piece)
            goal[here] = (base[here].astype(F32) + source[here].astype(F32)).astype(BF16)
            return carry

        lax.fori_loop(0, size // piece, add_piece, 0)

    def sum_end(layer, job, step):
        if step == sum_steps - 1:
            for give, take, keep in last_copies(layer, job):
                pl.when(section != layer)(give.wait_send)
                pl.when(section == layer)(take.wait_recv)
                pl.when(section == layer)(keep.wait)
            return
        for item in sum_copies(layer, job, step):
            item.wait()
        if step == 0:
            base, job_rows = jobs[job]
            kept = sums_of(layer, base + section * (job_rows // 2), job_rows // 2)
            add_rows(kept, kept, landing_of(half_got.at[layer], job, 2))
            return
        if step > bits:
            return
        for group, (steps, start, size) in enumerate(groups[job]):
            goal = gathered(layer, job, group, start, size)
            if step < folds:
                base = sums_of(layer, steps[step - 1][1], steps[step - 1][3])
                add_rows(base, base, landing_of(first_got.at[group], job, 8))
            elif step == folds:
                add_rows(goal, sums_of(layer, start, size), landing_of(second_got.at[group], job, 16))
            else:
                landed = landing_of(more_got.at[layer, step - 1 - folds, group], job, 16)
                add_rows(goal, goal, landed)
            if layer == 1 and step <= folds:
                mate = mates[steps[step - 1][0]]
                pl.semaphore_signal(
                    free_sem.at[job, step - 1],
                    inc=1,
                    device_id=mate,
                    device_id_type=MESH,
                )

    steps_done = {(layer, job): 0 for layer in range(2) for job in range(len(jobs))}

    def move_sum(layer, job, step=None):
        step = steps_done[layer, job] if step is None else step
        if step < sum_steps:
            sum_end(layer, job, step)
            if step + 1 < sum_steps:
                sum_start(layer, job, step + 1)
            steps_done[layer, job] = max(steps_done[layer, job], step + 1)

    line_friends = [twin] + mates + [near, far]

    def line_copy(step):
        sems = (line_send.at[0], line_recv.at[step])
        return send(small, line_got.at[step], sems, line_friends[step])

    def line_end(step):
        line_copy(step).wait()
        if step <= bits:
            small[...] += line_got[step]
        else:
            small[:, 0:4] += line_got[step, :, 0:4]

    low_side = place < 2
    own_half = pl.multiple_of(jnp.where(low_side, 0, half_width), LANES)
    other_half = pl.multiple_of(jnp.where(low_side, half_width, 0), LANES)
    window = place * columns // LANES * LANES
    window = pl.multiple_of(window, LANES)
    end_window = pl.multiple_of(jnp.where(low_side, 0, width - padded), LANES)

    sent_width = width - LANES
    sent_lanes = pl.ds(pl.multiple_of(jnp.where(low_side, LANES, 0), LANES), sent_width)

    def spot(kind, u):
        chunk = u // halves if kind < 2 else chunks - 1 - u // halves
        return chunk, pl.ds(pl.multiple_of(lax.rem(u, halves) * unit, unit), unit)

    def buffers(kind, u):
        if kind == 1:
            return late_part.at[u], late_got.at[u], late_met.at[u]
        return part.at[u], got.at[u], met.at[u] if kind != 3 else met.at[u, :, :half_width]

    def hop_sems(kind, stage, u):
        late = int(kind == 1)
        return hop_send.at[late, (0, 0, 1)[stage], u], hop_recv.at[late, (0, 1, 0)[stage], u]

    def first_hop(kind, u):
        own, landing, _ = buffers(kind, u)
        if kind in (1, 3):
            own, landing = own.at[:, sent_lanes], landing.at[:, :sent_width]
        return send(own, landing, hop_sems(kind, 0, u), near)

    def second_hop(kind, u):
        own, _, landing = buffers(kind, u)
        if kind in (1, 3):
            own = own.at[:, pl.ds(other_half, half_width)]
        return send(own, landing, hop_sems(kind, 1, u), far)

    def third_hop(kind, u):
        own, _, landing = buffers(kind, u)
        if kind in (1, 3):
            own, landing = own.at[:, pl.ds(end_window, padded)], landing.at[:, :padded]
        else:
            chunk, here = spot(kind, u)
            own = landing = chain.at[kind + 1, chunk, here]
        return send(own, landing, hop_sems(kind, 2, u), near)

    def by_rows(count, work, step=32):
        def turn_rows(index, carry):
            work(pl.ds(pl.multiple_of(index * step, step), step))
            return carry

        lax.fori_loop(0, count // step, turn_rows, 0)

    def launch(kind, c, parts=(0, 1)):
        @pl.when(outer)
        def _():
            for half in parts:
                first_hop(kind, c * halves + half).start()

    def meet(kind, u):
        @pl.when(inner)
        def _():
            first_hop(kind, u).wait_recv()
            own, landed, _ = buffers(kind, u)
            if kind in (1, 3):
                own, landed = own.at[:, sent_lanes], landed.at[:, :sent_width]

            def add(here):
                own[here] = (own[here].astype(F32) + landed[here].astype(F32)).astype(BF16)

            by_rows(unit, add)
            second_hop(kind, u).start()

    def settle(kind, u):
        chunk, here = spot(kind, u)

        @pl.when(inner)
        def _():
            second_hop(kind, u).wait_recv()
            own, _, landed = buffers(kind, u)
            if kind in (1, 3):
                lanes_here = pl.ds(own_half, half_width)
                goal = own.at[:, lanes_here]
                source = goal
                base = chain.at[kind, chunk, here, lanes_here]
            else:
                lanes_here = slice(None)
                goal = chain.at[kind + 1, chunk, here]
                source = own
                base = chain.at[kind, chunk, here]

            def add(at):
                value = source[at].astype(F32) + landed[at].astype(F32) + base[at].astype(F32)
                if kind < 2:
                    value = value + vec[kind, 4:5, lanes_here]
                goal[at] = value.astype(BF16)

            by_rows(unit, add)
            if kind > 1:
                third_hop((0, 2)[kind - 2], u).wait_send()
            third_hop(kind, u).start()

    def arrive(kind, c):
        @pl.when(outer)
        def _():
            for half in range(halves):
                third_hop(kind, c * halves + half).wait_recv()

    def release(kind, c):
        for half in range(halves):
            u = c * halves + half
            pl.when(outer)(first_hop(kind, u).wait_send)
            pl.when(inner)(second_hop(kind, u).wait_send)

    def let_go(kind):
        for u in range(units):
            pl.when(inner)(third_hop(kind, u).wait_send)

    def serve(kind, meets, settles):
        for index in range(max(len(meets), len(settles))):
            if index < len(meets):
                meet(kind, meets[index])
            if index < len(settles):
                settle(kind, settles[index])

    def need(first, last, layer):
        @pl.when(section == layer)
        def _():
            for index in range(max(first, 1), last):
                loads[index - 1].wait()

        @pl.when(section != layer)
        def _():
            for index in range(first, last):
                gifts[index].wait_recv()

    input_load.wait()

    first_turns = (((), ()), ((), ()), ((0,), ()), ((1, 2), (0, 1)))
    second_turns = (
        (((3,), (2,)), ((4,), (3,))),
        (((5,), (4,)), ((6,), (5,))),
        (((7,), (6,)), ((), (7,))),
        (((), ()), ((), ())),
    )

    def weigh(c):
        chain[2, c] = (vec[0, 7:8] * chain[2, c].astype(F32)).astype(BF16)

    def find_share():
        own_mark = jnp.where(section == 0, marks[0], marks[1])[0:1]
        own_count = jnp.sum(own_mark * tally[0:1], axis=-1, keepdims=True)
        share = (tissue.shape[0] * copies / TISSUES) / own_count
        gifts[0].wait_send()
        vec[0, 7:8] = jnp.broadcast_to(share, (1, width))
        target_load.wait()

    def forward_layer(layer, carry):
        for c in range(chunks):
            pl.when(layer == 1)(functools.partial(arrive, 0, c))
            second = forward_chunk(layer, c)

            @pl.when(layer == 0)
            def _():
                launch(0, c)
                serve(0, *first_turns[c])
                for bit in range(bits):
                    if min(bit, chunks - 1) == c:
                        count_on(bit)

            @pl.when(layer == 1)
            def _():
                serve(0, *second_turns[c][0])
                if c in (1, 2):
                    launch(1, c - 1)
                if c == 2:
                    launch(1, 2, (0,))
                if c == 0:
                    find_share()
                weigh(c)
                feed_back(c, second)
                serve(0, *second_turns[c][1])

        return carry

    lax.fori_loop(0, 2, forward_layer, 0)

    meets = {1: (1, 1, 3, 3, 5), 2: (4, 5, 6, 7, 8, 9, 10, 11), 3: (13, 14, 14)}
    settles = {1: (3, 3, 5, 5, 7), 2: (6, 7, 8, 9, 10, 11, 12, 12), 3: (14,)}
    backward_points = [[] for _ in range(8 * 2)]
    for kind in (1, 2, 3):
        order = [(2 * u, meet, kind, u, meets[kind][u]) for u in range(len(meets[kind]))]
        order += [(2 * u + 3, settle, kind, u, settles[kind][u]) for u in range(len(settles[kind]))]
        for _, work, kind_now, u, point in sorted(order, key=lambda item: item[0]):
            backward_points[point].append((work, kind_now, u))

    def serve_point(point):
        for work, kind, u in backward_points[point]:
            work(kind, u)

    sum_moves = {
        5: ((1, 0, 0), (1, 1, 0)),
        8: ((1, 2, 0),),
        9: ((1, 0, 2), (1, 1, 2)),
        10: ((1, 2, 1),),
        11: ((1, 2, 2),),
        12: ((1, 0, 3), (1, 1, 3)),
        13: ((1, 2, 3),),
        14: ((0, 0, 0),),
    }

    def serve_at(step, point):
        for index in range(2 * chunks):
            number = index * 2 + point

            @pl.when(step == index)
            def _():
                serve_point(number)
                for moved in sum_moves.get(number, ()):
                    move_sum(*moved)

    def backward_step(step, carry):
        turn_index = step // chunks
        at = lax.rem(step, chunks)
        layer = 1 - turn_index
        c = chunks - 1 - at
        last_step = step == 2 * chunks - 1

        @pl.when(layer == 0)
        def _():

            @pl.when(at == 0)
            def _():
                move_sum(1, 0, 1)
                move_sum(1, 1, 1)

            arrive(2, at)
            release(2, at)

        pl.when(layer == 1)(functools.partial(release, 0, at))

        @pl.when(last_step)
        def _():
            add_forward_grads(0, 0, False, ("fc2",))
            sum_start(0, 0, 0)

        backward_front(layer, c)

        @pl.when(last_step)
        def _():
            spread, _ = normalise(chain[0, 0].astype(F32))
            norm_rows[...] = (spread * vec[0, 2:3] + vec[0, 3:4]).astype(BF16)
            add_forward_grads(0, 0, False, ("fc1",))
            sum_start(0, 1, 0)

        for index in range(chunks):
            pl.when(c == index)(functools.partial(backward_attention, layer, index))
        serve_at(step, 0)
        first = backward_rest(layer, c)
        for index in range(2):
            pl.when(turn_index == index)(functools.partial(launch, 2 + index, at))
        pl.when(last_step)(functools.partial(move_sum, 0, 1))
        add_weight_grads(layer, c, first)

        @pl.when(jnp.logical_or(step == 0, jnp.logical_and(layer == 0, c > 0)))
        def _():
            add_forward_grads(layer, c, step == chunks)

        @pl.when(step == 0)
        def _():
            sum_start(1, 0, 0)
            sum_start(1, 1, 0)

        @pl.when(jnp.logical_and(layer == 0, at > 1))
        def _():
            pl.when(at == 2)(functools.partial(launch, 1, 2, (1,)))
            pl.when(at == 3)(functools.partial(launch, 1, 3))

        pl.when(step == chunks - 1)(functools.partial(sum_start, 1, 2, 0))
        pl.when(last_step)(functools.partial(sum_start, 0, 2, 0))
        serve_at(step, 1)
        return carry

    lax.fori_loop(0, 2 * chunks, backward_step, 0)

    shift = lax.rem(place * columns, LANES)

    def staged(index, layer):
        return probs[-1].at[layer, index, :columns]

    def stage(index, layer, row, value):
        turned_value = value.astype(F32).T
        low = turned_value[:columns]
        high = turned_value[LANES // 2 : LANES // 2 + columns]
        goal = pl.ds(pl.multiple_of(row, unit), unit)
        staged(index, layer)[:, goal] = jnp.where(shift == 0, low, high).astype(BF16)

    def stage_whole(index, layer, kind):
        def stage_unit(u, carry):
            rows_here = pl.ds(pl.multiple_of(lax.rem(u, halves) * unit, unit), unit)
            source = chain.at[kind + 1, u // halves, rows_here, pl.ds(window, padded)]
            stage(index, layer, u * unit, source[...])
            return carry

        lax.fori_loop(0, units, stage_unit, 0)

    def stage_own(index, layer, kind):
        for c in range(chunks):
            arrive(kind, c)
            release(kind, c)
        let_go(kind)
        tile = lax.broadcasted_iota(jnp.int32, (1, padded), 1) // LANES
        unsent = tile == jnp.where(low_side, 0, padded // LANES - 1)
        store, landing = (late_part, late_met) if kind == 1 else (part, met)

        def stage_unit(u, carry):
            chunk = u // halves if kind == 1 else chunks - 1 - u // halves
            row = chunk * rows + lax.rem(u, halves) * unit

            @pl.when(outer)
            def _():
                mine = store[u, :, pl.ds(end_window, padded)]
                value = landing[u, :, :padded].astype(F32) + only(unsent, mine.astype(F32))
                stage(index, layer, row, value)

            @pl.when(inner)
            def _():
                stage(index, layer, row, store[u, :, pl.ds(window, padded)])

            return carry

        lax.fori_loop(0, units, stage_unit, 0)

    def swap_columns(index, goal):
        sems = (swap_send.at[index], swap_recv.at[index])
        return [
            send(staged(index, 1 - section), goal.at[section], sems, twin),
            pltpu.make_async_copy(staged(index, section), goal.at[section], load_sem.at[1 + index]),
        ]

    def line_next(step):
        if step < len(line_friends):
            line_end(step)
            if step + 1 < len(line_friends):
                line_copy(step + 1).start()

    line_copy(0).start()
    for item in gifts[1:]:
        item.wait_send()
    meet(3, 3)
    settle(3, 1)
    meet(3, 4)
    move_sum(0, 2)
    settle(3, 2)
    meet(3, 5)
    settle(3, 3)
    line_next(0)
    stage_whole(0, 0, 0)
    meet(1, 5)
    settle(3, 4)
    move_sum(0, 0)
    settle(3, 5)
    meet(3, 6)
    move_sum(0, 1)
    stage_whole(1, 1, 2)
    settle(1, 5)
    for job in range(2):
        move_sum(1, job)
    move_sum(0, 2)
    line_next(1)
    meet(3, 7)
    settle(3, 6)
    move_sum(0, 0)
    meet(1, 6)
    settle(3, 7)
    move_sum(0, 1)
    move_sum(0, 2)
    line_next(2)
    meet(1, 7)
    move_sum(0, 0)
    settle(1, 6)
    move_sum(0, 1)
    settle(1, 7)
    move_sum(0, 2)
    line_next(3)
    move_sum(1, 2)
    stage_own(1, 0, 3)
    moves = swap_columns(1, grad_cols)
    for item in moves:
        item.start()
    stage_own(0, 1, 1)
    late_moves = swap_columns(0, out_cols)
    for item in late_moves:
        item.start()
    move_sum(0, 0)
    move_sum(0, 1)
    for step in range(4, len(line_friends)):
        line_next(step)
    lines_store = pltpu.make_async_copy(small.at[section], lines, load_sem.at[0])
    lines_store.start()
    for _ in range(sum_steps):
        for job in range(len(jobs)):
            move_sum(0, job)
            move_sum(1, job)
    for item in moves + late_moves:
        item.wait()
    lines_store.wait()


def train(x, target, tissue, weights, qkv_bias, vec):
    wq, wd, w1, w2 = weights
    count, seq_len, width = x.shape
    rows = min(ROWS, seq_len)
    chunks = seq_len // rows
    unit = min(UNIT, rows)
    pieces = seq_len // unit
    valid = wd.shape[0]
    heads = valid // HEAD
    lanes = -(-valid // LANES) * LANES
    units = w1.shape[1]
    columns = width // lax.axis_size("tensor")
    bits = lax.axis_size("dp").bit_length() - 1
    tables = jnp.asarray(rotary_tables(seq_len))
    total_rows = 3 * valid + width + units + valid
    hbm = pl.BlockSpec(memory_space=pl.ANY)
    vmem = pl.BlockSpec(memory_space=pltpu.VMEM)
    smem = pl.BlockSpec(memory_space=pltpu.SMEM)
    scratch = [
        pltpu.VMEM((2, 8, width), F32),
        pltpu.VMEM((2, 3, lanes // HEAD, HEAD, width), BF16),
        pltpu.VMEM((2, lanes, width), BF16),
        pltpu.VMEM((2,) + w1.shape, BF16),
        pltpu.VMEM((2,) + w2.shape, BF16),
        pltpu.VMEM((2, 8, width), F32),
        pltpu.VMEM((4, chunks, rows, width), BF16),
        pltpu.VMEM((2, seq_len, 3 * lanes), BF16),
        pltpu.VMEM((2, seq_len, lanes), BF16),
        pltpu.VMEM((2, seq_len, units), BF16),
        pltpu.VMEM((2, seq_len, units), BF16),
        pltpu.VMEM((seq_len, lanes), F32),
        pltpu.VMEM((seq_len, lanes), F32),
        pltpu.VMEM((pieces, unit, width), BF16),
        pltpu.VMEM((pieces, unit, width), BF16),
        pltpu.VMEM((pieces, unit, width), BF16),
        pltpu.VMEM((pieces, unit, width), BF16),
        pltpu.VMEM((pieces, unit, width - LANES), BF16),
        pltpu.VMEM((pieces, unit, width // 2), BF16),
        pltpu.VMEM((rows, width), BF16),
        pltpu.VMEM((rows, lanes), BF16),
        pltpu.VMEM((rows, lanes), F32),
        pltpu.VMEM((2, total_rows, width), BF16),
        pltpu.VMEM((2, total_rows // 2, width), BF16),
        pltpu.VMEM((2, total_rows // 8, width), BF16),
        pltpu.VMEM((2, total_rows // 16, width), BF16),
        pltpu.VMEM((2, max(bits - 2, 1), 2, total_rows // 16 if bits > 2 else 16, width), BF16),
        pltpu.VMEM((3 + bits, 2, 8, width), F32),
        pltpu.VMEM((8, LANES), F32),
        pltpu.VMEM((max(bits, 1), 8, LANES), F32),
    ]
    probs = [pltpu.VMEM((2, heads, rows, (c + 1) * rows), BF16) for c in range(chunks)]
    semaphores = [
        pltpu.SemaphoreType.DMA((10,)),
        pltpu.SemaphoreType.DMA((7,)),
        pltpu.SemaphoreType.DMA((7,)),
        pltpu.SemaphoreType.DMA((2, 2, pieces)),
        pltpu.SemaphoreType.DMA((2, 2, pieces)),
        pltpu.SemaphoreType.DMA((2,)),
        pltpu.SemaphoreType.DMA((2,)),
        pltpu.SemaphoreType.DMA((2, 3, 2)),
        pltpu.SemaphoreType.DMA((3, min(bits, 2) + 2 * (bits + 2), 2)),
        pltpu.SemaphoreType.DMA((1,)),
        pltpu.SemaphoreType.DMA((3 + bits,)),
        pltpu.SemaphoreType.DMA((1,)),
        pltpu.SemaphoreType.DMA((max(bits, 1),)),
        pltpu.SemaphoreType.DMA((3, 2)),
        pltpu.SemaphoreType.REGULAR((3, 2)),
    ]

    def body(*refs):
        ends = np.cumsum([9, len(vec), 4 + len(scratch), chunks])
        head, lines, main, kept = (
            refs[start:stop] for start, stop in zip([0, *ends[:-1]], ends, strict=True)
        )
        train_kernel(heads, *head, lines, *main, kept, *refs[ends[-1] :])

    return pl.pallas_call(
        body,
        out_shape=(
            jax.ShapeDtypeStruct((count, columns, seq_len), BF16),
            jax.ShapeDtypeStruct((count, columns, seq_len), BF16),
            jax.ShapeDtypeStruct((total_rows, width), BF16),
            jax.ShapeDtypeStruct((8, width), F32),
        ),
        in_specs=[hbm, hbm, smem, vmem, hbm, hbm, hbm, hbm, vmem] + [vmem] * len(vec),
        out_specs=(hbm, hbm, hbm, hbm),
        scratch_shapes=scratch + probs + semaphores,
        compiler_params=pltpu.CompilerParams(
            collective_id=0, has_side_effects=True, vmem_limit_bytes=63 * 2**20
        ),
    )(
        x.reshape(count, chunks, rows, width),
        target.reshape(count, chunks, rows, width),
        tissue,
        tables,
        wq.reshape(heads, 3, HEAD, width),
        wd,
        w1,
        w2,
        qkv_bias,
        *vec,
    )


def widen_kernel(
    heads,
    sizes,
    cols,
    grad_cols,
    total,
    lines,
    out_cols,
    out_grad_cols,
    goal0,
    goal1,
    goal2,
    goal3,
    gain1,
    bias1,
    gain2,
    bias2,
    out_bias,
    out_bias_again,
    fc1_bias,
    qkv_bias,
    cols_kept,
    cols_low,
    cols_wide,
    rows_low,
    rows_wide,
    pass_sem,
    load_sem,
    store_sem,
):
    block = sizes[-1]
    through = pltpu.make_async_copy(cols, cols_kept, pass_sem.at[0])
    onward = pltpu.make_async_copy(cols_kept, out_cols, pass_sem.at[1])
    moves = []
    for index in range(cols.shape[0]):
        moves.append(
            (grad_cols.at[index], cols_low.at[index], cols_wide.at[index], out_grad_cols.at[index])
        )
    start = 0
    for size, goal in zip(sizes, (goal0, goal1, goal2, goal3), strict=True):
        for at in range(0, size, block):
            here = slice(start + at, start + at + block)
            moves.append(
                (total.at[here], rows_low.at[here], rows_wide.at[here], goal.at[at : at + block])
            )
        start += size
    loads = [
        pltpu.make_async_copy(source, low, load_sem.at[index])
        for index, (source, low, _, _) in enumerate(moves)
    ]
    stores = [
        pltpu.make_async_copy(wide, goal, store_sem.at[index])
        for index, (_, _, wide, goal) in enumerate(moves)
    ]
    for item in loads:
        item.start()
    through.start()
    for index, goal in enumerate((gain1, bias1, gain2, bias2)):
        goal[...] = lines[index : index + 1]
    out_bias[...] = lines[5:6]
    out_bias_again[...] = lines[5:6]
    fc1_bias[...] = lines[6:7]
    line = lines[4:5]
    lanes = line.shape[1] // 3
    pieces = []
    for h in range(heads):
        for part_index in range(3):
            at = part_index * lanes + h * HEAD
            pieces.append(line[:, at : at + HEAD])
    qkv_bias[...] = jnp.concatenate(pieces, axis=1)
    for load, store, (_, low, wide, _) in zip(loads, stores, moves, strict=True):
        load.wait()
        wide[...] = low[...].astype(F32)
        store.start()
    through.wait()
    onward.start()
    for item in stores:
        item.wait()
    onward.wait()


def widen(out_cols, grad_cols, total, lines, heads, units):
    width = total.shape[1]
    sizes = (width, units, 3 * heads * HEAD, heads * HEAD)
    count = out_cols.shape[0] + sum(sizes) // sizes[-1]
    hbm = pl.BlockSpec(memory_space=pl.ANY)
    vmem = pl.BlockSpec(memory_space=pltpu.VMEM)
    line = jax.ShapeDtypeStruct((1, width), F32)
    return pl.pallas_call(
        functools.partial(widen_kernel, heads, sizes),
        in_specs=[hbm, hbm, hbm, vmem],
        out_specs=[hbm] * 6 + [vmem] * 8,
        out_shape=[
            jax.ShapeDtypeStruct(out_cols.shape, BF16),
            jax.ShapeDtypeStruct(out_cols.shape, F32),
        ]
        + [jax.ShapeDtypeStruct((size, width), F32) for size in sizes]
        + [line] * 7
        + [jax.ShapeDtypeStruct((1, sizes[2]), F32)],
        scratch_shapes=[
            pltpu.VMEM(out_cols.shape, BF16),
            pltpu.VMEM(out_cols.shape, BF16),
            pltpu.VMEM(out_cols.shape, F32),
            pltpu.VMEM(total.shape, BF16),
            pltpu.VMEM(total.shape, F32),
            pltpu.SemaphoreType.DMA((2,)),
            pltpu.SemaphoreType.DMA((count,)),
            pltpu.SemaphoreType.DMA((count,)),
        ],
        compiler_params=pltpu.CompilerParams(vmem_limit_bytes=60 * 2**20),
    )(out_cols, grad_cols, total, lines)


def per_device(
    hidden_in,
    target,
    tissue,
    ln1_gain,
    ln1_bias,
    ln2_gain,
    ln2_bias,
    qkv_weight,
    qkv_bias,
    dense_weight,
    dense_bias,
    fc1_weight,
    fc1_bias,
    fc2_weight,
    fc2_bias,
):
    heads = dense_weight.shape[1] // HEAD
    units = fc1_weight.shape[-1]
    weights = (qkv_weight[0].T, dense_weight[0], fc1_weight[0], fc2_weight[0])
    vec = (ln1_gain, ln1_bias, ln2_gain, ln2_bias, dense_bias, fc2_bias, fc1_bias)
    out_cols, grad_cols, total, lines = train(hidden_in, target, tissue, weights, qkv_bias, vec)
    out_cols, grad_cols, fc1_grad, fc2_grad, qkv_grad, dense_grad, *lines = widen(
        out_cols, grad_cols, total, lines, heads, units
    )
    gain1, bias1, gain2, bias2, dense_bias_grad, fc2_bias_grad, fc1_bias_grad, qkv_bias_grad = lines
    return (
        out_cols.transpose(0, 2, 1)[None],
        grad_cols.transpose(0, 2, 1)[None],
        gain1,
        bias1,
        gain2,
        bias2,
        qkv_grad.T[None],
        qkv_bias_grad,
        dense_grad[None],
        dense_bias_grad,
        fc1_grad[None],
        fc1_bias_grad,
        fc2_grad[None],
        fc2_bias_grad,
    )


def solution(mesh):
    return jax.shard_map(
        per_device,
        mesh=mesh,
        in_specs=(
            P("dp", None, None),
            P("dp", None, None),
            P("dp"),
            P("section", None),
            P("section", None),
            P("section", None),
            P("section", None),
            P("section", None, "tensor"),
            P("section", "tensor"),
            P("section", "tensor", None),
            P("section", None),
            P("section", None, "tensor"),
            P("section", "tensor"),
            P("section", "tensor", None),
            P("section", None),
        ),
        out_specs=(
            P("section", "dp", None, "tensor"),
            P("section", "dp", None, "tensor"),
            P("section", None),
            P("section", None),
            P("section", None),
            P("section", None),
            P("section", None, "tensor"),
            P("section", "tensor"),
            P("section", "tensor", None),
            P("section", None),
            P("section", None, "tensor"),
            P("section", "tensor"),
            P("section", "tensor", None),
            P("section", None),
        ),
        check_vma=False,
    )
```
